32 devices in a mesh: grp: 2 (over y), wide: 16 (over z, x, core), narrow: 1.
Axes of the slice: x: 2, y: 2, z: 4, core: 2. Of those that a mesh axis runs over, the one named last changes fastest.
Arguments:
- dissim: float32 [1, 768, 384], P(None, ('grp', 'wide'), 'narrow'), parts along dimension 1, may hold values from 0.5 to 9.5
- classes: int32 [1, 768, 384], P(None, ('grp', 'wide'), 'narrow'), parts along dimension 1, may hold values from 0 to 3
- coords: float32 [16, 1, 768], P(None, 'narrow', ('grp', 'wide')), parts along dimension 2, may hold values from -3 to 3
Outputs:
- final_coords: float32 [16, 1, 768], P(None, 'narrow', ('grp', 'wide')), parts along dimension 2
- stress: float32 [6], P('grp'), parts along dimension 0
The draws below stay inside these ranges and needn't reach their ends.
There are 2 independent parts, one for each index of `grp`. The reference program is written for one: setup_inputs(seed, part) draws one part's arguments, and reference() takes and returns one part's arrays. A program takes and returns all parts, laid end to end along the dimension named above; each array names one. Nothing has to cross between parts.
All inputs are finite; a program needn't handle non-finite values.
Results may differ from the reference program's by a relative error of at most 0.0003.
Values sent between devices are 32-bit elements; how exact they have to be, the bound alone decides.
No kernel may reach another device: no remote copies, remote signals or barrier semaphores. Data moves between devices by JAX's collectives and lax.ppermute only.
A program may use at most 64 MiB of HBM per device.

```python
import math
import jax
import jax.numpy as jnp
from jax import lax

P_SIZE = 16
PTS_DEV = 24
ITERS = 3
HALF = 384
NPTS = 384
N_NARROW = 1


def draw_dissim(key, part):
    key = jax.random.fold_in(key, 11)
    key_rows, key_cols, key_cells = jax.random.split(key, 3)
    index = jnp.arange(NPTS, dtype=jnp.float32) / NPTS
    row_scale = jnp.exp(math.log(3.0) * index) * jax.random.uniform(key_rows, (NPTS,), jnp.float32, 0.7, 1.4)
    col_scale = jnp.exp(math.log(3.0) * index) * jax.random.uniform(key_cols, (NPTS,), jnp.float32, 0.7, 1.4)
    cells = jax.random.uniform(key_cells, (NPTS, NPTS), jnp.float32)
    factor = 0.5 + cells
    values = 1.5 * jnp.sqrt(row_scale[:, None] * col_scale[None, :]) * factor
    return values.reshape(N_NARROW, HALF, NPTS).astype(jnp.float32)


def draw_classes(key, part):
    key = jax.random.fold_in(key, 29)
    key_live, key_code = jax.random.split(key, 2)
    shape = (N_NARROW, HALF, NPTS)
    live = jax.random.randint(key_live, shape, 0, NPTS) < max(8, NPTS // 48)
    codes = jax.random.randint(key_code, shape, 1, 4)
    return jnp.where(live, codes, 0).astype(jnp.int32)


def draw_coords(key, part):
    key = jax.random.fold_in(key, 17)
    key_blocks, key_values = jax.random.split(key, 2)
    count = HALF // PTS_DEV
    levels = jax.random.uniform(key_blocks, (N_NARROW, count), jnp.float32, -1.5, 1.0)
    values = jax.random.normal(key_values, (P_SIZE, N_NARROW, HALF), jnp.float32)
    scale = 0.5 * jnp.exp(jnp.repeat(levels, PTS_DEV, axis=1))
    return jnp.clip(values * scale[None, :, :], -3.0, 3.0).astype(jnp.float32)


def setup_inputs(seed: int = 0, part: int = 0) -> dict:
    arg_keys = jax.random.split(jax.random.key(seed), 4)
    part_splits = jax.random.split(jax.random.fold_in(arg_keys[3], part), 4)
    dissim = draw_dissim(jax.random.fold_in(jax.random.fold_in(arg_keys[3], part), 71), part)
    classes = draw_classes(jax.random.fold_in(jax.random.fold_in(arg_keys[3], part), 71), part)
    coords = draw_coords(jax.random.fold_in(jax.random.fold_in(arg_keys[3], part), 71), part)
    return dict(dissim=dissim, classes=classes, coords=coords)


def class_weight(class_codes):
    return jnp.where(class_codes == 3, 1.0, jnp.where(class_codes == 2, 0.5, jnp.where(class_codes == 1, 0.25, 0.0))).astype(jnp.float32)

def reference(dissim, classes, coords):
    coord_dims = coords.shape[0]
    total_pts = dissim.shape[0] * dissim.shape[1]
    block = math.gcd(total_pts, 512)
    blocks = total_pts // block
    dissim_rows = dissim.reshape(blocks, block, total_pts)
    class_rows = classes.reshape(blocks, block, total_pts)
    positions = coords.reshape(coord_dims, total_pts)

    def normal_block(args):
        dis_blk, cls_blk = args
        weight = class_weight(cls_blk)
        return jnp.sum(weight * dis_blk * dis_blk)
    denom = jnp.sum(lax.map(normal_block, (dissim_rows, class_rows)))
    stresses = []
    for sweep in range(ITERS):
        col_sq = lax.optimization_barrier(jnp.sum(positions * positions, axis=0))
        row_blocks = positions.reshape(coord_dims, blocks, block).transpose(1, 0, 2)
        current = positions

        def row_block(args):
            dis_blk, cls_blk, row_x = args
            weight = class_weight(cls_blk)
            inner_prod = jnp.dot(row_x.T, current, precision=lax.Precision.HIGHEST, preferred_element_type=jnp.float32)
            row_sq = lax.optimization_barrier(jnp.sum(row_x * row_x, axis=0))
            distance = jnp.sqrt(row_sq[:, None] + col_sq[None, :] - 2.0 * inner_prod + 1.0)
            ratios = weight * dis_blk / distance
            pull_term = jnp.dot(weight - ratios, current.T, precision=lax.Precision.HIGHEST, preferred_element_type=jnp.float32)
            misfit = dis_blk - distance
            return (lax.optimization_barrier(jnp.sum(weight, axis=1)), lax.optimization_barrier(jnp.sum(ratios, axis=1)), pull_term, jnp.sum(weight * misfit * misfit))
        wsum, rsum, pulls, misfits = lax.map(row_block, (dissim_rows, class_rows, row_blocks))
        stresses.append(jnp.sum(misfits) / denom)
        wsum = wsum.reshape(total_pts)
        rsum = rsum.reshape(total_pts)
        pulls = pulls.reshape(total_pts, coord_dims).T
        positions = (positions * (1.0 + rsum) + pulls) / (1.0 + wsum)
    return (positions.reshape(coords.shape), jnp.stack(stresses))
```

```python
import functools

import jax
import jax.numpy as jnp
from jax import lax
from jax.experimental import pallas as pl
from jax.experimental.pallas import tpu as pltpu
from jax.sharding import PartitionSpec as P

ITERS = 3
REPLICATED_BYTES = 1 << 22
HIGHEST = lax.Precision.HIGHEST


def class_weight(class_codes):
    return jnp.where(
        class_codes == 3,
        1.0,
        jnp.where(class_codes == 2, 0.5, jnp.where(class_codes == 1, 0.25, 0.0)),
    ).astype(jnp.float32)


def group_kernel(per_dev, dis_ref, cls_ref, x_ref, out_ref, stress_ref, w_ref, wd_ref):
    weight = class_weight(cls_ref[...])
    dis = dis_ref[...]
    weighted = weight * dis
    w_ref[...] = weight
    wd_ref[...] = weighted
    denom = jnp.sum(weighted * dis)
    x = x_ref[...]
    ones = jnp.ones((8, x.shape[1]), jnp.float32)
    nt = (((1,), (1,)), ((), ()))
    dot = functools.partial(
        lax.dot_general, dimension_numbers=nt, precision=HIGHEST, preferred_element_type=jnp.float32
    )
    weight_sum = dot(ones, weight)[0:1]
    for sweep in range(ITERS):
        xt = x.T
        col_sq = jnp.sum(x * x, axis=0, keepdims=True)
        row_sq = jnp.sum(xt * xt, axis=1, keepdims=True)
        inner = jnp.dot(xt, x, precision=HIGHEST, preferred_element_type=jnp.float32)
        distance = jnp.sqrt(row_sq + col_sq - 2.0 * inner + 1.0)
        ratios = wd_ref[...] / distance
        misfit = dis_ref[...] - distance
        stress_ref[sweep] = jnp.sum(w_ref[...] * misfit * misfit) / denom
        pull = dot(x, w_ref[...] - ratios)
        ratio_sum = dot(ones, ratios)[0:1]
        x = (x * (1.0 + ratio_sum) + pull) / (1.0 + weight_sum)
    mine = lax.axis_index("wide") * per_dev
    points = x.shape[1]
    pick = lax.broadcasted_iota(jnp.int32, (points, per_dev), 0) == mine + lax.broadcasted_iota(
        jnp.int32, (points, per_dev), 1
    )
    out_ref[...] = jnp.dot(
        x, pick.astype(jnp.float32), precision=HIGHEST, preferred_element_type=jnp.float32
    )


def replicated_body(dissim, classes, coords):
    coord_dims, _, per_dev = coords.shape
    columns = dissim.shape[2]
    dis = lax.all_gather(dissim[0], "wide", axis=0, tiled=True)
    cls = lax.all_gather(classes[0], "wide", axis=0, tiled=True)
    x = lax.all_gather(coords[:, 0, :].T, "wide", axis=0, tiled=True).T
    vmem = pl.BlockSpec(memory_space=pltpu.VMEM)
    final, stress = pl.pallas_call(
        functools.partial(group_kernel, per_dev),
        out_shape=(
            jax.ShapeDtypeStruct((coord_dims, per_dev), jnp.float32),
            jax.ShapeDtypeStruct((ITERS,), jnp.float32),
        ),
        in_specs=[vmem, vmem, vmem],
        out_specs=(vmem, pl.BlockSpec(memory_space=pltpu.SMEM)),
        scratch_shapes=[
            pltpu.VMEM((columns, columns), jnp.float32),
            pltpu.VMEM((columns, columns), jnp.float32),
        ],
        compiler_params=pltpu.CompilerParams(vmem_limit_bytes=32 << 20),
        cost_estimate=pl.CostEstimate(
            flops=ITERS * 24 * columns * columns * coord_dims,
            bytes_accessed=8 * columns * columns,
            transcendentals=ITERS * columns * columns,
        ),
        name="group_smacof",
    )(dis, cls, x)
    return (final[:, None, :], stress)


def distributed_body(dissim, classes, coords):
    halves = dissim.shape[0]
    per_dev = dissim.shape[1]
    columns = dissim.shape[2]
    coord_dims = coords.shape[0]
    row_count = halves * per_dev
    dis_tile = dissim.reshape(row_count, columns)
    weight = class_weight(classes.reshape(row_count, columns))
    denom_local = jnp.sum(weight * dis_tile * dis_tile)
    half_index = lax.axis_index("narrow")
    denom_total = lax.psum(denom_local, ("wide", "narrow"))
    positions = coords
    numbers = []
    for sweep in range(ITERS):
        row_points = lax.all_gather(positions, "narrow", axis=1, tiled=True)
        row_x = row_points.reshape(coord_dims, row_count)
        row_sq = jnp.sum(row_x * row_x, axis=0)
        fold_column_x = lax.dynamic_index_in_dim(
            lax.all_gather(row_points, "wide", axis=2, tiled=True), half_index, 1, keepdims=False
        )
        inner_prod = lax.dot_general(
            row_x,
            fold_column_x,
            (((0,), (0,)), ((), ())),
            precision=lax.Precision.HIGHEST,
            preferred_element_type=jnp.float32,
        )
        col_sq = jnp.sum(fold_column_x * fold_column_x, axis=0)
        distance = jnp.sqrt(row_sq[:, None] + col_sq[None, :] - 2.0 * inner_prod + 1.0)
        ratios = weight * dis_tile / distance
        pull_term = lax.dot_general(
            weight - ratios,
            fold_column_x,
            (((1,), (1,)), ((), ())),
            precision=lax.Precision.HIGHEST,
            preferred_element_type=jnp.float32,
        )
        misfit = dis_tile - distance
        pull_sums = pull_term.reshape(halves, per_dev, coord_dims).transpose(0, 2, 1)
        weight_sum, ratio_sum, pull_share = (
            lax.psum_scatter(
                jnp.sum(weight, axis=1).reshape(halves, per_dev),
                "narrow",
                scatter_dimension=0,
                tiled=True,
            ),
            lax.psum_scatter(
                jnp.sum(ratios, axis=1).reshape(halves, per_dev),
                "narrow",
                scatter_dimension=0,
                tiled=True,
            ),
            lax.psum_scatter(pull_sums, "narrow", scatter_dimension=0, tiled=True),
        )
        own_coords = positions[:, 0, :]
        updated = (own_coords * (1.0 + ratio_sum[0]) + pull_share[0]) / (1.0 + weight_sum[0])
        positions = updated[:, None, :]
        numbers.append(
            lax.psum(jnp.sum(weight * misfit * misfit), ("wide", "narrow")) / denom_total
        )
    stress = jnp.stack(numbers)
    return (positions, stress)


def solution(mesh):
    def body(dissim, classes, coords):
        group_bytes = 8 * dissim.size * mesh.shape["wide"]
        small = mesh.shape["narrow"] == 1 and group_bytes <= REPLICATED_BYTES
        return (replicated_body if small else distributed_body)(dissim, classes, coords)

    return jax.shard_map(
        body,
        mesh=mesh,
        in_specs=(
            P(None, ("grp", "wide"), "narrow"),
            P(None, ("grp", "wide"), "narrow"),
            P(None, "narrow", ("grp", "wide")),
        ),
        out_specs=(P(None, "narrow", ("grp", "wide")), P("grp")),
        check_vma=False,
    )
```

```python
import functools

import jax
import jax.numpy as jnp
from jax import lax
from jax.experimental import pallas as pl
from jax.experimental.pallas import tpu as pltpu
from jax.sharding import PartitionSpec as P

ITERS = 3
REPLICATED_BYTES = 1 << 22
LANES = 128


def class_weight(class_codes):
    return jnp.where(
        class_codes == 3,
        1.0,
        jnp.where(class_codes == 2, 0.5, jnp.where(class_codes == 1, 0.25, 0.0)),
    ).astype(jnp.float32)


def split_bf16(value, terms):
    parts = []
    for _ in range(terms):
        part = value.astype(jnp.bfloat16)
        parts.append(part)
        value = value - part.astype(jnp.float32)
    return parts


def pack_kernel(dis_ref, cls_ref, x_ref, out_ref):
    columns = dis_ref.shape[1]
    coord_dims, per_dev = x_ref.shape
    out_ref[:, :columns] = dis_ref[...]
    out_ref[:, columns : 2 * columns] = class_weight(cls_ref[...])
    padded = jnp.concatenate(
        [x_ref[...], jnp.zeros((LANES - coord_dims, per_dev), jnp.float32)], axis=0
    )
    out_ref[:, 2 * columns :] = padded.T


def group_kernel(per_dev, coord_dims, data_ref, out_ref, stress_ref, wd_ref):
    points = data_ref.shape[0]
    dis = data_ref[:, :points]
    weight = data_ref[:, points : 2 * points]
    weighted = weight * dis
    wd_ref[...] = weighted
    denom = jnp.sum(weighted * dis)
    x = data_ref[:, 2 * points :].T[:coord_dims]
    nt = (((1,), (1,)), ((), ()))
    tn = (((0,), (0,)), ((), ()))
    dot = functools.partial(lax.dot_general, preferred_element_type=jnp.float32)
    ones = jnp.ones((coord_dims, points), jnp.bfloat16)
    one = jnp.ones((3, points), jnp.float32)
    pad = jnp.zeros((coord_dims - 6, points), jnp.float32)
    scale = 1.0 / (1.0 + dot(weight.astype(jnp.bfloat16), ones, nt).T[0:1])
    for sweep in range(ITERS):
        hi, mid, lo = split_bf16(x, 3)
        norm = jnp.sum(x * x, axis=0, keepdims=True)
        row_norm = [p.astype(jnp.float32) for p in split_bf16(norm, 3)]
        col_norm = [p.astype(jnp.float32) for p in split_bf16(norm + 1.0, 3)]
        left_norm = jnp.concatenate([*row_norm, one, pad], axis=0).astype(jnp.bfloat16)
        right_norm = jnp.concatenate([one, *col_norm, pad], axis=0).astype(jnp.bfloat16)
        left = jnp.concatenate(
            [-2.0 * hi, -2.0 * hi, -2.0 * hi, -2.0 * mid, -2.0 * mid, -2.0 * lo, left_norm], axis=0
        )
        right = jnp.concatenate([hi, mid, lo, hi, mid, hi, right_norm], axis=0)
        square = dot(left, right, tn)
        inverse = lax.rsqrt(square)
        weight = data_ref[:, points : 2 * points]
        misfit = data_ref[:, :points] - square * inverse
        stress_ref[sweep] = jnp.sum(weight * misfit * misfit) / denom
        pull_hi, pull_lo = split_bf16(weight - wd_ref[...] * inverse, 2)
        sides = jnp.concatenate([hi, mid, ones], axis=0)
        sums = (dot(pull_hi, sides, nt) + dot(pull_lo, sides, nt)).T
        pull = sums[:coord_dims] + sums[coord_dims : 2 * coord_dims]
        x = x + (pull - x * sums[2 * coord_dims : 2 * coord_dims + 1]) * scale
    mine = lax.axis_index("wide") * per_dev
    shape = (points, per_dev)
    pick = lax.broadcasted_iota(jnp.int32, shape, 0) == mine + lax.broadcasted_iota(
        jnp.int32, shape, 1
    )
    pick = pick.astype(jnp.float32).astype(jnp.bfloat16)
    out_ref[...] = sum(dot(p, pick, (((1,), (0,)), ((), ()))) for p in split_bf16(x, 3))


def replicated_body(dissim, classes, coords):
    coord_dims, _, per_dev = coords.shape
    points = dissim.shape[2]
    vmem = pl.BlockSpec(memory_space=pltpu.VMEM)
    params = pltpu.CompilerParams(vmem_limit_bytes=32 << 20)
    packed = pl.pallas_call(
        pack_kernel,
        out_shape=jax.ShapeDtypeStruct((per_dev, 2 * points + LANES), jnp.float32),
        in_specs=[vmem, vmem, vmem],
        out_specs=vmem,
        compiler_params=params,
        name="pack_rows",
    )(dissim[0], classes[0], coords[:, 0, :])
    data = lax.all_gather(packed, "wide", axis=0, tiled=True)
    final, stress = pl.pallas_call(
        functools.partial(group_kernel, per_dev, coord_dims),
        out_shape=(
            jax.ShapeDtypeStruct((coord_dims, per_dev), jnp.float32),
            jax.ShapeDtypeStruct((ITERS,), jnp.float32),
        ),
        in_specs=[vmem],
        out_specs=(vmem, pl.BlockSpec(memory_space=pltpu.SMEM)),
        scratch_shapes=[pltpu.VMEM((points, points), jnp.float32)],
        compiler_params=params,
        cost_estimate=pl.CostEstimate(
            flops=ITERS * 24 * points * points * coord_dims,
            bytes_accessed=8 * points * points,
            transcendentals=ITERS * points * points,
        ),
        name="group_smacof",
    )(data)
    return (final[:, None, :], stress)


def distributed_body(dissim, classes, coords):
    halves = dissim.shape[0]
    per_dev = dissim.shape[1]
    columns = dissim.shape[2]
    coord_dims = coords.shape[0]
    row_count = halves * per_dev
    dis_tile = dissim.reshape(row_count, columns)
    weight = class_weight(classes.reshape(row_count, columns))
    denom_local = jnp.sum(weight * dis_tile * dis_tile)
    half_index = lax.axis_index("narrow")
    denom_total = lax.psum(denom_local, ("wide", "narrow"))
    positions = coords
    numbers = []
    for sweep in range(ITERS):
        row_points = lax.all_gather(positions, "narrow", axis=1, tiled=True)
        row_x = row_points.reshape(coord_dims, row_count)
        row_sq = jnp.sum(row_x * row_x, axis=0)
        fold_column_x = lax.dynamic_index_in_dim(
            lax.all_gather(row_points, "wide", axis=2, tiled=True), half_index, 1, keepdims=False
        )
        inner_prod = lax.dot_general(
            row_x,
            fold_column_x,
            (((0,), (0,)), ((), ())),
            precision=lax.Precision.HIGHEST,
            preferred_element_type=jnp.float32,
        )
        col_sq = jnp.sum(fold_column_x * fold_column_x, axis=0)
        distance = jnp.sqrt(row_sq[:, None] + col_sq[None, :] - 2.0 * inner_prod + 1.0)
        ratios = weight * dis_tile / distance
        pull_term = lax.dot_general(
            weight - ratios,
            fold_column_x,
            (((1,), (1,)), ((), ())),
            precision=lax.Precision.HIGHEST,
            preferred_element_type=jnp.float32,
        )
        misfit = dis_tile - distance
        pull_sums = pull_term.reshape(halves, per_dev, coord_dims).transpose(0, 2, 1)
        weight_sum, ratio_sum, pull_share = (
            lax.psum_scatter(
                jnp.sum(weight, axis=1).reshape(halves, per_dev),
                "narrow",
                scatter_dimension=0,
                tiled=True,
            ),
            lax.psum_scatter(
                jnp.sum(ratios, axis=1).reshape(halves, per_dev),
                "narrow",
                scatter_dimension=0,
                tiled=True,
            ),
            lax.psum_scatter(pull_sums, "narrow", scatter_dimension=0, tiled=True),
        )
        own_coords = positions[:, 0, :]
        updated = (own_coords * (1.0 + ratio_sum[0]) + pull_share[0]) / (1.0 + weight_sum[0])
        positions = updated[:, None, :]
        numbers.append(
            lax.psum(jnp.sum(weight * misfit * misfit), ("wide", "narrow")) / denom_total
        )
    stress = jnp.stack(numbers)
    return (positions, stress)


def solution(mesh):
    def body(dissim, classes, coords):
        group_bytes = 8 * dissim.size * mesh.shape["wide"]
        small = mesh.shape["narrow"] == 1 and group_bytes <= REPLICATED_BYTES
        return (replicated_body if small else distributed_body)(dissim, classes, coords)

    return jax.shard_map(
        body,
        mesh=mesh,
        in_specs=(
            P(None, ("grp", "wide"), "narrow"),
            P(None, ("grp", "wide"), "narrow"),
            P(None, "narrow", ("grp", "wide")),
        ),
        out_specs=(P(None, "narrow", ("grp", "wide")), P("grp")),
        check_vma=False,
    )
```

```python
import functools

import jax
import jax.numpy as jnp
from jax import lax
from jax.experimental import pallas as pl
from jax.experimental.pallas import tpu as pltpu
from jax.sharding import PartitionSpec as P

ITERS = 3
REPLICATED_BYTES = 1 << 22
LANES = 128


def class_weight(class_codes):
    return jnp.where(
        class_codes == 3,
        1.0,
        jnp.where(class_codes == 2, 0.5, jnp.where(class_codes == 1, 0.25, 0.0)),
    ).astype(jnp.float32)


def split_bf16(value, terms):
    parts = []
    for _ in range(terms):
        part = value.astype(jnp.bfloat16)
        parts.append(part)
        value = value - part.astype(jnp.float32)
    return parts


def pack_kernel(dis_hbm, cls_hbm, x_hbm, out_ref, cls_ref, x_ref, sems):
    columns = cls_ref.shape[1]
    copies = [
        pltpu.make_async_copy(dis_hbm, out_ref.at[:, :columns], sems.at[0]),
        pltpu.make_async_copy(cls_hbm, cls_ref, sems.at[1]),
        pltpu.make_async_copy(x_hbm, x_ref, sems.at[2]),
    ]
    for copy in copies:
        copy.start()
    for copy in copies:
        copy.wait()
    out_ref[:, columns : 2 * columns] = class_weight(cls_ref[...])
    coord_dims, per_dev = x_ref.shape
    padded = jnp.concatenate(
        [x_ref[...], jnp.zeros((LANES - coord_dims, per_dev), jnp.float32)], axis=0
    )
    out_ref[:, 2 * columns :] = padded.T


def group_kernel(per_dev, coord_dims, offsets, slots_ref, out_ref, stress_ref, data_ref, wd_ref):
    points = data_ref.shape[0]
    me = lax.axis_index("wide")
    for slot, offset in enumerate(offsets):
        rows = pl.ds(pl.multiple_of((me ^ offset) * per_dev, 8), per_dev)
        data_ref[rows, :] = slots_ref[slot * per_dev : (slot + 1) * per_dev, :]
    dis = data_ref[:, :points]
    weight = data_ref[:, points : 2 * points]
    weighted = weight * dis
    wd_ref[...] = weighted
    denom = jnp.sum(weighted * dis)
    x = data_ref[:, 2 * points :].T[:coord_dims]
    nt = (((1,), (1,)), ((), ()))
    tn = (((0,), (0,)), ((), ()))
    dot = functools.partial(lax.dot_general, preferred_element_type=jnp.float32)
    ones = jnp.ones((coord_dims, points), jnp.bfloat16)
    one = jnp.ones((3, points), jnp.float32)
    pad = jnp.zeros((coord_dims - 6, points), jnp.float32)
    scale = 1.0 / (1.0 + dot(weight.astype(jnp.bfloat16), ones, nt).T[0:1])
    for sweep in range(ITERS):
        hi, mid, lo = split_bf16(x, 3)
        norm = jnp.sum(x * x, axis=0, keepdims=True)
        row_norm = [p.astype(jnp.float32) for p in split_bf16(norm, 3)]
        col_norm = [p.astype(jnp.float32) for p in split_bf16(norm + 1.0, 3)]
        left_norm = jnp.concatenate([*row_norm, one, pad], axis=0).astype(jnp.bfloat16)
        right_norm = jnp.concatenate([one, *col_norm, pad], axis=0).astype(jnp.bfloat16)
        left = jnp.concatenate(
            [-2.0 * hi, -2.0 * hi, -2.0 * hi, -2.0 * mid, -2.0 * mid, -2.0 * lo, left_norm], axis=0
        )
        right = jnp.concatenate([hi, mid, lo, hi, mid, hi, right_norm], axis=0)
        square = dot(left, right, tn)
        inverse = lax.rsqrt(square)
        weight = data_ref[:, points : 2 * points]
        misfit = data_ref[:, :points] - square * inverse
        stress_ref[sweep] = jnp.sum(weight * misfit * misfit) / denom
        pull_hi, pull_lo = split_bf16(weight - wd_ref[...] * inverse, 2)
        sides = jnp.concatenate([hi, mid, ones], axis=0)
        sums = (dot(pull_hi, sides, nt) + dot(pull_lo, sides, nt)).T
        pull = sums[:coord_dims] + sums[coord_dims : 2 * coord_dims]
        x = x + (pull - x * sums[2 * coord_dims : 2 * coord_dims + 1]) * scale
    mine = me * per_dev
    shape = (points, per_dev)
    pick = lax.broadcasted_iota(jnp.int32, shape, 0) == mine + lax.broadcasted_iota(
        jnp.int32, shape, 1
    )
    pick = pick.astype(jnp.float32).astype(jnp.bfloat16)
    out_ref[...] = sum(dot(p, pick, (((1,), (0,)), ((), ()))) for p in split_bf16(x, 3))


def exchange(block, devices):
    held, offsets = block, [0]
    distance = devices // 2
    while distance:
        other = lax.ppermute(held, "wide", [(i, i ^ distance) for i in range(devices)])
        held = jnp.concatenate([held, other], axis=0)
        offsets += [offset ^ distance for offset in offsets]
        distance //= 2
    return held, offsets


def replicated_body(dissim, classes, coords):
    coord_dims, _, per_dev = coords.shape
    points = dissim.shape[2]
    vmem = pl.BlockSpec(memory_space=pltpu.VMEM)
    hbm = pl.BlockSpec(memory_space=pl.ANY)
    params = pltpu.CompilerParams(vmem_limit_bytes=32 << 20)
    packed = pl.pallas_call(
        pack_kernel,
        out_shape=jax.ShapeDtypeStruct((per_dev, 2 * points + LANES), jnp.float32),
        in_specs=[hbm, hbm, hbm],
        out_specs=vmem,
        scratch_shapes=[
            pltpu.VMEM((per_dev, points), jnp.int32),
            pltpu.VMEM((coord_dims, per_dev), jnp.float32),
            pltpu.SemaphoreType.DMA((3,)),
        ],
        compiler_params=params,
        name="pack_rows",
    )(dissim[0], classes[0], coords[:, 0, :])
    data, offsets = exchange(packed, points // per_dev)
    final, stress = pl.pallas_call(
        functools.partial(group_kernel, per_dev, coord_dims, offsets),
        out_shape=(
            jax.ShapeDtypeStruct((coord_dims, per_dev), jnp.float32),
            jax.ShapeDtypeStruct((ITERS,), jnp.float32),
        ),
        in_specs=[vmem],
        out_specs=(vmem, pl.BlockSpec(memory_space=pltpu.SMEM)),
        scratch_shapes=[
            pltpu.VMEM((points, 2 * points + LANES), jnp.float32),
            pltpu.VMEM((points, points), jnp.float32),
        ],
        compiler_params=params,
        cost_estimate=pl.CostEstimate(
            flops=ITERS * 24 * points * points * coord_dims,
            bytes_accessed=8 * points * points,
            transcendentals=ITERS * points * points,
        ),
        name="group_smacof",
    )(data)
    return (final[:, None, :], stress)


def distributed_body(dissim, classes, coords):
    halves = dissim.shape[0]
    per_dev = dissim.shape[1]
    columns = dissim.shape[2]
    coord_dims = coords.shape[0]
    row_count = halves * per_dev
    dis_tile = dissim.reshape(row_count, columns)
    weight = class_weight(classes.reshape(row_count, columns))
    denom_local = jnp.sum(weight * dis_tile * dis_tile)
    half_index = lax.axis_index("narrow")
    denom_total = lax.psum(denom_local, ("wide", "narrow"))
    positions = coords
    numbers = []
    for sweep in range(ITERS):
        row_points = lax.all_gather(positions, "narrow", axis=1, tiled=True)
        row_x = row_points.reshape(coord_dims, row_count)
        row_sq = jnp.sum(row_x * row_x, axis=0)
        fold_column_x = lax.dynamic_index_in_dim(
            lax.all_gather(row_points, "wide", axis=2, tiled=True), half_index, 1, keepdims=False
        )
        inner_prod = lax.dot_general(
            row_x,
            fold_column_x,
            (((0,), (0,)), ((), ())),
            precision=lax.Precision.HIGHEST,
            preferred_element_type=jnp.float32,
        )
        col_sq = jnp.sum(fold_column_x * fold_column_x, axis=0)
        distance = jnp.sqrt(row_sq[:, None] + col_sq[None, :] - 2.0 * inner_prod + 1.0)
        ratios = weight * dis_tile / distance
        pull_term = lax.dot_general(
            weight - ratios,
            fold_column_x,
            (((1,), (1,)), ((), ())),
            precision=lax.Precision.HIGHEST,
            preferred_element_type=jnp.float32,
        )
        misfit = dis_tile - distance
        pull_sums = pull_term.reshape(halves, per_dev, coord_dims).transpose(0, 2, 1)
        weight_sum, ratio_sum, pull_share = (
            lax.psum_scatter(
                jnp.sum(weight, axis=1).reshape(halves, per_dev),
                "narrow",
                scatter_dimension=0,
                tiled=True,
            ),
            lax.psum_scatter(
                jnp.sum(ratios, axis=1).reshape(halves, per_dev),
                "narrow",
                scatter_dimension=0,
                tiled=True,
            ),
            lax.psum_scatter(pull_sums, "narrow", scatter_dimension=0, tiled=True),
        )
        own_coords = positions[:, 0, :]
        updated = (own_coords * (1.0 + ratio_sum[0]) + pull_share[0]) / (1.0 + weight_sum[0])
        positions = updated[:, None, :]
        numbers.append(
            lax.psum(jnp.sum(weight * misfit * misfit), ("wide", "narrow")) / denom_total
        )
    stress = jnp.stack(numbers)
    return (positions, stress)


def solution(mesh):
    def body(dissim, classes, coords):
        group_bytes = 8 * dissim.size * mesh.shape["wide"]
        devices = mesh.shape["wide"]
        whole = mesh.shape["narrow"] == 1 and group_bytes <= REPLICATED_BYTES
        small = whole and devices & (devices - 1) == 0 and dissim.shape[1] % 8 == 0
        return (replicated_body if small else distributed_body)(dissim, classes, coords)

    return jax.shard_map(
        body,
        mesh=mesh,
        in_specs=(
            P(None, ("grp", "wide"), "narrow"),
            P(None, ("grp", "wide"), "narrow"),
            P(None, "narrow", ("grp", "wide")),
        ),
        out_specs=(P(None, "narrow", ("grp", "wide")), P("grp")),
        check_vma=False,
    )
```

```python
import functools

import jax
import jax.numpy as jnp
from jax import lax
from jax.experimental import pallas as pl
from jax.experimental.pallas import tpu as pltpu
from jax.sharding import PartitionSpec as P

ITERS = 3
LANES = 128


def class_weight(class_codes):
    return jnp.where(
        class_codes == 3,
        1.0,
        jnp.where(class_codes == 2, 0.5, jnp.where(class_codes == 1, 0.25, 0.0)),
    ).astype(jnp.float32)


def split_bf16(value, terms):
    parts = []
    for _ in range(terms):
        part = value.astype(jnp.bfloat16)
        parts.append(part)
        value = value - part.astype(jnp.float32)
    return parts


def as_tile(x):
    half = x.shape[0] // 2
    pad = jnp.zeros((half, LANES - 2 * x.shape[1]), jnp.float32)
    return jnp.concatenate([x[:half], x[half:], pad], axis=1)


def from_tiles(tiles_ref, per_dev):
    tiles = [tiles_ref[i] for i in range(tiles_ref.shape[0])]
    top = jnp.concatenate([t[:, :per_dev] for t in tiles], axis=1)
    bottom = jnp.concatenate([t[:, per_dev : 2 * per_dev] for t in tiles], axis=1)
    return jnp.concatenate([top, bottom], axis=0)


def lane_sums(value):
    rows = jnp.sum(value, axis=0, keepdims=True)
    return sum(rows[:, i : i + LANES] for i in range(0, rows.shape[1], LANES))


def start_kernel(x_ref, tiles_ref):
    tiles_ref[...] = jnp.broadcast_to(as_tile(x_ref[...])[None], tiles_ref.shape)


def sweep_kernel(last, dis_ref, cls_ref, x_ref, tiles_ref, sums_ref, out_ref, send_ref):
    coord_dims, per_dev = x_ref.shape
    points = dis_ref.shape[1]
    nt = (((1,), (1,)), ((), ()))
    tn = (((0,), (0,)), ((), ()))
    dot = functools.partial(lax.dot_general, preferred_element_type=jnp.float32)
    dis = dis_ref[...]
    weight = class_weight(cls_ref[...])
    weighted = weight * dis
    own = x_ref[...]
    x = from_tiles(tiles_ref, per_dev)
    ones = jnp.ones((coord_dims, points), jnp.bfloat16)
    own_hi, own_mid, own_lo = (-2.0 * p for p in split_bf16(own, 3))
    hi, mid, lo = split_bf16(x, 3)
    norm = jnp.sum(x * x, axis=0, keepdims=True)
    own_norm = jnp.sum(own * own, axis=0, keepdims=True)
    row_norm = [p.astype(jnp.float32) for p in split_bf16(own_norm, 3)]
    col_norm = [p.astype(jnp.float32) for p in split_bf16(norm + 1.0, 3)]
    left_norm = jnp.concatenate(
        [
            *row_norm,
            jnp.ones((3, per_dev), jnp.float32),
            jnp.zeros((coord_dims - 6, per_dev), jnp.float32),
        ],
        axis=0,
    ).astype(jnp.bfloat16)
    right_norm = jnp.concatenate(
        [
            jnp.ones((3, points), jnp.float32),
            *col_norm,
            jnp.zeros((coord_dims - 6, points), jnp.float32),
        ],
        axis=0,
    ).astype(jnp.bfloat16)
    left = jnp.concatenate(
        [own_hi, own_hi, own_hi, own_mid, own_mid, own_lo, left_norm], axis=0
    )
    right = jnp.concatenate([hi, mid, lo, hi, mid, hi, right_norm], axis=0)
    square = dot(left, right, tn)
    inverse = lax.rsqrt(square)
    misfit = dis - square * inverse
    pulls = jnp.concatenate(
        [*split_bf16(weight - weighted * inverse, 2), weight.astype(jnp.bfloat16)], axis=0
    )
    sides = jnp.concatenate([hi, mid, ones], axis=0)
    sums = dot(pulls, sides, nt).T
    weight_sum = sums[2 * coord_dims : 2 * coord_dims + 1, 2 * per_dev :]
    sums = sums[:, :per_dev] + sums[:, per_dev : 2 * per_dev]
    pull = sums[:coord_dims] + sums[coord_dims : 2 * coord_dims]
    own = own + (pull - own * sums[2 * coord_dims : 2 * coord_dims + 1]) / (1.0 + weight_sum)
    out_ref[...] = own
    stress = lane_sums(weight * misfit * misfit)
    if last:
        rows = [sums_ref[0:1], sums_ref[1:2], stress, lane_sums(weighted * dis)]
        pad = jnp.zeros((4, LANES), jnp.float32)
        send = jnp.concatenate([*rows, pad], axis=0)
    else:
        send = as_tile(own)
    send_ref[...] = jnp.broadcast_to(send[None], send_ref.shape)
    return stress


def early_kernel(dis_ref, cls_ref, x_ref, tiles_ref, stress_ref, out_ref, send_ref):
    stress_ref[...] = sweep_kernel(
        False, dis_ref, cls_ref, x_ref, tiles_ref, None, out_ref, send_ref
    )


def late_kernel(dis_ref, cls_ref, x_ref, tiles_ref, first_ref, second_ref, out_ref, send_ref):
    sums = jnp.concatenate([first_ref[...], second_ref[...]], axis=0)
    sweep_kernel(True, dis_ref, cls_ref, x_ref, tiles_ref, sums, out_ref, send_ref)


def stress_kernel(tiles_ref, stress_ref):
    total = tiles_ref[0]
    for i in range(1, tiles_ref.shape[0]):
        total = total + tiles_ref[i]
    total = jnp.sum(total, axis=1, keepdims=True)
    for sweep in range(ITERS):
        stress_ref[sweep] = jnp.sum(total[sweep : sweep + 1] / total[ITERS : ITERS + 1])


def small_body(dissim, classes, coords):
    coord_dims, _, per_dev = coords.shape
    points = dissim.shape[2]
    devices = points // per_dev
    vmem = pl.BlockSpec(memory_space=pltpu.VMEM)
    call = functools.partial(
        pl.pallas_call, compiler_params=pltpu.CompilerParams(vmem_limit_bytes=16 << 20)
    )
    tiles_shape = jax.ShapeDtypeStruct((devices, coord_dims // 2, LANES), jnp.float32)
    x_shape = jax.ShapeDtypeStruct((coord_dims, per_dev), jnp.float32)
    sums_shape = jax.ShapeDtypeStruct((1, LANES), jnp.float32)
    dis, cls, x = dissim[0], classes[0], coords[:, 0, :]
    swap = functools.partial(
        lax.all_to_all, axis_name="wide", split_axis=0, concat_axis=0, tiled=True
    )
    tiles = swap(
        call(start_kernel, out_shape=tiles_shape, in_specs=[vmem], out_specs=vmem, name="start")(x)
    )
    stresses = []
    for sweep in range(ITERS - 1):
        stress, x, tiles = call(
            early_kernel,
            out_shape=(sums_shape, x_shape, tiles_shape),
            in_specs=[vmem] * 4,
            out_specs=(vmem,) * 3,
            name="sweep",
        )(dis, cls, x, tiles)
        tiles = swap(tiles)
        stresses.append(stress)
    x, tiles = call(
        late_kernel,
        out_shape=(x_shape, tiles_shape),
        in_specs=[vmem] * 6,
        out_specs=(vmem,) * 2,
        name="last_sweep",
    )(dis, cls, x, tiles, *stresses)
    stress = call(
        stress_kernel,
        out_shape=jax.ShapeDtypeStruct((ITERS,), jnp.float32),
        in_specs=[vmem],
        out_specs=pl.BlockSpec(memory_space=pltpu.SMEM),
        name="stress",
    )(swap(tiles))
    return (x[:, None, :], stress)


def distributed_body(dissim, classes, coords):
    halves = dissim.shape[0]
    per_dev = dissim.shape[1]
    columns = dissim.shape[2]
    coord_dims = coords.shape[0]
    row_count = halves * per_dev
    dis_tile = dissim.reshape(row_count, columns)
    weight = class_weight(classes.reshape(row_count, columns))
    denom_local = jnp.sum(weight * dis_tile * dis_tile)
    half_index = lax.axis_index("narrow")
    denom_total = lax.psum(denom_local, ("wide", "narrow"))
    positions = coords
    numbers = []
    for sweep in range(ITERS):
        row_points = lax.all_gather(positions, "narrow", axis=1, tiled=True)
        row_x = row_points.reshape(coord_dims, row_count)
        row_sq = jnp.sum(row_x * row_x, axis=0)
        fold_column_x = lax.dynamic_index_in_dim(
            lax.all_gather(row_points, "wide", axis=2, tiled=True), half_index, 1, keepdims=False
        )
        inner_prod = lax.dot_general(
            row_x,
            fold_column_x,
            (((0,), (0,)), ((), ())),
            precision=lax.Precision.HIGHEST,
            preferred_element_type=jnp.float32,
        )
        col_sq = jnp.sum(fold_column_x * fold_column_x, axis=0)
        distance = jnp.sqrt(row_sq[:, None] + col_sq[None, :] - 2.0 * inner_prod + 1.0)
        ratios = weight * dis_tile / distance
        pull_term = lax.dot_general(
            weight - ratios,
            fold_column_x,
            (((1,), (1,)), ((), ())),
            precision=lax.Precision.HIGHEST,
            preferred_element_type=jnp.float32,
        )
        misfit = dis_tile - distance
        pull_sums = pull_term.reshape(halves, per_dev, coord_dims).transpose(0, 2, 1)
        weight_sum, ratio_sum, pull_share = (
            lax.psum_scatter(
                jnp.sum(weight, axis=1).reshape(halves, per_dev),
                "narrow",
                scatter_dimension=0,
                tiled=True,
            ),
            lax.psum_scatter(
                jnp.sum(ratios, axis=1).reshape(halves, per_dev),
                "narrow",
                scatter_dimension=0,
                tiled=True,
            ),
            lax.psum_scatter(pull_sums, "narrow", scatter_dimension=0, tiled=True),
        )
        own_coords = positions[:, 0, :]
        updated = (own_coords * (1.0 + ratio_sum[0]) + pull_share[0]) / (1.0 + weight_sum[0])
        positions = updated[:, None, :]
        numbers.append(
            lax.psum(jnp.sum(weight * misfit * misfit), ("wide", "narrow")) / denom_total
        )
    stress = jnp.stack(numbers)
    return (positions, stress)


def solution(mesh):
    def body(dissim, classes, coords):
        coord_dims, halves, per_dev = coords.shape
        small = halves == 1 and mesh.shape["narrow"] == 1 and coord_dims == 16
        small = small and 2 * per_dev <= LANES and dissim.shape[2] % LANES == 0
        return (small_body if small else distributed_body)(dissim, classes, coords)

    return jax.shard_map(
        body,
        mesh=mesh,
        in_specs=(
            P(None, ("grp", "wide"), "narrow"),
            P(None, ("grp", "wide"), "narrow"),
            P(None, "narrow", ("grp", "wide")),
        ),
        out_specs=(P(None, "narrow", ("grp", "wide")), P("grp")),
        check_vma=False,
    )
```

```python
import functools

import jax
import jax.numpy as jnp
from jax import lax
from jax.experimental import pallas as pl
from jax.experimental.pallas import tpu as pltpu
from jax.sharding import PartitionSpec as P

ITERS = 3
LANES = 128
MOST_PAIRS = 1 << 19


def class_weight(class_codes):
    return jnp.where(
        class_codes == 3,
        1.0,
        jnp.where(class_codes == 2, 0.5, jnp.where(class_codes == 1, 0.25, 0.0)),
    ).astype(jnp.float32)


def split_bf16(value, terms):
    parts = []
    for _ in range(terms):
        part = value.astype(jnp.bfloat16)
        parts.append(part)
        value = value - part.astype(jnp.float32)
    return parts


SUBLANES = 8
NT = (((1,), (1,)), ((), ()))
TN = (((0,), (0,)), ((), ()))
dot = functools.partial(lax.dot_general, preferred_element_type=jnp.float32)


def lane_sums(value):
    rows = jnp.sum(value, axis=0, keepdims=True)
    return sum(rows[:, i : i + LANES] for i in range(0, rows.shape[1], LANES))


def tile_spots(per_dev, points):
    return [
        (slice(row, row + SUBLANES), slice(column, column + LANES))
        for row in range(0, per_dev, SUBLANES)
        for column in range(0, points, LANES)
    ]


def pack_kernel(dis_hbm, cls_hbm, x_hbm, out_ref, dis_ref, cls_ref, x_ref, sems):
    copies = [
        pltpu.make_async_copy(src, dst, sems.at[i])
        for i, (src, dst) in enumerate(
            [(dis_hbm, dis_ref), (cls_hbm, cls_ref), (x_hbm, x_ref)]
        )
    ]
    for copy in copies:
        copy.start()
    for copy in copies:
        copy.wait()
    spots = tile_spots(*dis_ref.shape)
    for i, spot in enumerate(spots):
        out_ref[i] = dis_ref[spot]
        out_ref[len(spots) + i] = class_weight(cls_ref[spot])
    half, per_dev = x_ref.shape[0] // 2, x_ref.shape[1]
    pad = jnp.zeros((half, LANES - 2 * per_dev), jnp.float32)
    out_ref[2 * len(spots)] = jnp.concatenate([x_ref[:half], x_ref[half:], pad], axis=1)


def held_slots(offsets, own_ref, other_ref, tiles):
    me = lax.axis_index("wide")
    held = 2 * len(offsets)
    for bit, ref in enumerate((own_ref, other_ref)):
        for slot, offset in enumerate(offsets):
            yield ref, slot * tiles, lax.rem(me ^ offset ^ bit, held)


def coords_kernel(offsets, per_dev, own_ref, other_ref, x_ref, tile_ref):
    tiles = own_ref.shape[0] // len(offsets)
    for ref, base, place in held_slots(offsets, own_ref, other_ref, tiles):
        tile_ref[place] = ref[base + tiles - 1]
    blocks = [tile_ref[i] for i in range(tile_ref.shape[0])]
    halves = [
        jnp.concatenate([t[:, low : low + per_dev] for t in blocks], axis=1)
        for low in (0, per_dev)
    ]
    x_ref[...] = jnp.concatenate(halves, axis=0)


def rows_kernel(offsets, per_dev, own_ref, other_ref, dis_ref, weight_ref, scale_ref, denom_ref):
    points = dis_ref.shape[1]
    tiles = own_ref.shape[0] // len(offsets)
    spots = tile_spots(per_dev, points)
    for ref, base, place in held_slots(offsets, own_ref, other_ref, tiles):
        for i, (rows, columns) in enumerate(spots):
            start = pl.multiple_of(place * per_dev + rows.start, SUBLANES)
            dis_ref[pl.ds(start, SUBLANES), columns] = ref[base + i]
            weight_ref[pl.ds(start, SUBLANES), columns] = ref[base + len(spots) + i]
    weight = weight_ref[...]
    ones = jnp.ones((16, points), jnp.bfloat16)
    scale_ref[...] = 1.0 / (1.0 + dot(weight.astype(jnp.bfloat16), ones, NT).T[0:1])
    denom_ref[...] = lane_sums(weight * dis_ref[...] * dis_ref[...])


def both_halves(own, other):
    first = lax.axis_index("wide") < lax.axis_size("wide") // 2
    low = jnp.where(first, own, other)
    high = jnp.where(first, other, own)
    return jnp.concatenate([low, high], axis=1)


def side_norm(top, bottom, coord_dims):
    pad = jnp.zeros((coord_dims - 6, top[0].shape[1]), jnp.float32)
    rows = [p.astype(jnp.float32) for p in (*top, *bottom)]
    return jnp.concatenate([*rows, pad], axis=0).astype(jnp.bfloat16)


def squares(own, x):
    coord_dims = x.shape[0]
    own_hi, own_mid, own_lo = (-2.0 * p for p in split_bf16(own, 3))
    hi, mid, lo = split_bf16(x, 3)
    own_norm = split_bf16(jnp.sum(own * own, axis=0, keepdims=True), 3)
    norm = split_bf16(jnp.sum(x * x, axis=0, keepdims=True) + 1.0, 3)
    left_ones = [jnp.ones((3, own.shape[1]), jnp.bfloat16)]
    right_ones = [jnp.ones((3, x.shape[1]), jnp.bfloat16)]
    left = [own_hi, own_hi, own_hi, own_mid, own_mid, own_lo]
    right = [hi, mid, lo, hi, mid, hi]
    left = jnp.concatenate([*left, side_norm(own_norm, left_ones, coord_dims)], axis=0)
    right = jnp.concatenate([*right, side_norm(right_ones, norm, coord_dims)], axis=0)
    return dot(left, right, TN), hi, mid


def moved(own, hi, mid, pull, scale):
    coord_dims, count = own.shape
    ones = jnp.ones((coord_dims, hi.shape[1]), jnp.bfloat16)
    sides = jnp.concatenate([hi, mid, ones], axis=0)
    sums = dot(jnp.concatenate(split_bf16(pull, 2), axis=0), sides, NT)
    sums = (sums[:count] + sums[count:]).T
    pulled = sums[:coord_dims] + sums[coord_dims : 2 * coord_dims]
    return own + (pulled - own * sums[2 * coord_dims : 2 * coord_dims + 1]) * scale


def sweep_kernel(dis_ref, weight_ref, scale_ref, own_ref, other_ref, x_ref, distance_ref):
    own = own_ref[...]
    square, hi, mid = squares(own, both_halves(own, other_ref[...]))
    inverse = lax.rsqrt(square)
    distance_ref[...] = square * inverse
    weight = weight_ref[...]
    x_ref[...] = moved(own, hi, mid, weight - weight * dis_ref[...] * inverse, scale_ref[...])


def stress_rows(distance, dis_ref, weight_ref):
    misfit = dis_ref[...] - distance
    return lane_sums(weight_ref[...] * misfit * misfit)


def stress_kernel(dis_ref, weight_ref, distance_ref, sums_ref):
    sums_ref[...] = stress_rows(distance_ref[...], dis_ref, weight_ref)


def last_kernel(dis_ref, weight_ref, own_ref, other_ref, first_ref, second_ref, denom_ref,
                sums_ref, inverse_ref):
    own = own_ref[...]
    square, _, _ = squares(own, both_halves(own, other_ref[...]))
    inverse = lax.rsqrt(square)
    inverse_ref[...] = inverse
    last = stress_rows(square * inverse, dis_ref, weight_ref)
    pad = jnp.zeros((SUBLANES - 4, LANES), jnp.float32)
    rows = [first_ref[...], second_ref[...], last, denom_ref[...], pad]
    sums_ref[...] = jnp.concatenate(rows, axis=0)


def final_kernel(per_dev, dis_ref, weight_ref, inverse_ref, scale_ref, own_ref, other_ref, x_ref):
    own = own_ref[...]
    blocks = own.shape[1] // per_dev
    place = lax.rem(lax.axis_index("wide"), blocks)
    hi, mid = split_bf16(both_halves(own, other_ref[...]), 2)
    rows = pl.ds(pl.multiple_of(place * per_dev, SUBLANES), per_dev)
    scaled = jnp.concatenate([own, jnp.broadcast_to(scale_ref[...], (SUBLANES, own.shape[1]))], axis=0)
    mine = jnp.zeros((scaled.shape[0], per_dev), jnp.float32)
    for i in range(blocks):
        mine = jnp.where(place == i, scaled[:, i * per_dev : (i + 1) * per_dev], mine)
    own, scale = mine[: own.shape[0]], mine[own.shape[0] : own.shape[0] + 1]
    weight = weight_ref[rows, :]
    pull = weight - weight * dis_ref[rows, :] * inverse_ref[rows, :]
    x_ref[...] = moved(own, hi, mid, pull, scale)


def total_kernel(own_ref, other_ref, stress_ref):
    total = jnp.sum(own_ref[...] + other_ref[...], axis=1, keepdims=True)
    for sweep in range(ITERS):
        stress_ref[sweep] = jnp.sum(total[sweep : sweep + 1] / total[ITERS : ITERS + 1])


def small_body(dissim, classes, coords):
    coord_dims, _, per_dev = coords.shape
    points = dissim.shape[2]
    devices = points // per_dev
    held = devices // 2
    rows = held * per_dev
    offsets = [0, *sorted(range(2, held, 2), key=lambda i: (i & (i - 1) != 0, -i))]
    vmem = pl.BlockSpec(memory_space=pltpu.VMEM)
    hbm = pl.BlockSpec(memory_space=pltpu.HBM)
    f32 = functools.partial(jax.ShapeDtypeStruct, dtype=jnp.float32)

    def call(kernel, name, outs, *args, spec=vmem, grant=16, out_spec=vmem, scratch=()):
        return pl.pallas_call(
            kernel,
            out_shape=outs,
            in_specs=[spec] * len(args),
            out_specs=jax.tree.map(lambda _: out_spec, outs),
            scratch_shapes=scratch,
            compiler_params=pltpu.CompilerParams(vmem_limit_bytes=grant << 20),
            cost_estimate=pl.CostEstimate(
                flops=rows * points, bytes_accessed=4 * rows * points, transcendentals=rows * points
            ),
            name=name,
        )(*args)

    def swap(value, offset):
        return lax.ppermute(value, "wide", [(i, i ^ offset) for i in range(devices)])

    tiles = 2 * len(tile_spots(per_dev, points)) + 1
    packed = call(
        pack_kernel,
        "pack",
        f32((tiles, SUBLANES, LANES)),
        dissim[0],
        classes[0],
        coords[:, 0, :],
        spec=hbm,
        grant=60,
        scratch=[
            pltpu.VMEM((per_dev, points), jnp.float32),
            pltpu.VMEM((per_dev, points), jnp.int32),
            pltpu.VMEM((coord_dims, per_dev), jnp.float32),
            pltpu.SemaphoreType.DMA((3,)),
        ],
    )
    mine = jnp.concatenate([packed, *(swap(packed, offset) for offset in offsets[1:])], axis=0)
    theirs = swap(mine, 1)
    own = call(
        functools.partial(coords_kernel, offsets, per_dev),
        "half_coords",
        f32((coord_dims, rows)),
        mine,
        theirs,
        scratch=[pltpu.VMEM((held, SUBLANES, LANES), jnp.float32)],
    )
    other = swap(own, held)
    dis, weight, scale, denom = call(
        functools.partial(rows_kernel, offsets, per_dev),
        "half_rows",
        (f32((rows, points)), f32((rows, points)), f32((1, rows)), f32((1, LANES))),
        mine,
        theirs,
    )
    sums = []
    for _ in range(ITERS - 1):
        own, distance = call(
            sweep_kernel,
            "sweep",
            (f32((coord_dims, rows)), f32((rows, points))),
            dis,
            weight,
            scale,
            own,
            other,
        )
        other = swap(own, held)
        sums.append(call(stress_kernel, "stress_sum", f32((1, LANES)), dis, weight, distance))
    sums, inverse = call(
        last_kernel,
        "last_stress",
        (f32((SUBLANES, LANES)), f32((rows, points))),
        dis,
        weight,
        own,
        other,
        *sums,
        denom,
    )
    other_sums = swap(sums, held)
    final = call(
        functools.partial(final_kernel, per_dev),
        "final",
        f32((coord_dims, per_dev)),
        dis,
        weight,
        inverse,
        scale,
        own,
        other,
    )
    stress = call(
        total_kernel,
        "total",
        f32((ITERS,)),
        sums,
        other_sums,
        out_spec=pl.BlockSpec(memory_space=pltpu.SMEM),
    )
    return (final[:, None, :], stress)


def distributed_body(dissim, classes, coords):
    halves = dissim.shape[0]
    per_dev = dissim.shape[1]
    columns = dissim.shape[2]
    coord_dims = coords.shape[0]
    row_count = halves * per_dev
    dis_tile = dissim.reshape(row_count, columns)
    weight = class_weight(classes.reshape(row_count, columns))
    denom_local = jnp.sum(weight * dis_tile * dis_tile)
    half_index = lax.axis_index("narrow")
    denom_total = lax.psum(denom_local, ("wide", "narrow"))
    positions = coords
    numbers = []
    for sweep in range(ITERS):
        row_points = lax.all_gather(positions, "narrow", axis=1, tiled=True)
        row_x = row_points.reshape(coord_dims, row_count)
        row_sq = jnp.sum(row_x * row_x, axis=0)
        fold_column_x = lax.dynamic_index_in_dim(
            lax.all_gather(row_points, "wide", axis=2, tiled=True), half_index, 1, keepdims=False
        )
        inner_prod = lax.dot_general(
            row_x,
            fold_column_x,
            (((0,), (0,)), ((), ())),
            precision=lax.Precision.HIGHEST,
            preferred_element_type=jnp.float32,
        )
        col_sq = jnp.sum(fold_column_x * fold_column_x, axis=0)
        distance = jnp.sqrt(row_sq[:, None] + col_sq[None, :] - 2.0 * inner_prod + 1.0)
        ratios = weight * dis_tile / distance
        pull_term = lax.dot_general(
            weight - ratios,
            fold_column_x,
            (((1,), (1,)), ((), ())),
            precision=lax.Precision.HIGHEST,
            preferred_element_type=jnp.float32,
        )
        misfit = dis_tile - distance
        pull_sums = pull_term.reshape(halves, per_dev, coord_dims).transpose(0, 2, 1)
        weight_sum, ratio_sum, pull_share = (
            lax.psum_scatter(
                jnp.sum(weight, axis=1).reshape(halves, per_dev),
                "narrow",
                scatter_dimension=0,
                tiled=True,
            ),
            lax.psum_scatter(
                jnp.sum(ratios, axis=1).reshape(halves, per_dev),
                "narrow",
                scatter_dimension=0,
                tiled=True,
            ),
            lax.psum_scatter(pull_sums, "narrow", scatter_dimension=0, tiled=True),
        )
        own_coords = positions[:, 0, :]
        updated = (own_coords * (1.0 + ratio_sum[0]) + pull_share[0]) / (1.0 + weight_sum[0])
        positions = updated[:, None, :]
        numbers.append(
            lax.psum(jnp.sum(weight * misfit * misfit), ("wide", "narrow")) / denom_total
        )
    stress = jnp.stack(numbers)
    return (positions, stress)


def solution(mesh):
    def body(dissim, classes, coords):
        coord_dims, halves, per_dev = coords.shape
        points, devices = dissim.shape[2], mesh.shape["wide"]
        small = halves == 1 and mesh.shape["narrow"] == 1 and points * points <= MOST_PAIRS
        small = small and coord_dims == 2 * SUBLANES and 2 * per_dev <= LANES
        small = small and per_dev % SUBLANES == 0 and points % LANES == 0
        small = small and devices >= 4 and devices & (devices - 1) == 0
        return (small_body if small else distributed_body)(dissim, classes, coords)

    return jax.shard_map(
        body,
        mesh=mesh,
        in_specs=(
            P(None, ("grp", "wide"), "narrow"),
            P(None, ("grp", "wide"), "narrow"),
            P(None, "narrow", ("grp", "wide")),
        ),
        out_specs=(P(None, "narrow", ("grp", "wide")), P("grp")),
        check_vma=False,
    )
```

```python
import functools

import jax
import jax.numpy as jnp
from jax import lax
from jax.experimental import pallas as pl
from jax.experimental.pallas import tpu as pltpu
from jax.sharding import PartitionSpec as P

ITERS = 3
LANES = 128
MOST_PAIRS = 1 << 19


def class_weight(class_codes):
    return jnp.where(
        class_codes == 3,
        1.0,
        jnp.where(class_codes == 2, 0.5, jnp.where(class_codes == 1, 0.25, 0.0)),
    ).astype(jnp.float32)


def split_bf16(value, terms):
    parts = []
    for _ in range(terms):
        part = value.astype(jnp.bfloat16)
        parts.append(part)
        value = value - part.astype(jnp.float32)
    return parts


SUBLANES = 8
NT = (((1,), (1,)), ((), ()))
TN = (((0,), (0,)), ((), ()))
dot = functools.partial(lax.dot_general, preferred_element_type=jnp.float32)


def lane_sums(value):
    rows = jnp.sum(value, axis=0, keepdims=True)
    return sum(rows[:, i : i + LANES] for i in range(0, rows.shape[1], LANES))


def tile_spots(per_dev, points):
    return [
        (slice(row, row + SUBLANES), slice(column, column + LANES))
        for row in range(0, per_dev, SUBLANES)
        for column in range(0, points, LANES)
    ]


def pack_kernel(dis_hbm, cls_hbm, x_hbm, out_ref, dis_ref, cls_ref, x_ref, sems):
    copies = [
        pltpu.make_async_copy(src, dst, sems.at[i])
        for i, (src, dst) in enumerate(
            [(dis_hbm, dis_ref), (cls_hbm, cls_ref), (x_hbm, x_ref)]
        )
    ]
    for copy in copies:
        copy.start()
    for copy in copies:
        copy.wait()
    spots = tile_spots(*dis_ref.shape)
    for i, spot in enumerate(spots):
        out_ref[i] = dis_ref[spot]
        out_ref[len(spots) + i] = class_weight(cls_ref[spot])
    half, per_dev = x_ref.shape[0] // 2, x_ref.shape[1]
    pad = jnp.zeros((half, LANES - 2 * per_dev), jnp.float32)
    out_ref[2 * len(spots)] = jnp.concatenate([x_ref[:half], x_ref[half:], pad], axis=1)


def held_slots(offsets, refs, tiles):
    me = lax.axis_index("wide")
    for bit, ref in enumerate(refs):
        for slot, offset in enumerate(offsets):
            yield ref, slot * tiles, me ^ offset ^ bit


def side_norm(top, bottom, coord_dims):
    pad = jnp.zeros((coord_dims - 6, top[0].shape[1]), jnp.float32)
    rows = [p.astype(jnp.float32) for p in (*top, *bottom)]
    return jnp.concatenate([*rows, pad], axis=0).astype(jnp.bfloat16)


def squares(own, x):
    coord_dims = x.shape[0]
    own_hi, own_mid, own_lo = (-2.0 * p for p in split_bf16(own, 3))
    hi, mid, lo = split_bf16(x, 3)
    own_norm = split_bf16(jnp.sum(own * own, axis=0, keepdims=True), 3)
    norm = split_bf16(jnp.sum(x * x, axis=0, keepdims=True) + 1.0, 3)
    left_ones = [jnp.ones((3, own.shape[1]), jnp.bfloat16)]
    right_ones = [jnp.ones((3, x.shape[1]), jnp.bfloat16)]
    left = [own_hi, own_hi, own_hi, own_mid, own_mid, own_lo]
    right = [hi, mid, lo, hi, mid, hi]
    left = jnp.concatenate([*left, side_norm(own_norm, left_ones, coord_dims)], axis=0)
    right = jnp.concatenate([*right, side_norm(right_ones, norm, coord_dims)], axis=0)
    return dot(left, right, TN), hi, mid


def moved(own, hi, mid, pull, scale):
    coord_dims, count = own.shape
    ones = jnp.ones((coord_dims, hi.shape[1]), jnp.bfloat16)
    sides = jnp.concatenate([hi, mid, ones], axis=0)
    sums = dot(jnp.concatenate(split_bf16(pull, 2), axis=0), sides, NT)
    sums = (sums[:count] + sums[count:]).T
    pulled = sums[:coord_dims] + sums[coord_dims : 2 * coord_dims]
    return own + (pulled - own * sums[2 * coord_dims : 2 * coord_dims + 1]) * scale


def group_kernel(offsets, per_dev, mine_ref, theirs_ref, out_ref, stress_ref,
                 dis_ref, weight_ref, tile_ref, inverse_ref):
    points = dis_ref.shape[0]
    spots = tile_spots(per_dev, points)
    tiles = 2 * len(spots) + 1
    for ref, base, place in held_slots(offsets, (mine_ref, theirs_ref), tiles):
        tile_ref[place] = ref[base + tiles - 1]
        for i, (rows, columns) in enumerate(spots):
            start = pl.multiple_of(place * per_dev + rows.start, SUBLANES)
            dis_ref[pl.ds(start, SUBLANES), columns] = ref[base + i]
            weight_ref[pl.ds(start, SUBLANES), columns] = ref[base + len(spots) + i]
    blocks = [tile_ref[i] for i in range(tile_ref.shape[0])]
    halves = [
        jnp.concatenate([t[:, low : low + per_dev] for t in blocks], axis=1)
        for low in (0, per_dev)
    ]
    x = jnp.concatenate(halves, axis=0)
    weight = weight_ref[...]
    ones = jnp.ones((x.shape[0], points), jnp.bfloat16)
    scale = 1.0 / (1.0 + dot(weight.astype(jnp.bfloat16), ones, NT).T[0:1])
    sums = [lane_sums(weight * dis_ref[...] * dis_ref[...])]
    for sweep in range(ITERS):
        square, hi, mid = squares(x, x)
        inverse = lax.rsqrt(square)
        misfit = dis_ref[...] - square * inverse
        weight = weight_ref[...]
        sums.append(lane_sums(weight * misfit * misfit))
        if sweep < ITERS - 1:
            x = moved(x, hi, mid, weight - weight * dis_ref[...] * inverse, scale)
    inverse_ref[...] = inverse
    place = lax.axis_index("wide")
    rows = pl.ds(pl.multiple_of(place * per_dev, SUBLANES), per_dev)
    scaled = jnp.concatenate([x, jnp.broadcast_to(scale, (SUBLANES, points))], axis=0)
    mine = jnp.zeros((scaled.shape[0], per_dev), jnp.float32)
    for i in range(points // per_dev):
        mine = jnp.where(place == i, scaled[:, i * per_dev : (i + 1) * per_dev], mine)
    own, scale = mine[: x.shape[0]], mine[x.shape[0] : x.shape[0] + 1]
    weight = weight_ref[rows, :]
    pull = weight - weight * dis_ref[rows, :] * inverse_ref[rows, :]
    out_ref[...] = moved(own, hi, mid, pull, scale)
    total = jnp.sum(jnp.concatenate(sums, axis=0), axis=1, keepdims=True)
    for sweep in range(ITERS):
        stress_ref[sweep] = jnp.sum(total[sweep + 1 : sweep + 2] / total[0:1])


def small_body(dissim, classes, coords):
    coord_dims, _, per_dev = coords.shape
    points = dissim.shape[2]
    devices = points // per_dev
    vmem = pl.BlockSpec(memory_space=pltpu.VMEM)
    hbm = pl.BlockSpec(memory_space=pltpu.HBM)
    f32 = functools.partial(jax.ShapeDtypeStruct, dtype=jnp.float32)
    params = pltpu.CompilerParams(vmem_limit_bytes=16 << 20)

    def swap(value, offset):
        return lax.ppermute(value, "wide", [(i, i ^ offset) for i in range(devices)])

    tiles = 2 * len(tile_spots(per_dev, points)) + 1
    inputs = (dissim[0], classes[0], coords[:, 0, :])
    packed = pl.pallas_call(
        pack_kernel,
        out_shape=f32((tiles, SUBLANES, LANES)),
        in_specs=[hbm] * 3,
        out_specs=vmem,
        scratch_shapes=[
            pltpu.VMEM((per_dev, points), jnp.float32),
            pltpu.VMEM((per_dev, points), jnp.int32),
            pltpu.VMEM((coord_dims, per_dev), jnp.float32),
            pltpu.SemaphoreType.DMA((3,)),
        ],
        compiler_params=params,
        name="pack",
    )(*(pltpu.with_memory_space_constraint(array, pltpu.HBM) for array in inputs))
    top, relay = devices // 2, 2
    near, far = range(2, top, 2), range(top + relay + 2, devices, 2)
    direct = [top, *reversed(far), *reversed(near)]
    held = {0: packed, **{offset: swap(packed, offset) for offset in direct}}
    held[top + relay] = swap(held[top], relay)
    offsets = list(held)
    mine = jnp.concatenate(list(held.values()), axis=0)
    theirs = swap(mine, 1)
    final, stress = pl.pallas_call(
        functools.partial(group_kernel, offsets, per_dev),
        out_shape=(f32((coord_dims, per_dev)), f32((ITERS,))),
        in_specs=[vmem, vmem],
        out_specs=(vmem, pl.BlockSpec(memory_space=pltpu.SMEM)),
        scratch_shapes=[
            pltpu.VMEM((points, points), jnp.float32),
            pltpu.VMEM((points, points), jnp.float32),
            pltpu.VMEM((devices, SUBLANES, LANES), jnp.float32),
            pltpu.VMEM((points, points), jnp.float32),
        ],
        compiler_params=params,
        name="group_smacof",
    )(mine, theirs)
    return (final[:, None, :], stress)


def distributed_body(dissim, classes, coords):
    halves = dissim.shape[0]
    per_dev = dissim.shape[1]
    columns = dissim.shape[2]
    coord_dims = coords.shape[0]
    row_count = halves * per_dev
    dis_tile = dissim.reshape(row_count, columns)
    weight = class_weight(classes.reshape(row_count, columns))
    denom_local = jnp.sum(weight * dis_tile * dis_tile)
    half_index = lax.axis_index("narrow")
    denom_total = lax.psum(denom_local, ("wide", "narrow"))
    positions = coords
    numbers = []
    for sweep in range(ITERS):
        row_points = lax.all_gather(positions, "narrow", axis=1, tiled=True)
        row_x = row_points.reshape(coord_dims, row_count)
        row_sq = jnp.sum(row_x * row_x, axis=0)
        fold_column_x = lax.dynamic_index_in_dim(
            lax.all_gather(row_points, "wide", axis=2, tiled=True), half_index, 1, keepdims=False
        )
        inner_prod = lax.dot_general(
            row_x,
            fold_column_x,
            (((0,), (0,)), ((), ())),
            precision=lax.Precision.HIGHEST,
            preferred_element_type=jnp.float32,
        )
        col_sq = jnp.sum(fold_column_x * fold_column_x, axis=0)
        distance = jnp.sqrt(row_sq[:, None] + col_sq[None, :] - 2.0 * inner_prod + 1.0)
        ratios = weight * dis_tile / distance
        pull_term = lax.dot_general(
            weight - ratios,
            fold_column_x,
            (((1,), (1,)), ((), ())),
            precision=lax.Precision.HIGHEST,
            preferred_element_type=jnp.float32,
        )
        misfit = dis_tile - distance
        pull_sums = pull_term.reshape(halves, per_dev, coord_dims).transpose(0, 2, 1)
        weight_sum, ratio_sum, pull_share = (
            lax.psum_scatter(
                jnp.sum(weight, axis=1).reshape(halves, per_dev),
                "narrow",
                scatter_dimension=0,
                tiled=True,
            ),
            lax.psum_scatter(
                jnp.sum(ratios, axis=1).reshape(halves, per_dev),
                "narrow",
                scatter_dimension=0,
                tiled=True,
            ),
            lax.psum_scatter(pull_sums, "narrow", scatter_dimension=0, tiled=True),
        )
        own_coords = positions[:, 0, :]
        updated = (own_coords * (1.0 + ratio_sum[0]) + pull_share[0]) / (1.0 + weight_sum[0])
        positions = updated[:, None, :]
        numbers.append(
            lax.psum(jnp.sum(weight * misfit * misfit), ("wide", "narrow")) / denom_total
        )
    stress = jnp.stack(numbers)
    return (positions, stress)


def solution(mesh):
    def body(dissim, classes, coords):
        coord_dims, halves, per_dev = coords.shape
        points, devices = dissim.shape[2], mesh.shape["wide"]
        small = halves == 1 and mesh.shape["narrow"] == 1 and points * points <= MOST_PAIRS
        small = small and coord_dims == 2 * SUBLANES and 2 * per_dev <= LANES
        small = small and per_dev % SUBLANES == 0 and points % LANES == 0
        small = small and devices >= 8 and devices & (devices - 1) == 0
        return (small_body if small else distributed_body)(dissim, classes, coords)

    return jax.shard_map(
        body,
        mesh=mesh,
        in_specs=(
            P(None, ("grp", "wide"), "narrow"),
            P(None, ("grp", "wide"), "narrow"),
            P(None, "narrow", ("grp", "wide")),
        ),
        out_specs=(P(None, "narrow", ("grp", "wide")), P("grp")),
        check_vma=False,
    )
```

```python
import functools

import jax
import jax.numpy as jnp
from jax import lax
from jax.experimental import pallas as pl
from jax.experimental.pallas import tpu as pltpu
from jax.sharding import PartitionSpec as P

ITERS = 3
LANES = 128
MOST_PAIRS = 1 << 19


def class_weight(class_codes):
    return jnp.where(
        class_codes == 3,
        1.0,
        jnp.where(class_codes == 2, 0.5, jnp.where(class_codes == 1, 0.25, 0.0)),
    ).astype(jnp.float32)


def split_bf16(value, terms):
    parts = []
    for _ in range(terms):
        part = value.astype(jnp.bfloat16)
        parts.append(part)
        value = value - part.astype(jnp.float32)
    return parts


SUBLANES = 8
NT = (((1,), (1,)), ((), ()))
TN = (((0,), (0,)), ((), ()))
dot = functools.partial(lax.dot_general, preferred_element_type=jnp.float32)


def lane_sums(value):
    rows = jnp.sum(value, axis=0, keepdims=True)
    return sum(rows[:, i : i + LANES] for i in range(0, rows.shape[1], LANES))


def tile_spots(per_dev, points):
    return [
        (slice(row, row + SUBLANES), slice(column, column + LANES))
        for row in range(0, per_dev, SUBLANES)
        for column in range(0, points, LANES)
    ]


def pack_kernel(dis_hbm, cls_hbm, x_hbm, out_ref, dis_ref, cls_ref, x_ref, sems):
    copies = [
        pltpu.make_async_copy(src, dst, sems.at[i])
        for i, (src, dst) in enumerate(
            [(dis_hbm, dis_ref), (cls_hbm, cls_ref), (x_hbm, x_ref)]
        )
    ]
    for copy in copies:
        copy.start()
    for copy in copies:
        copy.wait()
    spots = tile_spots(*dis_ref.shape)
    for i, spot in enumerate(spots):
        out_ref[i] = dis_ref[spot]
        out_ref[len(spots) + i] = class_weight(cls_ref[spot])
    half, per_dev = x_ref.shape[0] // 2, x_ref.shape[1]
    pad = jnp.zeros((half, LANES - 2 * per_dev), jnp.float32)
    out_ref[2 * len(spots)] = jnp.concatenate([x_ref[:half], x_ref[half:], pad], axis=1)


def held_slots(refs, tiles):
    core = lax.rem(lax.axis_index("wide"), 2)
    for bit, ref in enumerate(refs):
        for slot in range(ref.shape[0] // tiles):
            yield ref, slot * tiles, 2 * slot + (core ^ bit)


def side_norm(top, bottom, coord_dims):
    pad = jnp.zeros((coord_dims - 6, top[0].shape[1]), jnp.float32)
    rows = [p.astype(jnp.float32) for p in (*top, *bottom)]
    return jnp.concatenate([*rows, pad], axis=0).astype(jnp.bfloat16)


def squares(own, x):
    coord_dims = x.shape[0]
    own_hi, own_mid, own_lo = (-2.0 * p for p in split_bf16(own, 3))
    hi, mid, lo = split_bf16(x, 3)
    own_norm = split_bf16(jnp.sum(own * own, axis=0, keepdims=True), 3)
    norm = split_bf16(jnp.sum(x * x, axis=0, keepdims=True) + 1.0, 3)
    left_ones = [jnp.ones((3, own.shape[1]), jnp.bfloat16)]
    right_ones = [jnp.ones((3, x.shape[1]), jnp.bfloat16)]
    left = [own_hi, own_hi, own_hi, own_mid, own_mid, own_lo]
    right = [hi, mid, lo, hi, mid, hi]
    left = jnp.concatenate([*left, side_norm(own_norm, left_ones, coord_dims)], axis=0)
    right = jnp.concatenate([*right, side_norm(right_ones, norm, coord_dims)], axis=0)
    return dot(left, right, TN), hi, mid


def moved(own, hi, mid, pull, scale):
    coord_dims, count = own.shape
    ones = jnp.ones((coord_dims, hi.shape[1]), jnp.bfloat16)
    sides = jnp.concatenate([hi, mid, ones], axis=0)
    sums = dot(jnp.concatenate(split_bf16(pull, 2), axis=0), sides, NT)
    sums = (sums[:count] + sums[count:]).T
    pulled = sums[:coord_dims] + sums[coord_dims : 2 * coord_dims]
    return own + (pulled - own * sums[2 * coord_dims : 2 * coord_dims + 1]) * scale


def group_kernel(per_dev, mine_ref, theirs_ref, out_ref, stress_ref,
                 dis_ref, weight_ref, tile_ref, inverse_ref):
    points = dis_ref.shape[0]
    spots = tile_spots(per_dev, points)
    tiles = 2 * len(spots) + 1
    for ref, base, place in held_slots((mine_ref, theirs_ref), tiles):
        tile_ref[place] = ref[base + tiles - 1]
        for i, (rows, columns) in enumerate(spots):
            start = pl.multiple_of(place * per_dev + rows.start, SUBLANES)
            dis_ref[pl.ds(start, SUBLANES), columns] = ref[base + i]
            weight_ref[pl.ds(start, SUBLANES), columns] = ref[base + len(spots) + i]
    blocks = [tile_ref[i] for i in range(tile_ref.shape[0])]
    halves = [
        jnp.concatenate([t[:, low : low + per_dev] for t in blocks], axis=1)
        for low in (0, per_dev)
    ]
    x = jnp.concatenate(halves, axis=0)
    weight = weight_ref[...]
    ones = jnp.ones((x.shape[0], points), jnp.bfloat16)
    scale = 1.0 / (1.0 + dot(weight.astype(jnp.bfloat16), ones, NT).T[0:1])
    sums = [lane_sums(weight * dis_ref[...] * dis_ref[...])]
    for sweep in range(ITERS):
        square, hi, mid = squares(x, x)
        inverse = lax.rsqrt(square)
        misfit = dis_ref[...] - square * inverse
        weight = weight_ref[...]
        sums.append(lane_sums(weight * misfit * misfit))
        if sweep < ITERS - 1:
            x = moved(x, hi, mid, weight - weight * dis_ref[...] * inverse, scale)
    inverse_ref[...] = inverse
    place = lax.axis_index("wide")
    rows = pl.ds(pl.multiple_of(place * per_dev, SUBLANES), per_dev)
    scaled = jnp.concatenate([x, jnp.broadcast_to(scale, (SUBLANES, points))], axis=0)
    mine = jnp.zeros((scaled.shape[0], per_dev), jnp.float32)
    for i in range(points // per_dev):
        mine = jnp.where(place == i, scaled[:, i * per_dev : (i + 1) * per_dev], mine)
    own, scale = mine[: x.shape[0]], mine[x.shape[0] : x.shape[0] + 1]
    weight = weight_ref[rows, :]
    pull = weight - weight * dis_ref[rows, :] * inverse_ref[rows, :]
    out_ref[...] = moved(own, hi, mid, pull, scale)
    total = jnp.sum(jnp.concatenate(sums, axis=0), axis=1, keepdims=True)
    for sweep in range(ITERS):
        stress_ref[sweep] = jnp.sum(total[sweep + 1 : sweep + 2] / total[0:1])


def small_body(dissim, classes, coords):
    coord_dims, _, per_dev = coords.shape
    points = dissim.shape[2]
    devices = points // per_dev
    vmem = pl.BlockSpec(memory_space=pltpu.VMEM)
    hbm = pl.BlockSpec(memory_space=pltpu.HBM)
    f32 = functools.partial(jax.ShapeDtypeStruct, dtype=jnp.float32)
    params = pltpu.CompilerParams(vmem_limit_bytes=16 << 20)

    def swap(value, offset):
        return lax.ppermute(value, "wide", [(i, i ^ offset) for i in range(devices)])

    tiles = 2 * len(tile_spots(per_dev, points)) + 1
    inputs = (dissim[0], classes[0], coords[:, 0, :])
    packed = pl.pallas_call(
        pack_kernel,
        out_shape=f32((tiles, SUBLANES, LANES)),
        in_specs=[hbm] * 3,
        out_specs=vmem,
        scratch_shapes=[
            pltpu.VMEM((per_dev, points), jnp.float32),
            pltpu.VMEM((per_dev, points), jnp.int32),
            pltpu.VMEM((coord_dims, per_dev), jnp.float32),
            pltpu.SemaphoreType.DMA((3,)),
        ],
        compiler_params=params,
        name="pack",
    )(*(pltpu.with_memory_space_constraint(array, pltpu.HBM) for array in inputs))
    same_core = [list(range(core, devices, 2)) for core in range(2)]
    mine = lax.all_gather(packed, "wide", axis=0, tiled=True, axis_index_groups=same_core)
    theirs = swap(mine, 1)
    final, stress = pl.pallas_call(
        functools.partial(group_kernel, per_dev),
        out_shape=(f32((coord_dims, per_dev)), f32((ITERS,))),
        in_specs=[vmem, vmem],
        out_specs=(vmem, pl.BlockSpec(memory_space=pltpu.SMEM)),
        scratch_shapes=[
            pltpu.VMEM((points, points), jnp.float32),
            pltpu.VMEM((points, points), jnp.float32),
            pltpu.VMEM((devices, SUBLANES, LANES), jnp.float32),
            pltpu.VMEM((points, points), jnp.float32),
        ],
        compiler_params=params,
        name="group_smacof",
    )(mine, theirs)
    return (final[:, None, :], stress)


def distributed_body(dissim, classes, coords):
    halves = dissim.shape[0]
    per_dev = dissim.shape[1]
    columns = dissim.shape[2]
    coord_dims = coords.shape[0]
    row_count = halves * per_dev
    dis_tile = dissim.reshape(row_count, columns)
    weight = class_weight(classes.reshape(row_count, columns))
    denom_local = jnp.sum(weight * dis_tile * dis_tile)
    half_index = lax.axis_index("narrow")
    denom_total = lax.psum(denom_local, ("wide", "narrow"))
    positions = coords
    numbers = []
    for sweep in range(ITERS):
        row_points = lax.all_gather(positions, "narrow", axis=1, tiled=True)
        row_x = row_points.reshape(coord_dims, row_count)
        row_sq = jnp.sum(row_x * row_x, axis=0)
        fold_column_x = lax.dynamic_index_in_dim(
            lax.all_gather(row_points, "wide", axis=2, tiled=True), half_index, 1, keepdims=False
        )
        inner_prod = lax.dot_general(
            row_x,
            fold_column_x,
            (((0,), (0,)), ((), ())),
            precision=lax.Precision.HIGHEST,
            preferred_element_type=jnp.float32,
        )
        col_sq = jnp.sum(fold_column_x * fold_column_x, axis=0)
        distance = jnp.sqrt(row_sq[:, None] + col_sq[None, :] - 2.0 * inner_prod + 1.0)
        ratios = weight * dis_tile / distance
        pull_term = lax.dot_general(
            weight - ratios,
            fold_column_x,
            (((1,), (1,)), ((), ())),
            precision=lax.Precision.HIGHEST,
            preferred_element_type=jnp.float32,
        )
        misfit = dis_tile - distance
        pull_sums = pull_term.reshape(halves, per_dev, coord_dims).transpose(0, 2, 1)
        weight_sum, ratio_sum, pull_share = (
            lax.psum_scatter(
                jnp.sum(weight, axis=1).reshape(halves, per_dev),
                "narrow",
                scatter_dimension=0,
                tiled=True,
            ),
            lax.psum_scatter(
                jnp.sum(ratios, axis=1).reshape(halves, per_dev),
                "narrow",
                scatter_dimension=0,
                tiled=True,
            ),
            lax.psum_scatter(pull_sums, "narrow", scatter_dimension=0, tiled=True),
        )
        own_coords = positions[:, 0, :]
        updated = (own_coords * (1.0 + ratio_sum[0]) + pull_share[0]) / (1.0 + weight_sum[0])
        positions = updated[:, None, :]
        numbers.append(
            lax.psum(jnp.sum(weight * misfit * misfit), ("wide", "narrow")) / denom_total
        )
    stress = jnp.stack(numbers)
    return (positions, stress)


def solution(mesh):
    def body(dissim, classes, coords):
        coord_dims, halves, per_dev = coords.shape
        points, devices = dissim.shape[2], mesh.shape["wide"]
        small = halves == 1 and mesh.shape["narrow"] == 1 and points * points <= MOST_PAIRS
        small = small and coord_dims == 2 * SUBLANES and 2 * per_dev <= LANES
        small = small and per_dev % SUBLANES == 0 and points % LANES == 0
        small = small and devices >= 8 and devices & (devices - 1) == 0
        return (small_body if small else distributed_body)(dissim, classes, coords)

    return jax.shard_map(
        body,
        mesh=mesh,
        in_specs=(
            P(None, ("grp", "wide"), "narrow"),
            P(None, ("grp", "wide"), "narrow"),
            P(None, "narrow", ("grp", "wide")),
        ),
        out_specs=(P(None, "narrow", ("grp", "wide")), P("grp")),
        check_vma=False,
    )
```

```python
import functools

import jax
import jax.numpy as jnp
from jax import lax
from jax.experimental import pallas as pl
from jax.experimental.pallas import tpu as pltpu
from jax.sharding import PartitionSpec as P

ITERS = 3
LANES = 128
MOST_PAIRS = 1 << 19


def class_weight(class_codes):
    return jnp.where(
        class_codes == 3,
        1.0,
        jnp.where(class_codes == 2, 0.5, jnp.where(class_codes == 1, 0.25, 0.0)),
    ).astype(jnp.float32)


def split_bf16(value, terms):
    parts = []
    for _ in range(terms):
        part = value.astype(jnp.bfloat16)
        parts.append(part)
        value = value - part.astype(jnp.float32)
    return parts


SUBLANES = 8
NT = (((1,), (1,)), ((), ()))
TN = (((0,), (0,)), ((), ()))
dot = functools.partial(lax.dot_general, preferred_element_type=jnp.float32)


def lane_sums(value):
    rows = jnp.sum(value, axis=0, keepdims=True)
    return sum(rows[:, i : i + LANES] for i in range(0, rows.shape[1], LANES))


def tile_spots(per_dev, points):
    return [
        (slice(row, row + SUBLANES), slice(column, column + LANES))
        for row in range(0, per_dev, SUBLANES)
        for column in range(0, points, LANES)
    ]


def pack_kernel(dis_hbm, cls_hbm, x_hbm, out_ref, dis_ref, cls_ref, x_ref, sems):
    copies = [
        pltpu.make_async_copy(src, dst, sems.at[i])
        for i, (src, dst) in enumerate(
            [(dis_hbm, dis_ref), (cls_hbm, cls_ref), (x_hbm, x_ref)]
        )
    ]
    for copy in copies:
        copy.start()
    for copy in copies:
        copy.wait()
    spots = tile_spots(*dis_ref.shape)
    for i, spot in enumerate(spots):
        out_ref[i] = dis_ref[spot]
        out_ref[len(spots) + i] = class_weight(cls_ref[spot])
    half, per_dev = x_ref.shape[0] // 2, x_ref.shape[1]
    pad = jnp.zeros((half, LANES - 2 * per_dev), jnp.float32)
    out_ref[2 * len(spots)] = jnp.concatenate([x_ref[:half], x_ref[half:], pad], axis=1)


def held_slots(offsets, refs, tiles):
    me = lax.axis_index("wide")
    for bit, ref in enumerate(refs):
        for slot, offset in enumerate(offsets):
            yield ref, slot * tiles, me ^ offset ^ bit


def side_norm(top, bottom, coord_dims):
    pad = jnp.zeros((coord_dims - 6, top[0].shape[1]), jnp.float32)
    rows = [p.astype(jnp.float32) for p in (*top, *bottom)]
    return jnp.concatenate([*rows, pad], axis=0).astype(jnp.bfloat16)


def squares(own, x):
    coord_dims = x.shape[0]
    own_hi, own_mid, own_lo = (-2.0 * p for p in split_bf16(own, 3))
    hi, mid, lo = split_bf16(x, 3)
    own_norm = split_bf16(jnp.sum(own * own, axis=0, keepdims=True), 3)
    norm = split_bf16(jnp.sum(x * x, axis=0, keepdims=True) + 1.0, 3)
    left_ones = [jnp.ones((3, own.shape[1]), jnp.bfloat16)]
    right_ones = [jnp.ones((3, x.shape[1]), jnp.bfloat16)]
    left = [own_hi, own_hi, own_hi, own_mid, own_mid, own_lo]
    right = [hi, mid, lo, hi, mid, hi]
    left = jnp.concatenate([*left, side_norm(own_norm, left_ones, coord_dims)], axis=0)
    right = jnp.concatenate([*right, side_norm(right_ones, norm, coord_dims)], axis=0)
    return dot(left, right, TN), hi, mid


def moved(own, hi, mid, pull, scale):
    coord_dims, count = own.shape
    ones = jnp.ones((coord_dims, hi.shape[1]), jnp.bfloat16)
    sides = jnp.concatenate([hi, mid, ones], axis=0)
    sums = dot(jnp.concatenate(split_bf16(pull, 2), axis=0), sides, NT)
    sums = (sums[:count] + sums[count:]).T
    pulled = sums[:coord_dims] + sums[coord_dims : 2 * coord_dims]
    return own + (pulled - own * sums[2 * coord_dims : 2 * coord_dims + 1]) * scale


def group_kernel(offsets, per_dev, mine_ref, theirs_ref, out_ref, stress_ref,
                 dis_ref, weight_ref, tile_ref, inverse_ref):
    points = dis_ref.shape[0]
    spots = tile_spots(per_dev, points)
    tiles = 2 * len(spots) + 1
    for ref, base, place in held_slots(offsets, (mine_ref, theirs_ref), tiles):
        tile_ref[place] = ref[base + tiles - 1]
        for i, (rows, columns) in enumerate(spots):
            start = pl.multiple_of(place * per_dev + rows.start, SUBLANES)
            dis_ref[pl.ds(start, SUBLANES), columns] = ref[base + i]
            weight_ref[pl.ds(start, SUBLANES), columns] = ref[base + len(spots) + i]
    blocks = [tile_ref[i] for i in range(tile_ref.shape[0])]
    halves = [
        jnp.concatenate([t[:, low : low + per_dev] for t in blocks], axis=1)
        for low in (0, per_dev)
    ]
    x = jnp.concatenate(halves, axis=0)
    weight = weight_ref[...]
    ones = jnp.ones((x.shape[0], points), jnp.bfloat16)
    scale = 1.0 / (1.0 + dot(weight.astype(jnp.bfloat16), ones, NT).T[0:1])
    sums = [lane_sums(weight * dis_ref[...] * dis_ref[...])]
    for sweep in range(ITERS):
        square, hi, mid = squares(x, x)
        inverse = lax.rsqrt(square)
        misfit = dis_ref[...] - square * inverse
        weight = weight_ref[...]
        sums.append(lane_sums(weight * misfit * misfit))
        if sweep < ITERS - 1:
            x = moved(x, hi, mid, weight - weight * dis_ref[...] * inverse, scale)
    inverse_ref[...] = inverse
    place = lax.axis_index("wide")
    rows = pl.ds(pl.multiple_of(place * per_dev, SUBLANES), per_dev)
    scaled = jnp.concatenate([x, jnp.broadcast_to(scale, (SUBLANES, points))], axis=0)
    mine = jnp.zeros((scaled.shape[0], per_dev), jnp.float32)
    for i in range(points // per_dev):
        mine = jnp.where(place == i, scaled[:, i * per_dev : (i + 1) * per_dev], mine)
    own, scale = mine[: x.shape[0]], mine[x.shape[0] : x.shape[0] + 1]
    weight = weight_ref[rows, :]
    pull = weight - weight * dis_ref[rows, :] * inverse_ref[rows, :]
    out_ref[...] = moved(own, hi, mid, pull, scale)
    total = jnp.sum(jnp.concatenate(sums, axis=0), axis=1, keepdims=True)
    for sweep in range(ITERS):
        stress_ref[sweep] = jnp.sum(total[sweep + 1 : sweep + 2] / total[0:1])


def small_body(dissim, classes, coords):
    coord_dims, _, per_dev = coords.shape
    points = dissim.shape[2]
    devices = points // per_dev
    vmem = pl.BlockSpec(memory_space=pltpu.VMEM)
    hbm = pl.BlockSpec(memory_space=pltpu.HBM)
    f32 = functools.partial(jax.ShapeDtypeStruct, dtype=jnp.float32)
    params = pltpu.CompilerParams(vmem_limit_bytes=16 << 20)

    def swap(value, offset):
        return lax.ppermute(value, "wide", [(i, i ^ offset) for i in range(devices)])

    tiles = 2 * len(tile_spots(per_dev, points)) + 1
    inputs = (dissim[0], classes[0], coords[:, 0, :])
    packed = pl.pallas_call(
        pack_kernel,
        out_shape=f32((tiles, SUBLANES, LANES)),
        in_specs=[hbm] * 3,
        out_specs=vmem,
        scratch_shapes=[
            pltpu.VMEM((per_dev, points), jnp.float32),
            pltpu.VMEM((per_dev, points), jnp.int32),
            pltpu.VMEM((coord_dims, per_dev), jnp.float32),
            pltpu.SemaphoreType.DMA((3,)),
        ],
        compiler_params=params,
        name="pack",
    )(*(pltpu.with_memory_space_constraint(array, pltpu.HBM) for array in inputs))
    far, near, side = devices // 2, devices // 4, devices // 8
    held = {0: packed}
    for offset in (far, near, far | near | side, far | near, side):
        held[offset] = swap(packed, offset)
    for offset in (near, far):
        held[offset | side] = swap(held[offset], side)
    offsets = list(held)
    mine = jnp.concatenate(list(held.values()), axis=0)
    theirs = swap(mine, 1)
    final, stress = pl.pallas_call(
        functools.partial(group_kernel, offsets, per_dev),
        out_shape=(f32((coord_dims, per_dev)), f32((ITERS,))),
        in_specs=[vmem, vmem],
        out_specs=(vmem, pl.BlockSpec(memory_space=pltpu.SMEM)),
        scratch_shapes=[
            pltpu.VMEM((points, points), jnp.float32),
            pltpu.VMEM((points, points), jnp.float32),
            pltpu.VMEM((devices, SUBLANES, LANES), jnp.float32),
            pltpu.VMEM((points, points), jnp.float32),
        ],
        compiler_params=params,
        name="group_smacof",
    )(mine, theirs)
    return (final[:, None, :], stress)


def distributed_body(dissim, classes, coords):
    halves = dissim.shape[0]
    per_dev = dissim.shape[1]
    columns = dissim.shape[2]
    coord_dims = coords.shape[0]
    row_count = halves * per_dev
    dis_tile = dissim.reshape(row_count, columns)
    weight = class_weight(classes.reshape(row_count, columns))
    denom_local = jnp.sum(weight * dis_tile * dis_tile)
    half_index = lax.axis_index("narrow")
    denom_total = lax.psum(denom_local, ("wide", "narrow"))
    positions = coords
    numbers = []
    for sweep in range(ITERS):
        row_points = lax.all_gather(positions, "narrow", axis=1, tiled=True)
        row_x = row_points.reshape(coord_dims, row_count)
        row_sq = jnp.sum(row_x * row_x, axis=0)
        fold_column_x = lax.dynamic_index_in_dim(
            lax.all_gather(row_points, "wide", axis=2, tiled=True), half_index, 1, keepdims=False
        )
        inner_prod = lax.dot_general(
            row_x,
            fold_column_x,
            (((0,), (0,)), ((), ())),
            precision=lax.Precision.HIGHEST,
            preferred_element_type=jnp.float32,
        )
        col_sq = jnp.sum(fold_column_x * fold_column_x, axis=0)
        distance = jnp.sqrt(row_sq[:, None] + col_sq[None, :] - 2.0 * inner_prod + 1.0)
        ratios = weight * dis_tile / distance
        pull_term = lax.dot_general(
            weight - ratios,
            fold_column_x,
            (((1,), (1,)), ((), ())),
            precision=lax.Precision.HIGHEST,
            preferred_element_type=jnp.float32,
        )
        misfit = dis_tile - distance
        pull_sums = pull_term.reshape(halves, per_dev, coord_dims).transpose(0, 2, 1)
        weight_sum, ratio_sum, pull_share = (
            lax.psum_scatter(
                jnp.sum(weight, axis=1).reshape(halves, per_dev),
                "narrow",
                scatter_dimension=0,
                tiled=True,
            ),
            lax.psum_scatter(
                jnp.sum(ratios, axis=1).reshape(halves, per_dev),
                "narrow",
                scatter_dimension=0,
                tiled=True,
            ),
            lax.psum_scatter(pull_sums, "narrow", scatter_dimension=0, tiled=True),
        )
        own_coords = positions[:, 0, :]
        updated = (own_coords * (1.0 + ratio_sum[0]) + pull_share[0]) / (1.0 + weight_sum[0])
        positions = updated[:, None, :]
        numbers.append(
            lax.psum(jnp.sum(weight * misfit * misfit), ("wide", "narrow")) / denom_total
        )
    stress = jnp.stack(numbers)
    return (positions, stress)


def solution(mesh):
    def body(dissim, classes, coords):
        coord_dims, halves, per_dev = coords.shape
        points, devices = dissim.shape[2], mesh.shape["wide"]
        small = halves == 1 and mesh.shape["narrow"] == 1 and points * points <= MOST_PAIRS
        small = small and coord_dims == 2 * SUBLANES and 2 * per_dev <= LANES
        small = small and per_dev % SUBLANES == 0 and points % LANES == 0
        small = small and devices == 16
        return (small_body if small else distributed_body)(dissim, classes, coords)

    return jax.shard_map(
        body,
        mesh=mesh,
        in_specs=(
            P(None, ("grp", "wide"), "narrow"),
            P(None, ("grp", "wide"), "narrow"),
            P(None, "narrow", ("grp", "wide")),
        ),
        out_specs=(P(None, "narrow", ("grp", "wide")), P("grp")),
        check_vma=False,
    )
```

```python
import functools

import jax
import jax.numpy as jnp
from jax import lax
from jax.experimental import pallas as pl
from jax.experimental.pallas import tpu as pltpu
from jax.sharding import PartitionSpec as P

ITERS = 3
LANES = 128
MOST_PAIRS = 1 << 19


def class_weight(class_codes):
    return jnp.where(
        class_codes == 3,
        1.0,
        jnp.where(class_codes == 2, 0.5, jnp.where(class_codes == 1, 0.25, 0.0)),
    ).astype(jnp.float32)


def split_bf16(value, terms):
    parts = []
    for _ in range(terms):
        part = value.astype(jnp.bfloat16)
        parts.append(part)
        value = value - part.astype(jnp.float32)
    return parts


SUBLANES = 8
NT = (((1,), (1,)), ((), ()))
TN = (((0,), (0,)), ((), ()))
dot = functools.partial(lax.dot_general, preferred_element_type=jnp.float32)


def lane_sums(value):
    rows = jnp.sum(value, axis=0, keepdims=True)
    return sum(rows[:, i : i + LANES] for i in range(0, rows.shape[1], LANES))


def tile_spots(per_dev, points):
    return [
        (slice(row, row + SUBLANES), slice(column, column + LANES))
        for row in range(0, per_dev, SUBLANES)
        for column in range(0, points, LANES)
    ]


def pack_kernel(dis_hbm, cls_hbm, x_hbm, out_ref, dis_ref, cls_ref, x_ref, sems):
    copies = [
        pltpu.make_async_copy(src, dst, sems.at[i])
        for i, (src, dst) in enumerate(
            [(dis_hbm, dis_ref), (cls_hbm, cls_ref), (x_hbm, x_ref)]
        )
    ]
    for copy in copies:
        copy.start()
    for copy in copies:
        copy.wait()
    spots = tile_spots(*dis_ref.shape)
    for i, spot in enumerate(spots):
        out_ref[i] = dis_ref[spot]
        out_ref[len(spots) + i] = class_weight(cls_ref[spot])
    half, per_dev = x_ref.shape[0] // 2, x_ref.shape[1]
    pad = jnp.zeros((half, LANES - 2 * per_dev), jnp.float32)
    out_ref[2 * len(spots)] = jnp.concatenate([x_ref[:half], x_ref[half:], pad], axis=1)


def held_slots(offsets, refs, tiles):
    me = lax.axis_index("wide")
    for bit, ref in enumerate(refs):
        for slot, offset in enumerate(offsets):
            yield ref, slot * tiles, me ^ offset ^ bit


def side_norm(top, bottom, coord_dims):
    pad = jnp.zeros((coord_dims - 6, top[0].shape[1]), jnp.float32)
    rows = [p.astype(jnp.float32) for p in (*top, *bottom)]
    return jnp.concatenate([*rows, pad], axis=0).astype(jnp.bfloat16)


def squares(own, x):
    coord_dims = x.shape[0]
    own_hi, own_mid, own_lo = (-2.0 * p for p in split_bf16(own, 3))
    hi, mid, lo = split_bf16(x, 3)
    own_norm = split_bf16(jnp.sum(own * own, axis=0, keepdims=True), 3)
    norm = split_bf16(jnp.sum(x * x, axis=0, keepdims=True) + 1.0, 3)
    left_ones = [jnp.ones((3, own.shape[1]), jnp.bfloat16)]
    right_ones = [jnp.ones((3, x.shape[1]), jnp.bfloat16)]
    left = [own_hi, own_hi, own_hi, own_mid, own_mid, own_lo]
    right = [hi, mid, lo, hi, mid, hi]
    left = jnp.concatenate([*left, side_norm(own_norm, left_ones, coord_dims)], axis=0)
    right = jnp.concatenate([*right, side_norm(right_ones, norm, coord_dims)], axis=0)
    return dot(left, right, TN), hi, mid


def moved(own, hi, mid, pull, scale):
    coord_dims, count = own.shape
    ones = jnp.ones((coord_dims, hi.shape[1]), jnp.bfloat16)
    sides = jnp.concatenate([hi, mid, ones], axis=0)
    sums = dot(jnp.concatenate(split_bf16(pull, 2), axis=0), sides, NT)
    sums = (sums[:count] + sums[count:]).T
    pulled = sums[:coord_dims] + sums[coord_dims : 2 * coord_dims]
    return own + (pulled - own * sums[2 * coord_dims : 2 * coord_dims + 1]) * scale


def group_kernel(offsets, per_dev, mine_ref, theirs_ref, out_ref, stress_ref,
                 dis_ref, weight_ref, tile_ref, inverse_ref):
    points = dis_ref.shape[0]
    spots = tile_spots(per_dev, points)
    tiles = 2 * len(spots) + 1
    for ref, base, place in held_slots(offsets, (mine_ref, theirs_ref), tiles):
        tile_ref[place] = ref[base + tiles - 1]
        for i, (rows, columns) in enumerate(spots):
            start = pl.multiple_of(place * per_dev + rows.start, SUBLANES)
            dis_ref[pl.ds(start, SUBLANES), columns] = ref[base + i]
            weight_ref[pl.ds(start, SUBLANES), columns] = ref[base + len(spots) + i]
    blocks = [tile_ref[i] for i in range(tile_ref.shape[0])]
    halves = [
        jnp.concatenate([t[:, low : low + per_dev] for t in blocks], axis=1)
        for low in (0, per_dev)
    ]
    x = jnp.concatenate(halves, axis=0)
    weight = weight_ref[...]
    ones = jnp.ones((x.shape[0], points), jnp.bfloat16)
    scale = 1.0 / (1.0 + dot(weight.astype(jnp.bfloat16), ones, NT).T[0:1])
    sums = [lane_sums(weight * dis_ref[...] * dis_ref[...])]
    for sweep in range(ITERS):
        square, hi, mid = squares(x, x)
        inverse = lax.rsqrt(square)
        misfit = dis_ref[...] - square * inverse
        weight = weight_ref[...]
        sums.append(lane_sums(weight * misfit * misfit))
        if sweep < ITERS - 1:
            x = moved(x, hi, mid, weight - weight * dis_ref[...] * inverse, scale)
    inverse_ref[...] = inverse
    place = lax.axis_index("wide")
    rows = pl.ds(pl.multiple_of(place * per_dev, SUBLANES), per_dev)
    scaled = jnp.concatenate([x, jnp.broadcast_to(scale, (SUBLANES, points))], axis=0)
    mine = jnp.zeros((scaled.shape[0], per_dev), jnp.float32)
    for i in range(points // per_dev):
        mine = jnp.where(place == i, scaled[:, i * per_dev : (i + 1) * per_dev], mine)
    own, scale = mine[: x.shape[0]], mine[x.shape[0] : x.shape[0] + 1]
    weight = weight_ref[rows, :]
    pull = weight - weight * dis_ref[rows, :] * inverse_ref[rows, :]
    out_ref[...] = moved(own, hi, mid, pull, scale)
    total = jnp.sum(jnp.concatenate(sums, axis=0), axis=1, keepdims=True)
    for sweep in range(ITERS):
        stress_ref[sweep] = jnp.sum(total[sweep + 1 : sweep + 2] / total[0:1])


def small_body(dissim, classes, coords):
    coord_dims, _, per_dev = coords.shape
    points = dissim.shape[2]
    devices = points // per_dev
    vmem = pl.BlockSpec(memory_space=pltpu.VMEM)
    hbm = pl.BlockSpec(memory_space=pltpu.HBM)
    f32 = functools.partial(jax.ShapeDtypeStruct, dtype=jnp.float32)
    params = pltpu.CompilerParams(vmem_limit_bytes=16 << 20)

    def swap(value, offset):
        return lax.ppermute(value, "wide", [(i, i ^ offset) for i in range(devices)])

    tiles = 2 * len(tile_spots(per_dev, points)) + 1
    inputs = (dissim[0], classes[0], coords[:, 0, :])
    packed = pl.pallas_call(
        pack_kernel,
        out_shape=f32((tiles, SUBLANES, LANES)),
        in_specs=[hbm] * 3,
        out_specs=vmem,
        scratch_shapes=[
            pltpu.VMEM((per_dev, points), jnp.float32),
            pltpu.VMEM((per_dev, points), jnp.int32),
            pltpu.VMEM((coord_dims, per_dev), jnp.float32),
            pltpu.SemaphoreType.DMA((3,)),
        ],
        compiler_params=params,
        name="pack",
    )(*(pltpu.with_memory_space_constraint(array, pltpu.HBM) for array in inputs))
    far, near, side = devices // 2, devices // 4, devices // 8
    held = {0: packed}
    for offset in (far, near, side, far | near | side):
        held[offset] = swap(packed, offset)
    for source, step in ((far, side), (near, side), (far, near)):
        held[source | step] = swap(held[source], step)
    offsets = list(held)
    mine = jnp.concatenate(list(held.values()), axis=0)
    theirs = swap(mine, 1)
    final, stress = pl.pallas_call(
        functools.partial(group_kernel, offsets, per_dev),
        out_shape=(f32((coord_dims, per_dev)), f32((ITERS,))),
        in_specs=[vmem, vmem],
        out_specs=(vmem, pl.BlockSpec(memory_space=pltpu.SMEM)),
        scratch_shapes=[
            pltpu.VMEM((points, points), jnp.float32),
            pltpu.VMEM((points, points), jnp.float32),
            pltpu.VMEM((devices, SUBLANES, LANES), jnp.float32),
            pltpu.VMEM((points, points), jnp.float32),
        ],
        compiler_params=params,
        name="group_smacof",
    )(mine, theirs)
    return (final[:, None, :], stress)


def distributed_body(dissim, classes, coords):
    halves = dissim.shape[0]
    per_dev = dissim.shape[1]
    columns = dissim.shape[2]
    coord_dims = coords.shape[0]
    row_count = halves * per_dev
    dis_tile = dissim.reshape(row_count, columns)
    weight = class_weight(classes.reshape(row_count, columns))
    denom_local = jnp.sum(weight * dis_tile * dis_tile)
    half_index = lax.axis_index("narrow")
    denom_total = lax.psum(denom_local, ("wide", "narrow"))
    positions = coords
    numbers = []
    for sweep in range(ITERS):
        row_points = lax.all_gather(positions, "narrow", axis=1, tiled=True)
        row_x = row_points.reshape(coord_dims, row_count)
        row_sq = jnp.sum(row_x * row_x, axis=0)
        fold_column_x = lax.dynamic_index_in_dim(
            lax.all_gather(row_points, "wide", axis=2, tiled=True), half_index, 1, keepdims=False
        )
        inner_prod = lax.dot_general(
            row_x,
            fold_column_x,
            (((0,), (0,)), ((), ())),
            precision=lax.Precision.HIGHEST,
            preferred_element_type=jnp.float32,
        )
        col_sq = jnp.sum(fold_column_x * fold_column_x, axis=0)
        distance = jnp.sqrt(row_sq[:, None] + col_sq[None, :] - 2.0 * inner_prod + 1.0)
        ratios = weight * dis_tile / distance
        pull_term = lax.dot_general(
            weight - ratios,
            fold_column_x,
            (((1,), (1,)), ((), ())),
            precision=lax.Precision.HIGHEST,
            preferred_element_type=jnp.float32,
        )
        misfit = dis_tile - distance
        pull_sums = pull_term.reshape(halves, per_dev, coord_dims).transpose(0, 2, 1)
        weight_sum, ratio_sum, pull_share = (
            lax.psum_scatter(
                jnp.sum(weight, axis=1).reshape(halves, per_dev),
                "narrow",
                scatter_dimension=0,
                tiled=True,
            ),
            lax.psum_scatter(
                jnp.sum(ratios, axis=1).reshape(halves, per_dev),
                "narrow",
                scatter_dimension=0,
                tiled=True,
            ),
            lax.psum_scatter(pull_sums, "narrow", scatter_dimension=0, tiled=True),
        )
        own_coords = positions[:, 0, :]
        updated = (own_coords * (1.0 + ratio_sum[0]) + pull_share[0]) / (1.0 + weight_sum[0])
        positions = updated[:, None, :]
        numbers.append(
            lax.psum(jnp.sum(weight * misfit * misfit), ("wide", "narrow")) / denom_total
        )
    stress = jnp.stack(numbers)
    return (positions, stress)


def solution(mesh):
    def body(dissim, classes, coords):
        coord_dims, halves, per_dev = coords.shape
        points, devices = dissim.shape[2], mesh.shape["wide"]
        small = halves == 1 and mesh.shape["narrow"] == 1 and points * points <= MOST_PAIRS
        small = small and coord_dims == 2 * SUBLANES and 2 * per_dev <= LANES
        small = small and per_dev % SUBLANES == 0 and points % LANES == 0
        small = small and devices == 16
        return (small_body if small else distributed_body)(dissim, classes, coords)

    return jax.shard_map(
        body,
        mesh=mesh,
        in_specs=(
            P(None, ("grp", "wide"), "narrow"),
            P(None, ("grp", "wide"), "narrow"),
            P(None, "narrow", ("grp", "wide")),
        ),
        out_specs=(P(None, "narrow", ("grp", "wide")), P("grp")),
        check_vma=False,
    )
```

```python
import functools

import jax
import jax.numpy as jnp
from jax import lax
from jax.experimental import pallas as pl
from jax.experimental.pallas import tpu as pltpu
from jax.sharding import PartitionSpec as P

ITERS = 3
LANES = 128
MOST_PAIRS = 1 << 19


def class_weight(class_codes):
    return jnp.where(
        class_codes == 3,
        1.0,
        jnp.where(class_codes == 2, 0.5, jnp.where(class_codes == 1, 0.25, 0.0)),
    ).astype(jnp.float32)


def split_bf16(value, terms):
    parts = []
    for _ in range(terms):
        part = value.astype(jnp.bfloat16)
        parts.append(part)
        value = value - part.astype(jnp.float32)
    return parts


SUBLANES = 8
NT = (((1,), (1,)), ((), ()))
TN = (((0,), (0,)), ((), ()))
dot = functools.partial(lax.dot_general, preferred_element_type=jnp.float32)


def lane_sums(value):
    rows = jnp.sum(value, axis=0, keepdims=True)
    return sum(rows[:, i : i + LANES] for i in range(0, rows.shape[1], LANES))


def tile_spots(per_dev, points):
    return [
        (slice(row, row + SUBLANES), slice(column, column + LANES))
        for row in range(0, per_dev, SUBLANES)
        for column in range(0, points, LANES)
    ]


def pack_kernel(dis_hbm, cls_hbm, x_hbm, out_ref, dis_ref, cls_ref, x_ref, sems):
    copies = [
        pltpu.make_async_copy(src, dst, sems.at[i])
        for i, (src, dst) in enumerate(
            [(dis_hbm, dis_ref), (cls_hbm, cls_ref), (x_hbm, x_ref)]
        )
    ]
    for copy in copies:
        copy.start()
    for copy in copies:
        copy.wait()
    spots = tile_spots(*dis_ref.shape)
    for i, spot in enumerate(spots):
        out_ref[i] = dis_ref[spot]
        out_ref[len(spots) + i] = class_weight(cls_ref[spot])
    half, per_dev = x_ref.shape[0] // 2, x_ref.shape[1]
    pad = jnp.zeros((half, LANES - 2 * per_dev), jnp.float32)
    out_ref[2 * len(spots)] = jnp.concatenate([x_ref[:half], x_ref[half:], pad], axis=1)


def held_slots(offsets, refs, tiles):
    me = lax.axis_index("wide")
    for bit, ref in enumerate(refs):
        for slot, offset in enumerate(offsets):
            yield ref, slot * tiles, me ^ offset ^ bit


def norm_rows(top, bottom, coord_dims):
    pad = jnp.zeros((coord_dims - 6, top[0].shape[1]), jnp.float32)
    rows = [p.astype(jnp.float32) for p in (*top, *bottom)]
    return jnp.concatenate([*rows, pad], axis=0).astype(jnp.bfloat16)


def left_side(x, parts):
    hi, mid, lo = (-2.0 * p for p in parts)
    norm = split_bf16(jnp.sum(x * x, axis=0, keepdims=True), 3)
    ones = [jnp.ones((3, x.shape[1]), jnp.bfloat16)]
    return jnp.concatenate([hi, hi, hi, mid, mid, lo, norm_rows(norm, ones, x.shape[0])], axis=0)


def right_side(x, parts):
    hi, mid, lo = parts
    norm = split_bf16(jnp.sum(x * x, axis=0, keepdims=True) + 1.0, 3)
    ones = [jnp.ones((3, x.shape[1]), jnp.bfloat16)]
    return jnp.concatenate([hi, mid, lo, hi, mid, hi, norm_rows(ones, norm, x.shape[0])], axis=0)


def moved(x, sides, pull, scale):
    coord_dims = x.shape[0]
    sums = sum(dot(sides, part, NT) for part in split_bf16(pull, 2))
    pulled = sums[:coord_dims] + sums[coord_dims : 2 * coord_dims]
    return x + (pulled - x * sums[2 * coord_dims : 2 * coord_dims + 1]) * scale


def group_kernel(offsets, per_dev, mine_ref, theirs_ref, out_ref, stress_ref,
                 dis_ref, weight_ref, tile_ref):
    points = dis_ref.shape[0]
    spots = tile_spots(per_dev, points)
    tiles = 2 * len(spots) + 1
    for ref, base, place in held_slots(offsets, (mine_ref, theirs_ref), tiles):
        tile_ref[place] = ref[base + tiles - 1]
        for i, (rows, columns) in enumerate(spots):
            start = pl.multiple_of(place * per_dev + rows.start, SUBLANES)
            dis_ref[pl.ds(start, SUBLANES), columns] = ref[base + i]
            weight_ref[pl.ds(start, SUBLANES), columns] = ref[base + len(spots) + i]
    blocks = [tile_ref[i] for i in range(tile_ref.shape[0])]
    halves = [
        jnp.concatenate([t[:, low : low + per_dev] for t in blocks], axis=1)
        for low in (0, per_dev)
    ]
    x = jnp.concatenate(halves, axis=0)
    coord_dims = x.shape[0]
    chunks = [slice(row, row + LANES) for row in range(0, points, LANES)]
    ones = jnp.ones((coord_dims, points), jnp.bfloat16)
    scales = [
        1.0 / (1.0 + dot(ones, weight_ref[rows].astype(jnp.bfloat16), NT)[0:1]) for rows in chunks
    ]
    denom = sum(lane_sums(weight_ref[rows] * dis_ref[rows] * dis_ref[rows]) for rows in chunks)
    place = lax.axis_index("wide")
    own_rows = pl.ds(pl.multiple_of(place * per_dev, SUBLANES), per_dev)
    shape = (points, per_dev)
    pick = lax.broadcasted_iota(jnp.int32, shape, 0) - lax.broadcasted_iota(jnp.int32, shape, 1)
    pick = (pick == place * per_dev).astype(jnp.float32).astype(jnp.bfloat16)
    sums = [denom]
    for sweep in range(ITERS):
        parts = split_bf16(x, 3)
        sides = jnp.concatenate([parts[0], parts[1], ones], axis=0)
        left, right = left_side(x, parts), right_side(x, parts)
        last = sweep == ITERS - 1
        stress, following = 0.0, []
        for rows, scale in zip(chunks, scales):
            square = dot(left[:, rows], right, TN)
            inverse = lax.rsqrt(square)
            weight, dis = weight_ref[rows], dis_ref[rows]
            misfit = dis - square * inverse
            stress += lane_sums(weight * misfit * misfit)
            if not last:
                pull = weight - weight * dis * inverse
                following.append(moved(x[:, rows], sides, pull, scale))
        sums.append(stress)
        if last:
            own = dot(jnp.concatenate(parts, axis=0), pick, (((1,), (0,)), ((), ())))
            own = sum(own[i * coord_dims : (i + 1) * coord_dims] for i in range(3))
            inverse = lax.rsqrt(dot(left_side(own, split_bf16(own, 3)), right, TN))
            weight = weight_ref[own_rows, :]
            scale = 1.0 / (1.0 + dot(ones, weight.astype(jnp.bfloat16), NT)[0:1])
            pull = weight - weight * dis_ref[own_rows, :] * inverse
            out_ref[...] = moved(own, sides, pull, scale)
        else:
            x = jnp.concatenate(following, axis=1)
    total = jnp.sum(jnp.concatenate(sums, axis=0), axis=1, keepdims=True)
    ratios = total[1:] / total[:1]
    lanes = lax.broadcasted_iota(jnp.int32, (ITERS, LANES), 1)
    lined = jnp.where(lanes == lax.broadcasted_iota(jnp.int32, (ITERS, LANES), 0), ratios, 0.0)
    stress_ref[...] = jnp.sum(lined, axis=0, keepdims=True)[:, :ITERS]


def small_body(dissim, classes, coords):
    coord_dims, _, per_dev = coords.shape
    points = dissim.shape[2]
    devices = points // per_dev
    vmem = pl.BlockSpec(memory_space=pltpu.VMEM)
    hbm = pl.BlockSpec(memory_space=pltpu.HBM)
    f32 = functools.partial(jax.ShapeDtypeStruct, dtype=jnp.float32)
    params = pltpu.CompilerParams(vmem_limit_bytes=16 << 20)

    def swap(value, offset):
        return lax.ppermute(value, "wide", [(i, i ^ offset) for i in range(devices)])

    tiles = 2 * len(tile_spots(per_dev, points)) + 1
    inputs = (dissim[0], classes[0], coords[:, 0, :])
    packed = pl.pallas_call(
        pack_kernel,
        out_shape=f32((tiles, SUBLANES, LANES)),
        in_specs=[hbm] * 3,
        out_specs=vmem,
        scratch_shapes=[
            pltpu.VMEM((per_dev, points), jnp.float32),
            pltpu.VMEM((per_dev, points), jnp.int32),
            pltpu.VMEM((coord_dims, per_dev), jnp.float32),
            pltpu.SemaphoreType.DMA((3,)),
        ],
        compiler_params=params,
        name="pack",
    )(*(pltpu.with_memory_space_constraint(array, pltpu.HBM) for array in inputs))
    far, near, side = devices // 2, devices // 4, devices // 8
    held = {0: packed}
    for offset in (far, near, side, far | near | side):
        held[offset] = swap(packed, offset)
    for source, step in ((far, side), (near, side), (far, near)):
        held[source | step] = swap(held[source], step)
    offsets = list(held)
    mine = jnp.concatenate(list(held.values()), axis=0)
    theirs = swap(mine, 1)
    final, stress = pl.pallas_call(
        functools.partial(group_kernel, offsets, per_dev),
        out_shape=(f32((coord_dims, per_dev)), f32((1, ITERS))),
        in_specs=[vmem, vmem],
        out_specs=(vmem, vmem),
        scratch_shapes=[
            pltpu.VMEM((points, points), jnp.float32),
            pltpu.VMEM((points, points), jnp.float32),
            pltpu.VMEM((devices, SUBLANES, LANES), jnp.float32),
        ],
        compiler_params=params,
        name="group_smacof",
    )(mine, theirs)
    return (final[:, None, :], stress[0])


def distributed_body(dissim, classes, coords):
    halves = dissim.shape[0]
    per_dev = dissim.shape[1]
    columns = dissim.shape[2]
    coord_dims = coords.shape[0]
    row_count = halves * per_dev
    dis_tile = dissim.reshape(row_count, columns)
    weight = class_weight(classes.reshape(row_count, columns))
    denom_local = jnp.sum(weight * dis_tile * dis_tile)
    half_index = lax.axis_index("narrow")
    denom_total = lax.psum(denom_local, ("wide", "narrow"))
    positions = coords
    numbers = []
    for sweep in range(ITERS):
        row_points = lax.all_gather(positions, "narrow", axis=1, tiled=True)
        row_x = row_points.reshape(coord_dims, row_count)
        row_sq = jnp.sum(row_x * row_x, axis=0)
        fold_column_x = lax.dynamic_index_in_dim(
            lax.all_gather(row_points, "wide", axis=2, tiled=True), half_index, 1, keepdims=False
        )
        inner_prod = lax.dot_general(
            row_x,
            fold_column_x,
            (((0,), (0,)), ((), ())),
            precision=lax.Precision.HIGHEST,
            preferred_element_type=jnp.float32,
        )
        col_sq = jnp.sum(fold_column_x * fold_column_x, axis=0)
        distance = jnp.sqrt(row_sq[:, None] + col_sq[None, :] - 2.0 * inner_prod + 1.0)
        ratios = weight * dis_tile / distance
        pull_term = lax.dot_general(
            weight - ratios,
            fold_column_x,
            (((1,), (1,)), ((), ())),
            precision=lax.Precision.HIGHEST,
            preferred_element_type=jnp.float32,
        )
        misfit = dis_tile - distance
        pull_sums = pull_term.reshape(halves, per_dev, coord_dims).transpose(0, 2, 1)
        weight_sum, ratio_sum, pull_share = (
            lax.psum_scatter(
                jnp.sum(weight, axis=1).reshape(halves, per_dev),
                "narrow",
                scatter_dimension=0,
                tiled=True,
            ),
            lax.psum_scatter(
                jnp.sum(ratios, axis=1).reshape(halves, per_dev),
                "narrow",
                scatter_dimension=0,
                tiled=True,
            ),
            lax.psum_scatter(pull_sums, "narrow", scatter_dimension=0, tiled=True),
        )
        own_coords = positions[:, 0, :]
        updated = (own_coords * (1.0 + ratio_sum[0]) + pull_share[0]) / (1.0 + weight_sum[0])
        positions = updated[:, None, :]
        numbers.append(
            lax.psum(jnp.sum(weight * misfit * misfit), ("wide", "narrow")) / denom_total
        )
    stress = jnp.stack(numbers)
    return (positions, stress)


def solution(mesh):
    def body(dissim, classes, coords):
        coord_dims, halves, per_dev = coords.shape
        points, devices = dissim.shape[2], mesh.shape["wide"]
        small = halves == 1 and mesh.shape["narrow"] == 1 and points * points <= MOST_PAIRS
        small = small and coord_dims == 2 * SUBLANES and 2 * per_dev <= LANES
        small = small and per_dev % SUBLANES == 0 and points % LANES == 0
        small = small and devices == 16
        return (small_body if small else distributed_body)(dissim, classes, coords)

    return jax.shard_map(
        body,
        mesh=mesh,
        in_specs=(
            P(None, ("grp", "wide"), "narrow"),
            P(None, ("grp", "wide"), "narrow"),
            P(None, "narrow", ("grp", "wide")),
        ),
        out_specs=(P(None, "narrow", ("grp", "wide")), P("grp")),
        check_vma=False,
    )
```

```python
import functools

import jax
import jax.numpy as jnp
from jax import lax
from jax.experimental import pallas as pl
from jax.experimental.pallas import tpu as pltpu
from jax.sharding import PartitionSpec as P

ITERS = 3
LANES = 128
MOST_PAIRS = 1 << 19


def class_weight(class_codes):
    return jnp.where(
        class_codes == 3,
        1.0,
        jnp.where(class_codes == 2, 0.5, jnp.where(class_codes == 1, 0.25, 0.0)),
    ).astype(jnp.float32)


def split_bf16(value, terms):
    parts = []
    for _ in range(terms):
        part = value.astype(jnp.bfloat16)
        parts.append(part)
        value = value - part.astype(jnp.float32)
    return parts


SUBLANES = 8
NT = (((1,), (1,)), ((), ()))
TN = (((0,), (0,)), ((), ()))
dot = functools.partial(lax.dot_general, preferred_element_type=jnp.float32)


def lane_sums(value):
    rows = jnp.sum(value, axis=0, keepdims=True)
    return sum(rows[:, i : i + LANES] for i in range(0, rows.shape[1], LANES))


def tile_spots(per_dev, points):
    return [
        (slice(row, row + SUBLANES), slice(column, column + LANES))
        for row in range(0, per_dev, SUBLANES)
        for column in range(0, points, LANES)
    ]


def pack_kernel(dis_hbm, cls_hbm, x_hbm, out_ref, dis_ref, cls_ref, x_ref, sems):
    copies = [
        pltpu.make_async_copy(src, dst, sems.at[i])
        for i, (src, dst) in enumerate(
            [(dis_hbm, dis_ref), (cls_hbm, cls_ref), (x_hbm, x_ref)]
        )
    ]
    for copy in copies:
        copy.start()
    for copy in copies:
        copy.wait()
    spots = tile_spots(*dis_ref.shape)
    for i, spot in enumerate(spots):
        out_ref[i] = dis_ref[spot]
        out_ref[len(spots) + i] = class_weight(cls_ref[spot])
    half, per_dev = x_ref.shape[0] // 2, x_ref.shape[1]
    pad = jnp.zeros((half, LANES - 2 * per_dev), jnp.float32)
    out_ref[2 * len(spots)] = jnp.concatenate([x_ref[:half], x_ref[half:], pad], axis=1)


def held_slots(offsets, refs, tiles):
    me = lax.axis_index("wide")
    for bit, ref in enumerate(refs):
        for slot, offset in enumerate(offsets):
            yield ref, slot * tiles, me ^ offset ^ bit


def norm_rows(top, bottom, coord_dims):
    pad = jnp.zeros((coord_dims - 6, top[0].shape[1]), jnp.float32)
    rows = [p.astype(jnp.float32) for p in (*top, *bottom)]
    return jnp.concatenate([*rows, pad], axis=0).astype(jnp.bfloat16)


def left_side(x, parts):
    hi, mid, lo = (-2.0 * p for p in parts)
    norm = split_bf16(jnp.sum(x * x, axis=0, keepdims=True), 3)
    ones = [jnp.ones((3, x.shape[1]), jnp.bfloat16)]
    return jnp.concatenate([hi, hi, hi, mid, mid, lo, norm_rows(norm, ones, x.shape[0])], axis=0)


def right_side(x, parts):
    hi, mid, lo = parts
    norm = split_bf16(jnp.sum(x * x, axis=0, keepdims=True) + 1.0, 3)
    ones = [jnp.ones((3, x.shape[1]), jnp.bfloat16)]
    return jnp.concatenate([hi, mid, lo, hi, mid, hi, norm_rows(ones, norm, x.shape[0])], axis=0)


def moved(x, sides, pull, scale):
    coord_dims = x.shape[0]
    parts = jnp.concatenate(split_bf16(pull, 2), axis=1)
    sums = dot(parts, jnp.concatenate([sides, sides], axis=1), NT).T
    pulled = sums[:coord_dims] + sums[coord_dims : 2 * coord_dims]
    return x + (pulled - x * sums[2 * coord_dims : 2 * coord_dims + 1]) * scale


def group_kernel(offsets, per_dev, mine_ref, theirs_ref, out_ref, stress_ref,
                 dis_ref, weight_ref, tile_ref):
    points = dis_ref.shape[0]
    spots = tile_spots(per_dev, points)
    tiles = 2 * len(spots) + 1
    for ref, base, place in held_slots(offsets, (mine_ref, theirs_ref), tiles):
        tile_ref[place] = ref[base + tiles - 1]
        for i, (rows, columns) in enumerate(spots):
            start = pl.multiple_of(place * per_dev + rows.start, SUBLANES)
            dis_ref[pl.ds(start, SUBLANES), columns] = ref[base + i]
            weight_ref[pl.ds(start, SUBLANES), columns] = ref[base + len(spots) + i]
    blocks = [tile_ref[i] for i in range(tile_ref.shape[0])]
    halves = [
        jnp.concatenate([t[:, low : low + per_dev] for t in blocks], axis=1)
        for low in (0, per_dev)
    ]
    x = jnp.concatenate(halves, axis=0)
    coord_dims = x.shape[0]
    chunks = [slice(row, row + LANES) for row in range(0, points, LANES)]
    ones = jnp.ones((coord_dims, points), jnp.bfloat16)
    scales = [
        1.0 / (1.0 + dot(ones, weight_ref[rows].astype(jnp.bfloat16), NT)[0:1]) for rows in chunks
    ]
    denom = sum(lane_sums(weight_ref[rows] * dis_ref[rows] * dis_ref[rows]) for rows in chunks)
    place = lax.axis_index("wide")
    own_rows = pl.ds(pl.multiple_of(place * per_dev, SUBLANES), per_dev)
    shape = (points, per_dev)
    pick = lax.broadcasted_iota(jnp.int32, shape, 0) - lax.broadcasted_iota(jnp.int32, shape, 1)
    pick = (pick == place * per_dev).astype(jnp.float32).astype(jnp.bfloat16)
    sums = [denom]
    for sweep in range(ITERS):
        parts = split_bf16(x, 3)
        sides = jnp.concatenate([parts[0], parts[1], ones], axis=0)
        left, right = left_side(x, parts), right_side(x, parts)
        last = sweep == ITERS - 1
        stress, following = 0.0, []
        for rows, scale in zip(chunks, scales):
            square = dot(left[:, rows], right, TN)
            inverse = lax.rsqrt(square)
            weight, dis = weight_ref[rows], dis_ref[rows]
            misfit = dis - square * inverse
            stress += lane_sums(weight * misfit * misfit)
            if not last:
                pull = weight - weight * dis * inverse
                following.append(moved(x[:, rows], sides, pull, scale))
        sums.append(stress)
        if last:
            own = dot(jnp.concatenate(parts, axis=0), pick, (((1,), (0,)), ((), ())))
            own = sum(own[i * coord_dims : (i + 1) * coord_dims] for i in range(3))
            inverse = lax.rsqrt(dot(left_side(own, split_bf16(own, 3)), right, TN))
            weight = weight_ref[own_rows, :]
            scale = 1.0 / (1.0 + dot(ones, weight.astype(jnp.bfloat16), NT)[0:1])
            pull = weight - weight * dis_ref[own_rows, :] * inverse
            out_ref[...] = moved(own, sides, pull, scale)
        else:
            x = jnp.concatenate(following, axis=1)
    total = jnp.sum(jnp.concatenate(sums, axis=0), axis=1, keepdims=True)
    ratios = total[1:] / total[:1]
    lanes = lax.broadcasted_iota(jnp.int32, (ITERS, LANES), 1)
    lined = jnp.where(lanes == lax.broadcasted_iota(jnp.int32, (ITERS, LANES), 0), ratios, 0.0)
    stress_ref[...] = jnp.sum(lined, axis=0, keepdims=True)[:, :ITERS]


def small_body(dissim, classes, coords):
    coord_dims, _, per_dev = coords.shape
    points = dissim.shape[2]
    devices = points // per_dev
    vmem = pl.BlockSpec(memory_space=pltpu.VMEM)
    hbm = pl.BlockSpec(memory_space=pltpu.HBM)
    f32 = functools.partial(jax.ShapeDtypeStruct, dtype=jnp.float32)
    params = pltpu.CompilerParams(vmem_limit_bytes=16 << 20)

    def swap(value, offset):
        return lax.ppermute(value, "wide", [(i, i ^ offset) for i in range(devices)])

    tiles = 2 * len(tile_spots(per_dev, points)) + 1
    inputs = (dissim[0], classes[0], coords[:, 0, :])
    packed = pl.pallas_call(
        pack_kernel,
        out_shape=f32((tiles, SUBLANES, LANES)),
        in_specs=[hbm] * 3,
        out_specs=vmem,
        scratch_shapes=[
            pltpu.VMEM((per_dev, points), jnp.float32),
            pltpu.VMEM((per_dev, points), jnp.int32),
            pltpu.VMEM((coord_dims, per_dev), jnp.float32),
            pltpu.SemaphoreType.DMA((3,)),
        ],
        compiler_params=params,
        name="pack",
    )(*(pltpu.with_memory_space_constraint(array, pltpu.HBM) for array in inputs))
    far, near, side = devices // 2, devices // 4, devices // 8
    held = {0: packed}
    for offset in (far, side, near, far | near | side, near | side):
        held[offset] = swap(packed, offset)
    for step in (side, near):
        held[far | step] = swap(held[far], step)
    offsets = list(held)
    mine = jnp.concatenate(list(held.values()), axis=0)
    theirs = swap(mine, 1)
    final, stress = pl.pallas_call(
        functools.partial(group_kernel, offsets, per_dev),
        out_shape=(f32((coord_dims, per_dev)), f32((1, ITERS))),
        in_specs=[vmem, vmem],
        out_specs=(vmem, vmem),
        scratch_shapes=[
            pltpu.VMEM((points, points), jnp.float32),
            pltpu.VMEM((points, points), jnp.float32),
            pltpu.VMEM((devices, SUBLANES, LANES), jnp.float32),
        ],
        compiler_params=params,
        name="group_smacof",
    )(mine, theirs)
    return (final[:, None, :], stress[0])


def distributed_body(dissim, classes, coords):
    halves = dissim.shape[0]
    per_dev = dissim.shape[1]
    columns = dissim.shape[2]
    coord_dims = coords.shape[0]
    row_count = halves * per_dev
    dis_tile = dissim.reshape(row_count, columns)
    weight = class_weight(classes.reshape(row_count, columns))
    denom_local = jnp.sum(weight * dis_tile * dis_tile)
    half_index = lax.axis_index("narrow")
    denom_total = lax.psum(denom_local, ("wide", "narrow"))
    positions = coords
    numbers = []
    for sweep in range(ITERS):
        row_points = lax.all_gather(positions, "narrow", axis=1, tiled=True)
        row_x = row_points.reshape(coord_dims, row_count)
        row_sq = jnp.sum(row_x * row_x, axis=0)
        fold_column_x = lax.dynamic_index_in_dim(
            lax.all_gather(row_points, "wide", axis=2, tiled=True), half_index, 1, keepdims=False
        )
        inner_prod = lax.dot_general(
            row_x,
            fold_column_x,
            (((0,), (0,)), ((), ())),
            precision=lax.Precision.HIGHEST,
            preferred_element_type=jnp.float32,
        )
        col_sq = jnp.sum(fold_column_x * fold_column_x, axis=0)
        distance = jnp.sqrt(row_sq[:, None] + col_sq[None, :] - 2.0 * inner_prod + 1.0)
        ratios = weight * dis_tile / distance
        pull_term = lax.dot_general(
            weight - ratios,
            fold_column_x,
            (((1,), (1,)), ((), ())),
            precision=lax.Precision.HIGHEST,
            preferred_element_type=jnp.float32,
        )
        misfit = dis_tile - distance
        pull_sums = pull_term.reshape(halves, per_dev, coord_dims).transpose(0, 2, 1)
        weight_sum, ratio_sum, pull_share = (
            lax.psum_scatter(
                jnp.sum(weight, axis=1).reshape(halves, per_dev),
                "narrow",
                scatter_dimension=0,
                tiled=True,
            ),
            lax.psum_scatter(
                jnp.sum(ratios, axis=1).reshape(halves, per_dev),
                "narrow",
                scatter_dimension=0,
                tiled=True,
            ),
            lax.psum_scatter(pull_sums, "narrow", scatter_dimension=0, tiled=True),
        )
        own_coords = positions[:, 0, :]
        updated = (own_coords * (1.0 + ratio_sum[0]) + pull_share[0]) / (1.0 + weight_sum[0])
        positions = updated[:, None, :]
        numbers.append(
            lax.psum(jnp.sum(weight * misfit * misfit), ("wide", "narrow")) / denom_total
        )
    stress = jnp.stack(numbers)
    return (positions, stress)


def solution(mesh):
    def body(dissim, classes, coords):
        coord_dims, halves, per_dev = coords.shape
        points, devices = dissim.shape[2], mesh.shape["wide"]
        small = halves == 1 and mesh.shape["narrow"] == 1 and points * points <= MOST_PAIRS
        small = small and coord_dims == 2 * SUBLANES and 2 * per_dev <= LANES
        small = small and per_dev % SUBLANES == 0 and points % LANES == 0
        small = small and devices == 16
        return (small_body if small else distributed_body)(dissim, classes, coords)

    return jax.shard_map(
        body,
        mesh=mesh,
        in_specs=(
            P(None, ("grp", "wide"), "narrow"),
            P(None, ("grp", "wide"), "narrow"),
            P(None, "narrow", ("grp", "wide")),
        ),
        out_specs=(P(None, "narrow", ("grp", "wide")), P("grp")),
        check_vma=False,
    )
```

```python
import functools

import jax
import jax.numpy as jnp
from jax import lax
from jax.experimental import pallas as pl
from jax.experimental.pallas import tpu as pltpu
from jax.sharding import PartitionSpec as P

ITERS = 3
LANES = 128
MOST_PAIRS = 1 << 19


def class_weight(class_codes):
    return jnp.where(
        class_codes == 3,
        1.0,
        jnp.where(class_codes == 2, 0.5, jnp.where(class_codes == 1, 0.25, 0.0)),
    ).astype(jnp.float32)


def split_bf16(value, terms):
    parts = []
    for _ in range(terms):
        part = value.astype(jnp.bfloat16)
        parts.append(part)
        value = value - part.astype(jnp.float32)
    return parts


SUBLANES = 8
NT = (((1,), (1,)), ((), ()))
TN = (((0,), (0,)), ((), ()))
dot = functools.partial(lax.dot_general, preferred_element_type=jnp.float32)


def lane_sums(value):
    rows = jnp.sum(value, axis=0, keepdims=True)
    return sum(rows[:, i : i + LANES] for i in range(0, rows.shape[1], LANES))


def tile_spots(per_dev, points):
    return [
        (slice(row, row + SUBLANES), slice(column, column + LANES))
        for row in range(0, per_dev, SUBLANES)
        for column in range(0, points, LANES)
    ]


def pack_kernel(dis_hbm, cls_hbm, x_hbm, out_ref, dis_ref, cls_ref, x_ref, sems):
    copies = [
        pltpu.make_async_copy(src, dst, sems.at[i])
        for i, (src, dst) in enumerate(
            [(dis_hbm, dis_ref), (cls_hbm, cls_ref), (x_hbm, x_ref)]
        )
    ]
    for copy in copies:
        copy.start()
    for copy in copies:
        copy.wait()
    spots = tile_spots(*dis_ref.shape)
    for i, spot in enumerate(spots):
        out_ref[i] = dis_ref[spot]
        out_ref[len(spots) + i] = class_weight(cls_ref[spot])
    half, per_dev = x_ref.shape[0] // 2, x_ref.shape[1]
    pad = jnp.zeros((half, LANES - 2 * per_dev), jnp.float32)
    out_ref[2 * len(spots)] = jnp.concatenate([x_ref[:half], x_ref[half:], pad], axis=1)


def held_slots(offsets, refs, tiles):
    me = lax.axis_index("wide")
    core = lax.rem(me, 2)
    for bit, ref in enumerate(refs):
        for slot, pair in enumerate(zip(*offsets)):
            offset = pair[bit] + core * (pair[1 - bit] - pair[bit])
            yield ref, slot * tiles, me ^ offset ^ bit


def norm_rows(top, bottom, coord_dims):
    pad = jnp.zeros((coord_dims - 6, top[0].shape[1]), jnp.float32)
    rows = [p.astype(jnp.float32) for p in (*top, *bottom)]
    return jnp.concatenate([*rows, pad], axis=0).astype(jnp.bfloat16)


def left_side(x, parts):
    hi, mid, lo = (-2.0 * p for p in parts)
    norm = split_bf16(jnp.sum(x * x, axis=0, keepdims=True), 3)
    ones = [jnp.ones((3, x.shape[1]), jnp.bfloat16)]
    return jnp.concatenate([hi, hi, hi, mid, mid, lo, norm_rows(norm, ones, x.shape[0])], axis=0)


def right_side(x, parts):
    hi, mid, lo = parts
    norm = split_bf16(jnp.sum(x * x, axis=0, keepdims=True) + 1.0, 3)
    ones = [jnp.ones((3, x.shape[1]), jnp.bfloat16)]
    return jnp.concatenate([hi, mid, lo, hi, mid, hi, norm_rows(ones, norm, x.shape[0])], axis=0)


def moved(x, sides, pull, scale):
    coord_dims = x.shape[0]
    parts = jnp.concatenate(split_bf16(pull, 2), axis=1)
    sums = dot(parts, jnp.concatenate([sides, sides], axis=1), NT).T
    pulled = sums[:coord_dims] + sums[coord_dims : 2 * coord_dims]
    return x + (pulled - x * sums[2 * coord_dims : 2 * coord_dims + 1]) * scale


def group_kernel(offsets, per_dev, mine_ref, theirs_ref, out_ref, stress_ref,
                 dis_ref, weight_ref, tile_ref):
    points = dis_ref.shape[0]
    spots = tile_spots(per_dev, points)
    tiles = 2 * len(spots) + 1
    for ref, base, place in held_slots(offsets, (mine_ref, theirs_ref), tiles):
        tile_ref[place] = ref[base + tiles - 1]
        for i, (rows, columns) in enumerate(spots):
            start = pl.multiple_of(place * per_dev + rows.start, SUBLANES)
            dis_ref[pl.ds(start, SUBLANES), columns] = ref[base + i]
            weight_ref[pl.ds(start, SUBLANES), columns] = ref[base + len(spots) + i]
    blocks = [tile_ref[i] for i in range(tile_ref.shape[0])]
    halves = [
        jnp.concatenate([t[:, low : low + per_dev] for t in blocks], axis=1)
        for low in (0, per_dev)
    ]
    x = jnp.concatenate(halves, axis=0)
    coord_dims = x.shape[0]
    chunks = [slice(row, row + LANES) for row in range(0, points, LANES)]
    ones = jnp.ones((coord_dims, points), jnp.bfloat16)
    scales = [
        1.0 / (1.0 + dot(ones, weight_ref[rows].astype(jnp.bfloat16), NT)[0:1]) for rows in chunks
    ]
    denom = sum(lane_sums(weight_ref[rows] * dis_ref[rows] * dis_ref[rows]) for rows in chunks)
    place = lax.axis_index("wide")
    own_rows = pl.ds(pl.multiple_of(place * per_dev, SUBLANES), per_dev)
    shape = (points, per_dev)
    pick = lax.broadcasted_iota(jnp.int32, shape, 0) - lax.broadcasted_iota(jnp.int32, shape, 1)
    pick = (pick == place * per_dev).astype(jnp.float32).astype(jnp.bfloat16)
    sums = [denom]
    for sweep in range(ITERS):
        parts = split_bf16(x, 3)
        sides = jnp.concatenate([parts[0], parts[1], ones], axis=0)
        left, right = left_side(x, parts), right_side(x, parts)
        last = sweep == ITERS - 1
        stress, following = 0.0, []
        for rows, scale in zip(chunks, scales):
            square = dot(left[:, rows], right, TN)
            inverse = lax.rsqrt(square)
            weight, dis = weight_ref[rows], dis_ref[rows]
            misfit = dis - square * inverse
            stress += lane_sums(weight * misfit * misfit)
            if not last:
                pull = weight - weight * dis * inverse
                following.append(moved(x[:, rows], sides, pull, scale))
        sums.append(stress)
        if last:
            own = dot(jnp.concatenate(parts, axis=0), pick, (((1,), (0,)), ((), ())))
            own = sum(own[i * coord_dims : (i + 1) * coord_dims] for i in range(3))
            inverse = lax.rsqrt(dot(left_side(own, split_bf16(own, 3)), right, TN))
            weight = weight_ref[own_rows, :]
            scale = 1.0 / (1.0 + dot(ones, weight.astype(jnp.bfloat16), NT)[0:1])
            pull = weight - weight * dis_ref[own_rows, :] * inverse
            out_ref[...] = moved(own, sides, pull, scale)
        else:
            x = jnp.concatenate(following, axis=1)
    total = jnp.sum(jnp.concatenate(sums, axis=0), axis=1, keepdims=True)
    ratios = total[1:] / total[:1]
    lanes = lax.broadcasted_iota(jnp.int32, (ITERS, LANES), 1)
    lined = jnp.where(lanes == lax.broadcasted_iota(jnp.int32, (ITERS, LANES), 0), ratios, 0.0)
    stress_ref[...] = jnp.sum(lined, axis=0, keepdims=True)[:, :ITERS]


def small_body(dissim, classes, coords):
    coord_dims, _, per_dev = coords.shape
    points = dissim.shape[2]
    devices = points // per_dev
    vmem = pl.BlockSpec(memory_space=pltpu.VMEM)
    hbm = pl.BlockSpec(memory_space=pltpu.HBM)
    f32 = functools.partial(jax.ShapeDtypeStruct, dtype=jnp.float32)
    params = pltpu.CompilerParams(vmem_limit_bytes=16 << 20)

    def swap(value, steps):
        return lax.ppermute(value, "wide", [(i, i ^ steps[i % 2]) for i in range(devices)])

    tiles = 2 * len(tile_spots(per_dev, points)) + 1
    inputs = (dissim[0], classes[0], coords[:, 0, :])
    packed = pl.pallas_call(
        pack_kernel,
        out_shape=f32((tiles, SUBLANES, LANES)),
        in_specs=[hbm] * 3,
        out_specs=vmem,
        scratch_shapes=[
            pltpu.VMEM((per_dev, points), jnp.float32),
            pltpu.VMEM((per_dev, points), jnp.int32),
            pltpu.VMEM((coord_dims, per_dev), jnp.float32),
            pltpu.SemaphoreType.DMA((3,)),
        ],
        compiler_params=params,
        name="pack",
    )(*(pltpu.with_memory_space_constraint(array, pltpu.HBM) for array in inputs))
    far, near, side = devices // 2, devices // 4, devices // 8
    firsts = (
        (far | side, near, near | side, far | near, side),
        (far | near, near, side, far | side, near | side),
    )
    relays = ((near, side), (side, near))
    held = [packed] + [swap(packed, steps) for steps in zip(*firsts)]
    held += [swap(held[1], steps) for steps in zip(*relays)]
    offsets = [
        (0, *first, *(first[0] ^ step for step in relay)) for first, relay in zip(firsts, relays)
    ]
    mine = jnp.concatenate(held, axis=0)
    theirs = swap(mine, (1, 1))
    final, stress = pl.pallas_call(
        functools.partial(group_kernel, offsets, per_dev),
        out_shape=(f32((coord_dims, per_dev)), f32((1, ITERS))),
        in_specs=[vmem, vmem],
        out_specs=(vmem, vmem),
        scratch_shapes=[
            pltpu.VMEM((points, points), jnp.float32),
            pltpu.VMEM((points, points), jnp.float32),
            pltpu.VMEM((devices, SUBLANES, LANES), jnp.float32),
        ],
        compiler_params=params,
        name="group_smacof",
    )(mine, theirs)
    return (final[:, None, :], stress[0])


def distributed_body(dissim, classes, coords):
    halves = dissim.shape[0]
    per_dev = dissim.shape[1]
    columns = dissim.shape[2]
    coord_dims = coords.shape[0]
    row_count = halves * per_dev
    dis_tile = dissim.reshape(row_count, columns)
    weight = class_weight(classes.reshape(row_count, columns))
    denom_local = jnp.sum(weight * dis_tile * dis_tile)
    half_index = lax.axis_index("narrow")
    denom_total = lax.psum(denom_local, ("wide", "narrow"))
    positions = coords
    numbers = []
    for sweep in range(ITERS):
        row_points = lax.all_gather(positions, "narrow", axis=1, tiled=True)
        row_x = row_points.reshape(coord_dims, row_count)
        row_sq = jnp.sum(row_x * row_x, axis=0)
        fold_column_x = lax.dynamic_index_in_dim(
            lax.all_gather(row_points, "wide", axis=2, tiled=True), half_index, 1, keepdims=False
        )
        inner_prod = lax.dot_general(
            row_x,
            fold_column_x,
            (((0,), (0,)), ((), ())),
            precision=lax.Precision.HIGHEST,
            preferred_element_type=jnp.float32,
        )
        col_sq = jnp.sum(fold_column_x * fold_column_x, axis=0)
        distance = jnp.sqrt(row_sq[:, None] + col_sq[None, :] - 2.0 * inner_prod + 1.0)
        ratios = weight * dis_tile / distance
        pull_term = lax.dot_general(
            weight - ratios,
            fold_column_x,
            (((1,), (1,)), ((), ())),
            precision=lax.Precision.HIGHEST,
            preferred_element_type=jnp.float32,
        )
        misfit = dis_tile - distance
        pull_sums = pull_term.reshape(halves, per_dev, coord_dims).transpose(0, 2, 1)
        weight_sum, ratio_sum, pull_share = (
            lax.psum_scatter(
                jnp.sum(weight, axis=1).reshape(halves, per_dev),
                "narrow",
                scatter_dimension=0,
                tiled=True,
            ),
            lax.psum_scatter(
                jnp.sum(ratios, axis=1).reshape(halves, per_dev),
                "narrow",
                scatter_dimension=0,
                tiled=True,
            ),
            lax.psum_scatter(pull_sums, "narrow", scatter_dimension=0, tiled=True),
        )
        own_coords = positions[:, 0, :]
        updated = (own_coords * (1.0 + ratio_sum[0]) + pull_share[0]) / (1.0 + weight_sum[0])
        positions = updated[:, None, :]
        numbers.append(
            lax.psum(jnp.sum(weight * misfit * misfit), ("wide", "narrow")) / denom_total
        )
    stress = jnp.stack(numbers)
    return (positions, stress)


def solution(mesh):
    def body(dissim, classes, coords):
        coord_dims, halves, per_dev = coords.shape
        points, devices = dissim.shape[2], mesh.shape["wide"]
        small = halves == 1 and mesh.shape["narrow"] == 1 and points * points <= MOST_PAIRS
        small = small and coord_dims == 2 * SUBLANES and 2 * per_dev <= LANES
        small = small and per_dev % SUBLANES == 0 and points % LANES == 0
        small = small and devices == 16
        return (small_body if small else distributed_body)(dissim, classes, coords)

    return jax.shard_map(
        body,
        mesh=mesh,
        in_specs=(
            P(None, ("grp", "wide"), "narrow"),
            P(None, ("grp", "wide"), "narrow"),
            P(None, "narrow", ("grp", "wide")),
        ),
        out_specs=(P(None, "narrow", ("grp", "wide")), P("grp")),
        check_vma=False,
    )
```

```python
import functools

import jax
import jax.numpy as jnp
from jax import lax
from jax.experimental import pallas as pl
from jax.experimental.pallas import tpu as pltpu
from jax.sharding import PartitionSpec as P

ITERS = 3
LANES = 128
MOST_PAIRS = 1 << 19


def class_weight(class_codes):
    return jnp.where(
        class_codes == 3,
        1.0,
        jnp.where(class_codes == 2, 0.5, jnp.where(class_codes == 1, 0.25, 0.0)),
    ).astype(jnp.float32)


def split_bf16(value, terms):
    parts = []
    for _ in range(terms):
        part = value.astype(jnp.bfloat16)
        parts.append(part)
        value = value - part.astype(jnp.float32)
    return parts


SUBLANES = 8
NT = (((1,), (1,)), ((), ()))
TN = (((0,), (0,)), ((), ()))
dot = functools.partial(lax.dot_general, preferred_element_type=jnp.float32)


def lane_sums(value):
    rows = jnp.sum(value, axis=0, keepdims=True)
    return sum(rows[:, i : i + LANES] for i in range(0, rows.shape[1], LANES))


def tile_spots(per_dev, points):
    return [
        (slice(row, row + SUBLANES), slice(column, column + LANES))
        for row in range(0, per_dev, SUBLANES)
        for column in range(0, points, LANES)
    ]


def pack_kernel(dis_hbm, cls_hbm, x_hbm, out_ref, dis_ref, cls_ref, x_ref, sems):
    copies = [
        pltpu.make_async_copy(src, dst, sems.at[i])
        for i, (src, dst) in enumerate(
            [(dis_hbm, dis_ref), (cls_hbm, cls_ref), (x_hbm, x_ref)]
        )
    ]
    for copy in copies:
        copy.start()
    for copy in copies:
        copy.wait()
    spots = tile_spots(*dis_ref.shape)
    for i, spot in enumerate(spots):
        out_ref[i] = dis_ref[spot]
        out_ref[len(spots) + i] = class_weight(cls_ref[spot])
    half, per_dev = x_ref.shape[0] // 2, x_ref.shape[1]
    pad = jnp.zeros((half, LANES - 2 * per_dev), jnp.float32)
    out_ref[2 * len(spots)] = jnp.concatenate([x_ref[:half], x_ref[half:], pad], axis=1)


def held_slots(offsets, refs, tiles):
    me = lax.axis_index("wide")
    for bit, ref in enumerate(refs):
        for slot, offset in enumerate(offsets):
            yield ref, slot * tiles, me ^ offset ^ bit


def norm_rows(top, bottom, coord_dims):
    pad = jnp.zeros((coord_dims - 6, top[0].shape[1]), jnp.float32)
    rows = [p.astype(jnp.float32) for p in (*top, *bottom)]
    return jnp.concatenate([*rows, pad], axis=0).astype(jnp.bfloat16)


def left_side(x, parts):
    hi, mid, lo = (-2.0 * p for p in parts)
    norm = split_bf16(jnp.sum(x * x, axis=0, keepdims=True), 3)
    ones = [jnp.ones((3, x.shape[1]), jnp.bfloat16)]
    return jnp.concatenate([hi, hi, hi, mid, mid, lo, norm_rows(norm, ones, x.shape[0])], axis=0)


def right_side(x, parts):
    hi, mid, lo = parts
    norm = split_bf16(jnp.sum(x * x, axis=0, keepdims=True) + 1.0, 3)
    ones = [jnp.ones((3, x.shape[1]), jnp.bfloat16)]
    return jnp.concatenate([hi, mid, lo, hi, mid, hi, norm_rows(ones, norm, x.shape[0])], axis=0)


def inverse_weight(weight, ones):
    return 1.0 / (1.0 + dot(weight.astype(jnp.bfloat16), ones, NT).T[0:1])


def moved(x, sides, push, scale):
    coord_dims = x.shape[0]
    parts = jnp.concatenate(split_bf16(push, 2), axis=1)
    sums = dot(parts, jnp.concatenate([sides, sides], axis=1), NT).T
    pushed = sums[:coord_dims] + sums[coord_dims : 2 * coord_dims]
    return x + (x * sums[2 * coord_dims : 2 * coord_dims + 1] - pushed) * scale


def group_kernel(offsets, per_dev, mine_ref, theirs_ref, out_ref, stress_ref,
                 dis_ref, weight_ref, tile_ref):
    points = dis_ref.shape[0]
    spots = tile_spots(per_dev, points)
    tiles = 2 * len(spots) + 1
    for ref, base, place in held_slots(offsets, (mine_ref, theirs_ref), tiles):
        tile_ref[place] = ref[base + tiles - 1]
        for i, (rows, columns) in enumerate(spots):
            start = pl.multiple_of(place * per_dev + rows.start, SUBLANES)
            dis_ref[pl.ds(start, SUBLANES), columns] = ref[base + i]
            weight_ref[pl.ds(start, SUBLANES), columns] = ref[base + len(spots) + i]
    blocks = [tile_ref[i] for i in range(tile_ref.shape[0])]
    halves = [
        jnp.concatenate([t[:, low : low + per_dev] for t in blocks], axis=1)
        for low in (0, per_dev)
    ]
    x = jnp.concatenate(halves, axis=0)
    coord_dims = x.shape[0]
    chunks = [slice(row, row + LANES) for row in range(0, points, LANES)]
    ones = jnp.ones((coord_dims, points), jnp.bfloat16)
    scales = [inverse_weight(weight_ref[rows], ones) for rows in chunks]
    denom = sum(lane_sums(weight_ref[rows] * dis_ref[rows] * dis_ref[rows]) for rows in chunks)
    place = lax.axis_index("wide")
    own_rows = pl.ds(pl.multiple_of(place * per_dev, SUBLANES), per_dev)
    shape = (points, per_dev)
    pick = lax.broadcasted_iota(jnp.int32, shape, 0) - lax.broadcasted_iota(jnp.int32, shape, 1)
    pick = (pick == place * per_dev).astype(jnp.float32).astype(jnp.bfloat16)
    sums = [denom]
    for sweep in range(ITERS):
        parts = split_bf16(x, 3)
        sides = jnp.concatenate([parts[0], parts[1], ones], axis=0)
        left, right = left_side(x, parts), right_side(x, parts)
        last = sweep == ITERS - 1
        stress, following = 0.0, []
        for rows, scale in zip(chunks, scales):
            square = dot(left[:, rows], right, TN)
            inverse = lax.rsqrt(square)
            weight, dis = weight_ref[rows], dis_ref[rows]
            misfit = dis - square * inverse
            weighted = weight * misfit
            stress += lane_sums(weighted * misfit)
            if not last:
                following.append(moved(x[:, rows], sides, weighted * inverse, scale))
        sums.append(stress)
        if last:
            own = dot(jnp.concatenate(parts, axis=0), pick, (((1,), (0,)), ((), ())))
            own = sum(own[i * coord_dims : (i + 1) * coord_dims] for i in range(3))
            square = dot(left_side(own, split_bf16(own, 3)), right, TN)
            inverse = lax.rsqrt(square)
            weight = weight_ref[own_rows, :]
            push = weight * (dis_ref[own_rows, :] - square * inverse) * inverse
            out_ref[...] = moved(own, sides, push, inverse_weight(weight, ones))
        else:
            x = jnp.concatenate(following, axis=1)
    total = jnp.sum(jnp.concatenate(sums, axis=0), axis=1, keepdims=True)
    ratios = total[1:] / total[:1]
    lanes = lax.broadcasted_iota(jnp.int32, (ITERS, LANES), 1)
    lined = jnp.where(lanes == lax.broadcasted_iota(jnp.int32, (ITERS, LANES), 0), ratios, 0.0)
    stress_ref[...] = jnp.sum(lined, axis=0, keepdims=True)[:, :ITERS]


def small_body(dissim, classes, coords):
    coord_dims, _, per_dev = coords.shape
    points = dissim.shape[2]
    devices = points // per_dev
    vmem = pl.BlockSpec(memory_space=pltpu.VMEM)
    hbm = pl.BlockSpec(memory_space=pltpu.HBM)
    f32 = functools.partial(jax.ShapeDtypeStruct, dtype=jnp.float32)
    params = pltpu.CompilerParams(vmem_limit_bytes=16 << 20)

    def swap(value, offset):
        return lax.ppermute(value, "wide", [(i, i ^ offset) for i in range(devices)])

    tiles = 2 * len(tile_spots(per_dev, points)) + 1
    inputs = (dissim[0], classes[0], coords[:, 0, :])
    packed = pl.pallas_call(
        pack_kernel,
        out_shape=f32((tiles, SUBLANES, LANES)),
        in_specs=[hbm] * 3,
        out_specs=vmem,
        scratch_shapes=[
            pltpu.VMEM((per_dev, points), jnp.float32),
            pltpu.VMEM((per_dev, points), jnp.int32),
            pltpu.VMEM((coord_dims, per_dev), jnp.float32),
            pltpu.SemaphoreType.DMA((3,)),
        ],
        compiler_params=params,
        name="pack",
    )(*(pltpu.with_memory_space_constraint(array, pltpu.HBM) for array in inputs))
    far, near, side = devices // 2, devices // 4, devices // 8
    held = {0: packed}
    for offset in (far, side, near, far | near | side, near | side):
        held[offset] = swap(packed, offset)
    for step in (side, near):
        held[far | step] = swap(held[far], step)
    offsets = list(held)
    mine = jnp.concatenate(list(held.values()), axis=0)
    theirs = swap(mine, 1)
    final, stress = pl.pallas_call(
        functools.partial(group_kernel, offsets, per_dev),
        out_shape=(f32((coord_dims, per_dev)), f32((1, ITERS))),
        in_specs=[vmem, vmem],
        out_specs=(vmem, vmem),
        scratch_shapes=[
            pltpu.VMEM((points, points), jnp.float32),
            pltpu.VMEM((points, points), jnp.float32),
            pltpu.VMEM((devices, SUBLANES, LANES), jnp.float32),
        ],
        compiler_params=params,
        name="group_smacof",
    )(mine, theirs)
    return (final[:, None, :], stress[0])


def distributed_body(dissim, classes, coords):
    halves = dissim.shape[0]
    per_dev = dissim.shape[1]
    columns = dissim.shape[2]
    coord_dims = coords.shape[0]
    row_count = halves * per_dev
    dis_tile = dissim.reshape(row_count, columns)
    weight = class_weight(classes.reshape(row_count, columns))
    denom_local = jnp.sum(weight * dis_tile * dis_tile)
    half_index = lax.axis_index("narrow")
    denom_total = lax.psum(denom_local, ("wide", "narrow"))
    positions = coords
    numbers = []
    for sweep in range(ITERS):
        row_points = lax.all_gather(positions, "narrow", axis=1, tiled=True)
        row_x = row_points.reshape(coord_dims, row_count)
        row_sq = jnp.sum(row_x * row_x, axis=0)
        fold_column_x = lax.dynamic_index_in_dim(
            lax.all_gather(row_points, "wide", axis=2, tiled=True), half_index, 1, keepdims=False
        )
        inner_prod = lax.dot_general(
            row_x,
            fold_column_x,
            (((0,), (0,)), ((), ())),
            precision=lax.Precision.HIGHEST,
            preferred_element_type=jnp.float32,
        )
        col_sq = jnp.sum(fold_column_x * fold_column_x, axis=0)
        distance = jnp.sqrt(row_sq[:, None] + col_sq[None, :] - 2.0 * inner_prod + 1.0)
        ratios = weight * dis_tile / distance
        pull_term = lax.dot_general(
            weight - ratios,
            fold_column_x,
            (((1,), (1,)), ((), ())),
            precision=lax.Precision.HIGHEST,
            preferred_element_type=jnp.float32,
        )
        misfit = dis_tile - distance
        pull_sums = pull_term.reshape(halves, per_dev, coord_dims).transpose(0, 2, 1)
        weight_sum, ratio_sum, pull_share = (
            lax.psum_scatter(
                jnp.sum(weight, axis=1).reshape(halves, per_dev),
                "narrow",
                scatter_dimension=0,
                tiled=True,
            ),
            lax.psum_scatter(
                jnp.sum(ratios, axis=1).reshape(halves, per_dev),
                "narrow",
                scatter_dimension=0,
                tiled=True,
            ),
            lax.psum_scatter(pull_sums, "narrow", scatter_dimension=0, tiled=True),
        )
        own_coords = positions[:, 0, :]
        updated = (own_coords * (1.0 + ratio_sum[0]) + pull_share[0]) / (1.0 + weight_sum[0])
        positions = updated[:, None, :]
        numbers.append(
            lax.psum(jnp.sum(weight * misfit * misfit), ("wide", "narrow")) / denom_total
        )
    stress = jnp.stack(numbers)
    return (positions, stress)


def solution(mesh):
    def body(dissim, classes, coords):
        coord_dims, halves, per_dev = coords.shape
        points, devices = dissim.shape[2], mesh.shape["wide"]
        small = halves == 1 and mesh.shape["narrow"] == 1 and points * points <= MOST_PAIRS
        small = small and coord_dims == 2 * SUBLANES and 2 * per_dev <= LANES
        small = small and per_dev % SUBLANES == 0 and points % LANES == 0
        small = small and devices == 16
        return (small_body if small else distributed_body)(dissim, classes, coords)

    return jax.shard_map(
        body,
        mesh=mesh,
        in_specs=(
            P(None, ("grp", "wide"), "narrow"),
            P(None, ("grp", "wide"), "narrow"),
            P(None, "narrow", ("grp", "wide")),
        ),
        out_specs=(P(None, "narrow", ("grp", "wide")), P("grp")),
        check_vma=False,
    )
```

```python
import functools

import jax
import jax.numpy as jnp
from jax import lax
from jax.experimental import pallas as pl
from jax.experimental.pallas import tpu as pltpu
from jax.sharding import PartitionSpec as P

ITERS = 3
LANES = 128
MOST_PAIRS = 1 << 19


def class_weight(class_codes):
    return jnp.where(
        class_codes == 3,
        1.0,
        jnp.where(class_codes == 2, 0.5, jnp.where(class_codes == 1, 0.25, 0.0)),
    ).astype(jnp.float32)


def split_bf16(value, terms):
    parts = []
    for _ in range(terms):
        part = value.astype(jnp.bfloat16)
        parts.append(part)
        value = value - part.astype(jnp.float32)
    return parts


SUBLANES = 8
NT = (((1,), (1,)), ((), ()))
TN = (((0,), (0,)), ((), ()))
dot = functools.partial(lax.dot_general, preferred_element_type=jnp.float32)


def lane_sums(value):
    rows = jnp.sum(value, axis=0, keepdims=True)
    return sum(rows[:, i : i + LANES] for i in range(0, rows.shape[1], LANES))


def tile_spots(per_dev, points):
    return [
        (slice(row, row + SUBLANES), slice(column, column + LANES))
        for row in range(0, per_dev, SUBLANES)
        for column in range(0, points, LANES)
    ]


def pack_kernel(dis_hbm, cls_hbm, x_hbm, out_ref, dis_ref, cls_ref, x_ref, sems):
    copies = [
        pltpu.make_async_copy(src, dst, sems.at[i])
        for i, (src, dst) in enumerate(
            [(dis_hbm, dis_ref), (cls_hbm, cls_ref), (x_hbm, x_ref)]
        )
    ]
    for copy in copies:
        copy.start()
    for copy in copies:
        copy.wait()
    spots = tile_spots(*dis_ref.shape)
    for i, spot in enumerate(spots):
        out_ref[i] = dis_ref[spot]
        out_ref[len(spots) + i] = class_weight(cls_ref[spot])
    half, per_dev = x_ref.shape[0] // 2, x_ref.shape[1]
    pad = jnp.zeros((half, LANES - 2 * per_dev), jnp.float32)
    out_ref[2 * len(spots)] = jnp.concatenate([x_ref[:half], x_ref[half:], pad], axis=1)


def norm_rows(top, bottom, coord_dims):
    pad = jnp.zeros((coord_dims - 6, top[0].shape[1]), jnp.float32)
    rows = [p.astype(jnp.float32) for p in (*top, *bottom)]
    return jnp.concatenate([*rows, pad], axis=0).astype(jnp.bfloat16)


def left_side(x, parts):
    hi, mid, lo = (-2.0 * p for p in parts)
    norm = split_bf16(jnp.sum(x * x, axis=0, keepdims=True), 3)
    ones = [jnp.ones((3, x.shape[1]), jnp.bfloat16)]
    return jnp.concatenate([hi, hi, hi, mid, mid, lo, norm_rows(norm, ones, x.shape[0])], axis=0)


def right_side(x, parts):
    hi, mid, lo = parts
    norm = split_bf16(jnp.sum(x * x, axis=0, keepdims=True) + 1.0, 3)
    ones = [jnp.ones((3, x.shape[1]), jnp.bfloat16)]
    return jnp.concatenate([hi, mid, lo, hi, mid, hi, norm_rows(ones, norm, x.shape[0])], axis=0)


def inverse_weight(weight, ones):
    return 1.0 / (1.0 + dot(weight.astype(jnp.bfloat16), ones, NT).T[0:1])


def moved(x, sides, push, scale):
    coord_dims = x.shape[0]
    parts = jnp.concatenate(split_bf16(push, 2), axis=1)
    sums = dot(parts, jnp.concatenate([sides, sides], axis=1), NT).T
    pushed = sums[:coord_dims] + sums[coord_dims : 2 * coord_dims]
    return x + (x * sums[2 * coord_dims : 2 * coord_dims + 1] - pushed) * scale


def place_of(offset, bit):
    return lax.axis_index("wide") ^ offset ^ bit


def sweep_rows(x, dis, weight, square, sides, scale):
    inverse = lax.rsqrt(square)
    misfit = dis - square * inverse
    weighted = weight * misfit
    return lane_sums(weighted * misfit), moved(x, sides, weighted * inverse, scale)


def sides_of(parts, points):
    ones = jnp.ones((parts[0].shape[0], points), jnp.bfloat16)
    return jnp.concatenate([parts[0], parts[1], ones], axis=0), ones


def row_chunks(count):
    return [slice(row, min(row + LANES, count)) for row in range(0, count, LANES)]


def from_tiles(tiles, per_dev):
    halves = [
        jnp.concatenate([t[:, low : low + per_dev] for t in tiles], axis=1) for low in (0, per_dev)
    ]
    return jnp.concatenate(halves, axis=0)


def static_rows(ref, per_dev, dis_ref, weight_ref):
    spots = tile_spots(per_dev, dis_ref.shape[1])
    tiles = 2 * len(spots) + 1
    for slot in range(ref.shape[0] // tiles):
        for i, (rows, columns) in enumerate(spots):
            spot = slice(slot * per_dev + rows.start, slot * per_dev + rows.stop)
            dis_ref[spot, columns] = ref[slot * tiles + i]
            weight_ref[spot, columns] = ref[slot * tiles + len(spots) + i]


def first_kernel(offsets, per_dev, mine_ref, tiles_ref, their_tiles_ref, x_ref, moved_ref, rest_ref,
                 inverse_ref, distance_ref, stress_ref, order_ref,
                 dis_ref, weight_ref, tile_ref):
    held, points = dis_ref.shape
    order = []
    shape = (per_dev, points)
    lanes = lax.broadcasted_iota(jnp.int32, shape, 1) - lax.broadcasted_iota(jnp.int32, shape, 0)
    for bit, ref in enumerate((tiles_ref, their_tiles_ref)):
        for slot, offset in enumerate(offsets):
            place = place_of(offset, bit)
            tile_ref[place] = ref[slot]
            order.append((lanes == place * per_dev).astype(jnp.float32))
    order_ref[...] = jnp.concatenate(order, axis=0).astype(jnp.bfloat16)
    static_rows(mine_ref, per_dev, dis_ref, weight_ref)
    mine = from_tiles([tiles_ref[i] for i in range(len(offsets))], per_dev)
    rest = from_tiles([their_tiles_ref[i] for i in range(len(offsets))], per_dev)
    x = from_tiles([tile_ref[i] for i in range(tile_ref.shape[0])], per_dev)
    x_ref[...] = x
    rest_ref[...] = rest
    parts = split_bf16(x, 3)
    sides, ones = sides_of(parts, points)
    right = right_side(x, parts)
    left = left_side(mine, split_bf16(mine, 3))
    rest_left = left_side(rest, split_bf16(rest, 3))
    stress, following = 0.0, []
    for rows in row_chunks(held):
        weight = weight_ref[rows]
        part, new = sweep_rows(
            mine[:, rows], dis_ref[rows], weight, dot(left[:, rows], right, TN), sides,
            inverse_weight(weight, ones),
        )
        stress += part
        following.append(new)
    moved_ref[...] = jnp.concatenate(following, axis=1)
    stress_ref[...] = stress
    for rows in row_chunks(held):
        square = dot(rest_left[:, rows], right, TN)
        inverse = lax.rsqrt(square)
        inverse_ref[rows] = inverse
        distance_ref[rows] = square * inverse


def second_kernel(offsets, per_dev, mine_ref, theirs_ref, x_ref, moved_ref, rest_ref, inverse_ref,
                  distance_ref, first_ref, order_ref, out_ref, stress_ref,
                  dis_ref, weight_ref, rest_dis_ref, rest_weight_ref, push_ref):
    held, points = rest_dis_ref.shape
    coord_dims = x_ref.shape[0]
    static_rows(theirs_ref, per_dev, rest_dis_ref, rest_weight_ref)
    sides, ones = sides_of(split_bf16(x_ref[...], 2), points)
    stress, following = first_ref[...], [moved_ref[...]]
    for rows in row_chunks(held):
        weight = rest_weight_ref[rows]
        misfit = rest_dis_ref[rows] - distance_ref[rows]
        weighted = weight * misfit
        stress += lane_sums(weighted * misfit)
        push = weighted * inverse_ref[rows]
        following.append(moved(rest_ref[:, rows], sides, push, inverse_weight(weight, ones)))
    sums = [stress]
    slots = jnp.concatenate(following, axis=1)
    spots = tile_spots(per_dev, points)
    tiles = 2 * len(spots) + 1
    for bit, ref in enumerate((mine_ref, theirs_ref)):
        for slot, offset in enumerate(offsets):
            for i, (rows, columns) in enumerate(spots):
                start = place_of(offset, bit) * per_dev + rows.start
                spot = pl.ds(pl.multiple_of(start, SUBLANES), SUBLANES)
                dis_ref[spot, columns] = ref[slot * tiles + i]
                weight_ref[spot, columns] = ref[slot * tiles + len(spots) + i]
    chunks = row_chunks(points)
    scales = [inverse_weight(weight_ref[rows], ones) for rows in chunks]
    denom = sum(lane_sums(weight_ref[rows] * dis_ref[rows] * dis_ref[rows]) for rows in chunks)
    ordered = dot(jnp.concatenate(split_bf16(slots, 3), axis=0), order_ref[...], (((1,), (0,)), ((), ())))
    parts = [ordered[i * coord_dims : (i + 1) * coord_dims] for i in range(3)]
    x = sum(parts)
    parts = [p.astype(jnp.bfloat16) for p in parts]
    for sweep in range(1, ITERS):
        last = sweep == ITERS - 1
        sides, _ = sides_of(parts, points)
        left, right = left_side(x, parts), right_side(x, parts)
        stress, following = 0.0, []
        for rows, scale in zip(chunks, scales):
            square = dot(left[:, rows], right, TN)
            if last:
                inverse = lax.rsqrt(square)
                misfit = dis_ref[rows] - square * inverse
                weighted = weight_ref[rows] * misfit
                stress += lane_sums(weighted * misfit)
                push_ref[rows] = weighted * inverse
            else:
                part, new = sweep_rows(
                    x[:, rows], dis_ref[rows], weight_ref[rows], square, sides, scale
                )
                stress += part
                following.append(new)
        sums.append(stress)
        if not last:
            x = jnp.concatenate(following, axis=1)
            parts = split_bf16(x, 3)
    place = lax.axis_index("wide")
    shape = (points, per_dev)
    pick = lax.broadcasted_iota(jnp.int32, shape, 0) - lax.broadcasted_iota(jnp.int32, shape, 1)
    pick = (pick == place * per_dev).astype(jnp.float32).astype(jnp.bfloat16)
    own = dot(jnp.concatenate(parts, axis=0), pick, (((1,), (0,)), ((), ())))
    own = sum(own[i * coord_dims : (i + 1) * coord_dims] for i in range(3))
    own_rows = pl.ds(pl.multiple_of(place * per_dev, SUBLANES), per_dev)
    scale = inverse_weight(weight_ref[own_rows, :], ones)
    out_ref[...] = moved(own, sides, push_ref[own_rows, :], scale)
    total = jnp.sum(jnp.concatenate([*sums, denom], axis=0), axis=1, keepdims=True)
    ratios = total[:ITERS] / total[ITERS:]
    lanes = lax.broadcasted_iota(jnp.int32, (ITERS, LANES), 1)
    lined = jnp.where(lanes == lax.broadcasted_iota(jnp.int32, (ITERS, LANES), 0), ratios, 0.0)
    stress_ref[...] = jnp.sum(lined, axis=0, keepdims=True)[:, :ITERS]


def small_body(dissim, classes, coords):
    coord_dims, _, per_dev = coords.shape
    points = dissim.shape[2]
    devices = points // per_dev
    vmem = pl.BlockSpec(memory_space=pltpu.VMEM)
    hbm = pl.BlockSpec(memory_space=pltpu.HBM)
    f32 = functools.partial(jax.ShapeDtypeStruct, dtype=jnp.float32)
    params = pltpu.CompilerParams(vmem_limit_bytes=16 << 20)

    def swap(value, offset):
        return lax.ppermute(value, "wide", [(i, i ^ offset) for i in range(devices)])

    tiles = 2 * len(tile_spots(per_dev, points)) + 1
    inputs = (dissim[0], classes[0], coords[:, 0, :])
    packed = pl.pallas_call(
        pack_kernel,
        out_shape=f32((tiles, SUBLANES, LANES)),
        in_specs=[hbm] * 3,
        out_specs=vmem,
        scratch_shapes=[
            pltpu.VMEM((per_dev, points), jnp.float32),
            pltpu.VMEM((per_dev, points), jnp.int32),
            pltpu.VMEM((coord_dims, per_dev), jnp.float32),
            pltpu.SemaphoreType.DMA((3,)),
        ],
        compiler_params=params,
        name="pack",
    )(*(pltpu.with_memory_space_constraint(array, pltpu.HBM) for array in inputs))
    far, near, side = devices // 2, devices // 4, devices // 8
    held = {0: packed}
    for offset in (far, side, near, far | near | side, near | side):
        held[offset] = swap(packed, offset)
    for step in (side, near):
        held[far | step] = swap(held[far], step)
    offsets = list(held)
    mine = jnp.concatenate(list(held.values()), axis=0)
    mine_tiles = jnp.stack([block[-1] for block in held.values()])
    their_tiles = swap(mine_tiles, 1)
    theirs = swap(mine, 1)
    rows = per_dev * len(offsets)
    shadow = pl.pallas_call(
        functools.partial(first_kernel, offsets, per_dev),
        out_shape=(
            f32((coord_dims, points)),
            f32((coord_dims, rows)),
            f32((coord_dims, rows)),
            f32((rows, points)),
            f32((rows, points)),
            f32((1, LANES)),
            jax.ShapeDtypeStruct((points, points), jnp.bfloat16),
        ),
        in_specs=[vmem] * 3,
        out_specs=(vmem,) * 7,
        scratch_shapes=[
            pltpu.VMEM((rows, points), jnp.float32),
            pltpu.VMEM((rows, points), jnp.float32),
            pltpu.VMEM((devices, SUBLANES, LANES), jnp.float32),
        ],
        compiler_params=params,
        cost_estimate=pl.CostEstimate(flops=10**7, bytes_accessed=0, transcendentals=0),
        name="first_sweep",
    )(mine, mine_tiles, their_tiles)
    final, stress = pl.pallas_call(
        functools.partial(second_kernel, offsets, per_dev),
        out_shape=(f32((coord_dims, per_dev)), f32((1, ITERS))),
        in_specs=[vmem] * 9,
        out_specs=(vmem, vmem),
        scratch_shapes=[
            pltpu.VMEM((points, points), jnp.float32),
            pltpu.VMEM((points, points), jnp.float32),
            pltpu.VMEM((rows, points), jnp.float32),
            pltpu.VMEM((rows, points), jnp.float32),
            pltpu.VMEM((points, points), jnp.float32),
        ],
        compiler_params=params,
        name="group_smacof",
    )(mine, theirs, *shadow)
    return (final[:, None, :], stress[0])


def distributed_body(dissim, classes, coords):
    halves = dissim.shape[0]
    per_dev = dissim.shape[1]
    columns = dissim.shape[2]
    coord_dims = coords.shape[0]
    row_count = halves * per_dev
    dis_tile = dissim.reshape(row_count, columns)
    weight = class_weight(classes.reshape(row_count, columns))
    denom_local = jnp.sum(weight * dis_tile * dis_tile)
    half_index = lax.axis_index("narrow")
    denom_total = lax.psum(denom_local, ("wide", "narrow"))
    positions = coords
    numbers = []
    for sweep in range(ITERS):
        row_points = lax.all_gather(positions, "narrow", axis=1, tiled=True)
        row_x = row_points.reshape(coord_dims, row_count)
        row_sq = jnp.sum(row_x * row_x, axis=0)
        fold_column_x = lax.dynamic_index_in_dim(
            lax.all_gather(row_points, "wide", axis=2, tiled=True), half_index, 1, keepdims=False
        )
        inner_prod = lax.dot_general(
            row_x,
            fold_column_x,
            (((0,), (0,)), ((), ())),
            precision=lax.Precision.HIGHEST,
            preferred_element_type=jnp.float32,
        )
        col_sq = jnp.sum(fold_column_x * fold_column_x, axis=0)
        distance = jnp.sqrt(row_sq[:, None] + col_sq[None, :] - 2.0 * inner_prod + 1.0)
        ratios = weight * dis_tile / distance
        pull_term = lax.dot_general(
            weight - ratios,
            fold_column_x,
            (((1,), (1,)), ((), ())),
            precision=lax.Precision.HIGHEST,
            preferred_element_type=jnp.float32,
        )
        misfit = dis_tile - distance
        pull_sums = pull_term.reshape(halves, per_dev, coord_dims).transpose(0, 2, 1)
        weight_sum, ratio_sum, pull_share = (
            lax.psum_scatter(
                jnp.sum(weight, axis=1).reshape(halves, per_dev),
                "narrow",
                scatter_dimension=0,
                tiled=True,
            ),
            lax.psum_scatter(
                jnp.sum(ratios, axis=1).reshape(halves, per_dev),
                "narrow",
                scatter_dimension=0,
                tiled=True,
            ),
            lax.psum_scatter(pull_sums, "narrow", scatter_dimension=0, tiled=True),
        )
        own_coords = positions[:, 0, :]
        updated = (own_coords * (1.0 + ratio_sum[0]) + pull_share[0]) / (1.0 + weight_sum[0])
        positions = updated[:, None, :]
        numbers.append(
            lax.psum(jnp.sum(weight * misfit * misfit), ("wide", "narrow")) / denom_total
        )
    stress = jnp.stack(numbers)
    return (positions, stress)


def solution(mesh):
    def body(dissim, classes, coords):
        coord_dims, halves, per_dev = coords.shape
        points, devices = dissim.shape[2], mesh.shape["wide"]
        small = halves == 1 and mesh.shape["narrow"] == 1 and points * points <= MOST_PAIRS
        small = small and coord_dims == 2 * SUBLANES and 2 * per_dev <= LANES
        small = small and per_dev % SUBLANES == 0 and points % LANES == 0
        small = small and devices == 16
        return (small_body if small else distributed_body)(dissim, classes, coords)

    return jax.shard_map(
        body,
        mesh=mesh,
        in_specs=(
            P(None, ("grp", "wide"), "narrow"),
            P(None, ("grp", "wide"), "narrow"),
            P(None, "narrow", ("grp", "wide")),
        ),
        out_specs=(P(None, "narrow", ("grp", "wide")), P("grp")),
        check_vma=False,
    )
```

```python
import functools

import jax
import jax.numpy as jnp
from jax import lax
from jax.experimental import pallas as pl
from jax.experimental.pallas import tpu as pltpu
from jax.sharding import PartitionSpec as P

ITERS = 3
LANES = 128
MOST_PAIRS = 1 << 19


def class_weight(class_codes):
    return jnp.where(
        class_codes == 3,
        1.0,
        jnp.where(class_codes == 2, 0.5, jnp.where(class_codes == 1, 0.25, 0.0)),
    ).astype(jnp.float32)


def split_bf16(value, terms):
    parts = []
    for _ in range(terms):
        part = value.astype(jnp.bfloat16)
        parts.append(part)
        value = value - part.astype(jnp.float32)
    return parts


SUBLANES = 8
NT = (((1,), (1,)), ((), ()))
TN = (((0,), (0,)), ((), ()))
dot = functools.partial(lax.dot_general, preferred_element_type=jnp.float32)


def lane_sums(value):
    rows = jnp.sum(value, axis=0, keepdims=True)
    return sum(rows[:, i : i + LANES] for i in range(0, rows.shape[1], LANES))


def tile_spots(per_dev, points):
    return [
        (slice(row, row + SUBLANES), slice(column, column + LANES))
        for row in range(0, per_dev, SUBLANES)
        for column in range(0, points, LANES)
    ]


def pack_kernel(dis_hbm, cls_hbm, x_hbm, out_ref, dis_ref, cls_ref, x_ref, sems):
    copies = [
        pltpu.make_async_copy(src, dst, sems.at[i])
        for i, (src, dst) in enumerate(
            [(dis_hbm, dis_ref), (cls_hbm, cls_ref), (x_hbm, x_ref)]
        )
    ]
    for copy in copies:
        copy.start()
    for copy in copies:
        copy.wait()
    spots = tile_spots(*dis_ref.shape)
    for i, spot in enumerate(spots):
        out_ref[i] = dis_ref[spot]
        out_ref[len(spots) + i] = class_weight(cls_ref[spot])
    half, per_dev = x_ref.shape[0] // 2, x_ref.shape[1]
    pad = jnp.zeros((half, LANES - 2 * per_dev), jnp.float32)
    out_ref[2 * len(spots)] = jnp.concatenate([x_ref[:half], x_ref[half:], pad], axis=1)


def held_slots(offsets, refs, tiles):
    me = lax.axis_index("wide")
    for group, ref in zip(offsets, refs):
        for slot, offset in enumerate(group):
            yield ref, slot * tiles, me ^ offset


def norm_rows(top, bottom, coord_dims):
    pad = jnp.zeros((coord_dims - 6, top[0].shape[1]), jnp.float32)
    rows = [p.astype(jnp.float32) for p in (*top, *bottom)]
    return jnp.concatenate([*rows, pad], axis=0).astype(jnp.bfloat16)


def left_side(x, parts):
    hi, mid, lo = (-2.0 * p for p in parts)
    norm = split_bf16(jnp.sum(x * x, axis=0, keepdims=True), 3)
    ones = [jnp.ones((3, x.shape[1]), jnp.bfloat16)]
    return jnp.concatenate([hi, hi, hi, mid, mid, lo, norm_rows(norm, ones, x.shape[0])], axis=0)


def right_side(x, parts):
    hi, mid, lo = parts
    norm = split_bf16(jnp.sum(x * x, axis=0, keepdims=True) + 1.0, 3)
    ones = [jnp.ones((3, x.shape[1]), jnp.bfloat16)]
    return jnp.concatenate([hi, mid, lo, hi, mid, hi, norm_rows(ones, norm, x.shape[0])], axis=0)


def inverse_weight(weight, ones):
    return 1.0 / (1.0 + dot(weight.astype(jnp.bfloat16), ones, NT).T[0:1])


def moved(x, sides, push, scale):
    coord_dims = x.shape[0]
    parts = jnp.concatenate(split_bf16(push, 2), axis=1)
    sums = dot(parts, jnp.concatenate([sides, sides], axis=1), NT).T
    pushed = sums[:coord_dims] + sums[coord_dims : 2 * coord_dims]
    return x + (x * sums[2 * coord_dims : 2 * coord_dims + 1] - pushed) * scale


def join_kernel(*refs):
    *block_refs, out_ref = refs
    size = block_refs[0].shape[0]
    for i, ref in enumerate(block_refs):
        out_ref[i * size : (i + 1) * size] = ref[...]


def group_kernel(offsets, per_dev, *refs):
    slot_refs = refs[: len(offsets)]
    out_ref, stress_ref, dis_ref, weight_ref, tile_ref = refs[len(offsets) :]
    points = dis_ref.shape[0]
    spots = tile_spots(per_dev, points)
    tiles = 2 * len(spots) + 1
    for ref, base, place in held_slots(offsets, slot_refs, tiles):
        tile_ref[place] = ref[base + tiles - 1]
        for i, (rows, columns) in enumerate(spots):
            start = pl.multiple_of(place * per_dev + rows.start, SUBLANES)
            dis_ref[pl.ds(start, SUBLANES), columns] = ref[base + i]
            weight_ref[pl.ds(start, SUBLANES), columns] = ref[base + len(spots) + i]
    blocks = [tile_ref[i] for i in range(tile_ref.shape[0])]
    halves = [
        jnp.concatenate([t[:, low : low + per_dev] for t in blocks], axis=1)
        for low in (0, per_dev)
    ]
    x = jnp.concatenate(halves, axis=0)
    coord_dims = x.shape[0]
    chunks = [slice(row, row + LANES) for row in range(0, points, LANES)]
    ones = jnp.ones((coord_dims, points), jnp.bfloat16)
    scales = [inverse_weight(weight_ref[rows], ones) for rows in chunks]
    denom = sum(lane_sums(weight_ref[rows] * dis_ref[rows] * dis_ref[rows]) for rows in chunks)
    place = lax.axis_index("wide")
    own_rows = pl.ds(pl.multiple_of(place * per_dev, SUBLANES), per_dev)
    shape = (points, per_dev)
    pick = lax.broadcasted_iota(jnp.int32, shape, 0) - lax.broadcasted_iota(jnp.int32, shape, 1)
    pick = (pick == place * per_dev).astype(jnp.float32).astype(jnp.bfloat16)
    sums = [denom]
    for sweep in range(ITERS):
        parts = split_bf16(x, 3)
        sides = jnp.concatenate([parts[0], parts[1], ones], axis=0)
        left, right = left_side(x, parts), right_side(x, parts)
        last = sweep == ITERS - 1
        stress, following = 0.0, []
        for rows, scale in zip(chunks, scales):
            square = dot(left[:, rows], right, TN)
            inverse = lax.rsqrt(square)
            weight, dis = weight_ref[rows], dis_ref[rows]
            misfit = dis - square * inverse
            weighted = weight * misfit
            stress += lane_sums(weighted * misfit)
            if not last:
                following.append(moved(x[:, rows], sides, weighted * inverse, scale))
        sums.append(stress)
        if last:
            own = dot(jnp.concatenate(parts, axis=0), pick, (((1,), (0,)), ((), ())))
            own = sum(own[i * coord_dims : (i + 1) * coord_dims] for i in range(3))
            square = dot(left_side(own, split_bf16(own, 3)), right, TN)
            inverse = lax.rsqrt(square)
            weight = weight_ref[own_rows, :]
            push = weight * (dis_ref[own_rows, :] - square * inverse) * inverse
            out_ref[...] = moved(own, sides, push, inverse_weight(weight, ones))
        else:
            x = jnp.concatenate(following, axis=1)
    total = jnp.sum(jnp.concatenate(sums, axis=0), axis=1, keepdims=True)
    ratios = total[1:] / total[:1]
    lanes = lax.broadcasted_iota(jnp.int32, (ITERS, LANES), 1)
    lined = jnp.where(lanes == lax.broadcasted_iota(jnp.int32, (ITERS, LANES), 0), ratios, 0.0)
    stress_ref[...] = jnp.sum(lined, axis=0, keepdims=True)[:, :ITERS]


def small_body(dissim, classes, coords):
    coord_dims, _, per_dev = coords.shape
    points = dissim.shape[2]
    devices = points // per_dev
    vmem = pl.BlockSpec(memory_space=pltpu.VMEM)
    hbm = pl.BlockSpec(memory_space=pltpu.HBM)
    f32 = functools.partial(jax.ShapeDtypeStruct, dtype=jnp.float32)
    params = pltpu.CompilerParams(vmem_limit_bytes=16 << 20)

    def swap(value, offset):
        return lax.ppermute(value, "wide", [(i, i ^ offset) for i in range(devices)])

    tiles = 2 * len(tile_spots(per_dev, points)) + 1
    inputs = (dissim[0], classes[0], coords[:, 0, :])
    packed = pl.pallas_call(
        pack_kernel,
        out_shape=f32((tiles, SUBLANES, LANES)),
        in_specs=[hbm] * 3,
        out_specs=vmem,
        scratch_shapes=[
            pltpu.VMEM((per_dev, points), jnp.float32),
            pltpu.VMEM((per_dev, points), jnp.int32),
            pltpu.VMEM((coord_dims, per_dev), jnp.float32),
            pltpu.SemaphoreType.DMA((3,)),
        ],
        compiler_params=params,
        name="pack",
    )(*(pltpu.with_memory_space_constraint(array, pltpu.HBM) for array in inputs))
    far, near, side = devices // 2, devices // 4, devices // 8
    held = {0: packed}
    for offset in (far, side, near, near | side, far | near | side):
        held[offset] = swap(packed, offset)
    for step in (near, side):
        held[far | step] = swap(held[far], step)
    early = [0, far, near, side]
    late = [offset for offset in held if offset not in early]
    block = packed.shape[0]

    def join(group, flops):
        return pl.pallas_call(
            join_kernel,
            out_shape=f32((len(group) * block, SUBLANES, LANES)),
            in_specs=[vmem] * len(group),
            out_specs=vmem,
            compiler_params=params,
            cost_estimate=pl.CostEstimate(flops=flops, bytes_accessed=0, transcendentals=0),
            name="join",
        )(*(held[offset] for offset in group))

    first, second = join(early, 1), join(late, 1)
    first_swapped = swap(first, 1)

    slots = [first, first_swapped, second, swap(second, 1)]
    offsets = [early, [o ^ 1 for o in early], late, [o ^ 1 for o in late]]
    final, stress = pl.pallas_call(
        functools.partial(group_kernel, offsets, per_dev),
        out_shape=(f32((coord_dims, per_dev)), f32((1, ITERS))),
        in_specs=[vmem] * len(slots),
        out_specs=(vmem, vmem),
        scratch_shapes=[
            pltpu.VMEM((points, points), jnp.float32),
            pltpu.VMEM((points, points), jnp.float32),
            pltpu.VMEM((devices, SUBLANES, LANES), jnp.float32),
        ],
        compiler_params=params,
        name="group_smacof",
    )(*slots)
    return (final[:, None, :], stress[0])


def distributed_body(dissim, classes, coords):
    halves = dissim.shape[0]
    per_dev = dissim.shape[1]
    columns = dissim.shape[2]
    coord_dims = coords.shape[0]
    row_count = halves * per_dev
    dis_tile = dissim.reshape(row_count, columns)
    weight = class_weight(classes.reshape(row_count, columns))
    denom_local = jnp.sum(weight * dis_tile * dis_tile)
    half_index = lax.axis_index("narrow")
    denom_total = lax.psum(denom_local, ("wide", "narrow"))
    positions = coords
    numbers = []
    for sweep in range(ITERS):
        row_points = lax.all_gather(positions, "narrow", axis=1, tiled=True)
        row_x = row_points.reshape(coord_dims, row_count)
        row_sq = jnp.sum(row_x * row_x, axis=0)
        fold_column_x = lax.dynamic_index_in_dim(
            lax.all_gather(row_points, "wide", axis=2, tiled=True), half_index, 1, keepdims=False
        )
        inner_prod = lax.dot_general(
            row_x,
            fold_column_x,
            (((0,), (0,)), ((), ())),
            precision=lax.Precision.HIGHEST,
            preferred_element_type=jnp.float32,
        )
        col_sq = jnp.sum(fold_column_x * fold_column_x, axis=0)
        distance = jnp.sqrt(row_sq[:, None] + col_sq[None, :] - 2.0 * inner_prod + 1.0)
        ratios = weight * dis_tile / distance
        pull_term = lax.dot_general(
            weight - ratios,
            fold_column_x,
            (((1,), (1,)), ((), ())),
            precision=lax.Precision.HIGHEST,
            preferred_element_type=jnp.float32,
        )
        misfit = dis_tile - distance
        pull_sums = pull_term.reshape(halves, per_dev, coord_dims).transpose(0, 2, 1)
        weight_sum, ratio_sum, pull_share = (
            lax.psum_scatter(
                jnp.sum(weight, axis=1).reshape(halves, per_dev),
                "narrow",
                scatter_dimension=0,
                tiled=True,
            ),
            lax.psum_scatter(
                jnp.sum(ratios, axis=1).reshape(halves, per_dev),
                "narrow",
                scatter_dimension=0,
                tiled=True,
            ),
            lax.psum_scatter(pull_sums, "narrow", scatter_dimension=0, tiled=True),
        )
        own_coords = positions[:, 0, :]
        updated = (own_coords * (1.0 + ratio_sum[0]) + pull_share[0]) / (1.0 + weight_sum[0])
        positions = updated[:, None, :]
        numbers.append(
            lax.psum(jnp.sum(weight * misfit * misfit), ("wide", "narrow")) / denom_total
        )
    stress = jnp.stack(numbers)
    return (positions, stress)


def solution(mesh):
    def body(dissim, classes, coords):
        coord_dims, halves, per_dev = coords.shape
        points, devices = dissim.shape[2], mesh.shape["wide"]
        small = halves == 1 and mesh.shape["narrow"] == 1 and points * points <= MOST_PAIRS
        small = small and coord_dims == 2 * SUBLANES and 2 * per_dev <= LANES
        small = small and per_dev % SUBLANES == 0 and points % LANES == 0
        small = small and devices == 16
        return (small_body if small else distributed_body)(dissim, classes, coords)

    return jax.shard_map(
        body,
        mesh=mesh,
        in_specs=(
            P(None, ("grp", "wide"), "narrow"),
            P(None, ("grp", "wide"), "narrow"),
            P(None, "narrow", ("grp", "wide")),
        ),
        out_specs=(P(None, "narrow", ("grp", "wide")), P("grp")),
        check_vma=False,
    )
```

```python
import functools

import jax
import jax.numpy as jnp
from jax import lax
from jax.experimental import pallas as pl
from jax.experimental.pallas import tpu as pltpu
from jax.sharding import PartitionSpec as P

ITERS = 3
LANES = 128
MOST_PAIRS = 1 << 19


def class_weight(class_codes):
    return jnp.where(
        class_codes == 3,
        1.0,
        jnp.where(class_codes == 2, 0.5, jnp.where(class_codes == 1, 0.25, 0.0)),
    ).astype(jnp.float32)


def split_bf16(value, terms):
    parts = []
    for _ in range(terms):
        part = value.astype(jnp.bfloat16)
        parts.append(part)
        value = value - part.astype(jnp.float32)
    return parts


SUBLANES = 8
NT = (((1,), (1,)), ((), ()))
TN = (((0,), (0,)), ((), ()))
dot = functools.partial(lax.dot_general, preferred_element_type=jnp.float32)


def lane_sums(value):
    rows = jnp.sum(value, axis=0, keepdims=True)
    return sum(rows[:, i : i + LANES] for i in range(0, rows.shape[1], LANES))


def tile_spots(per_dev, points):
    return [
        (slice(row, row + SUBLANES), slice(column, column + LANES))
        for row in range(0, per_dev, SUBLANES)
        for column in range(0, points, LANES)
    ]


def pack_kernel(dis_hbm, cls_hbm, x_hbm, out_ref, dis_ref, cls_ref, x_ref, sems):
    copies = [
        pltpu.make_async_copy(src, dst, sems.at[i])
        for i, (src, dst) in enumerate(
            [(dis_hbm, dis_ref), (cls_hbm, cls_ref), (x_hbm, x_ref)]
        )
    ]
    for copy in copies:
        copy.start()
    for copy in copies:
        copy.wait()
    spots = tile_spots(*dis_ref.shape)
    for i, spot in enumerate(spots):
        out_ref[i] = dis_ref[spot]
        out_ref[len(spots) + i] = class_weight(cls_ref[spot])
    half, per_dev = x_ref.shape[0] // 2, x_ref.shape[1]
    pad = jnp.zeros((half, LANES - 2 * per_dev), jnp.float32)
    out_ref[2 * len(spots)] = jnp.concatenate([x_ref[:half], x_ref[half:], pad], axis=1)


def held_slots(offsets, refs, tiles):
    me = lax.axis_index("wide")
    for group, ref in zip(offsets, refs):
        for slot, offset in enumerate(group):
            yield ref, slot * tiles, me ^ offset


def norm_rows(top, bottom, coord_dims):
    pad = jnp.zeros((coord_dims - 6, top[0].shape[1]), jnp.float32)
    rows = [p.astype(jnp.float32) for p in (*top, *bottom)]
    return jnp.concatenate([*rows, pad], axis=0).astype(jnp.bfloat16)


def left_side(x, parts):
    hi, mid, lo = (-2.0 * p for p in parts)
    norm = split_bf16(jnp.sum(x * x, axis=0, keepdims=True), 3)
    ones = [jnp.ones((3, x.shape[1]), jnp.bfloat16)]
    return jnp.concatenate([hi, hi, hi, mid, mid, lo, norm_rows(norm, ones, x.shape[0])], axis=0)


def right_side(x, parts):
    hi, mid, lo = parts
    norm = split_bf16(jnp.sum(x * x, axis=0, keepdims=True) + 1.0, 3)
    ones = [jnp.ones((3, x.shape[1]), jnp.bfloat16)]
    return jnp.concatenate([hi, mid, lo, hi, mid, hi, norm_rows(ones, norm, x.shape[0])], axis=0)


def inverse_weight(weight, ones):
    return 1.0 / (1.0 + dot(weight.astype(jnp.bfloat16), ones, NT).T[0:1])


def moved(x, sides, push, scale):
    coord_dims = x.shape[0]
    parts = jnp.concatenate(split_bf16(push, 2), axis=1)
    sums = dot(parts, jnp.concatenate([sides, sides], axis=1), NT).T
    pushed = sums[:coord_dims] + sums[coord_dims : 2 * coord_dims]
    return x + (x * sums[2 * coord_dims : 2 * coord_dims + 1] - pushed) * scale


def join_kernel(*refs):
    *block_refs, out_ref = refs
    size = block_refs[0].shape[0]
    for i, ref in enumerate(block_refs):
        out_ref[i * size : (i + 1) * size] = ref[...]


def group_kernel(offsets, per_dev, *refs):
    slot_refs = refs[: len(offsets)]
    out_ref, stress_ref, dis_ref, weight_ref, tile_ref = refs[len(offsets) :]
    points = dis_ref.shape[0]
    spots = tile_spots(per_dev, points)
    tiles = 2 * len(spots) + 1
    for ref, base, place in held_slots(offsets, slot_refs, tiles):
        tile_ref[place] = ref[base + tiles - 1]
        for i, (rows, columns) in enumerate(spots):
            start = pl.multiple_of(place * per_dev + rows.start, SUBLANES)
            dis_ref[pl.ds(start, SUBLANES), columns] = ref[base + i]
            weight_ref[pl.ds(start, SUBLANES), columns] = ref[base + len(spots) + i]
    blocks = [tile_ref[i] for i in range(tile_ref.shape[0])]
    halves = [
        jnp.concatenate([t[:, low : low + per_dev] for t in blocks], axis=1)
        for low in (0, per_dev)
    ]
    x = jnp.concatenate(halves, axis=0)
    coord_dims = x.shape[0]
    chunks = [slice(row, row + LANES) for row in range(0, points, LANES)]
    ones = jnp.ones((coord_dims, points), jnp.bfloat16)
    scales = [inverse_weight(weight_ref[rows], ones) for rows in chunks]
    denom = sum(lane_sums(weight_ref[rows] * dis_ref[rows] * dis_ref[rows]) for rows in chunks)
    place = lax.axis_index("wide")
    own_rows = pl.ds(pl.multiple_of(place * per_dev, SUBLANES), per_dev)
    shape = (points, per_dev)
    pick = lax.broadcasted_iota(jnp.int32, shape, 0) - lax.broadcasted_iota(jnp.int32, shape, 1)
    pick = (pick == place * per_dev).astype(jnp.float32).astype(jnp.bfloat16)
    sums = [denom]
    for sweep in range(ITERS):
        parts = split_bf16(x, 3)
        sides = jnp.concatenate([parts[0], parts[1], ones], axis=0)
        left, right = left_side(x, parts), right_side(x, parts)
        last = sweep == ITERS - 1
        stress, following = 0.0, []
        for rows, scale in zip(chunks, scales):
            square = dot(left[:, rows], right, TN)
            inverse = lax.rsqrt(square)
            weight, dis = weight_ref[rows], dis_ref[rows]
            misfit = dis - square * inverse
            weighted = weight * misfit
            stress += lane_sums(weighted * misfit)
            if not last:
                following.append(moved(x[:, rows], sides, weighted * inverse, scale))
        sums.append(stress)
        if last:
            own = dot(jnp.concatenate(parts, axis=0), pick, (((1,), (0,)), ((), ())))
            own = sum(own[i * coord_dims : (i + 1) * coord_dims] for i in range(3))
            square = dot(left_side(own, split_bf16(own, 3)), right, TN)
            inverse = lax.rsqrt(square)
            weight = weight_ref[own_rows, :]
            push = weight * (dis_ref[own_rows, :] - square * inverse) * inverse
            out_ref[...] = moved(own, sides, push, inverse_weight(weight, ones))
        else:
            x = jnp.concatenate(following, axis=1)
    total = jnp.sum(jnp.concatenate(sums, axis=0), axis=1, keepdims=True)
    ratios = total[1:] / total[:1]
    lanes = lax.broadcasted_iota(jnp.int32, (ITERS, LANES), 1)
    lined = jnp.where(lanes == lax.broadcasted_iota(jnp.int32, (ITERS, LANES), 0), ratios, 0.0)
    stress_ref[...] = jnp.sum(lined, axis=0, keepdims=True)[:, :ITERS]


def small_body(dissim, classes, coords):
    coord_dims, _, per_dev = coords.shape
    points = dissim.shape[2]
    devices = points // per_dev
    vmem = pl.BlockSpec(memory_space=pltpu.VMEM)
    hbm = pl.BlockSpec(memory_space=pltpu.HBM)
    f32 = functools.partial(jax.ShapeDtypeStruct, dtype=jnp.float32)
    params = pltpu.CompilerParams(vmem_limit_bytes=16 << 20)

    def swap(value, offset):
        return lax.ppermute(value, "wide", [(i, i ^ offset) for i in range(devices)])

    tiles = 2 * len(tile_spots(per_dev, points)) + 1
    inputs = (dissim[0], classes[0], coords[:, 0, :])
    packed = pl.pallas_call(
        pack_kernel,
        out_shape=f32((tiles, SUBLANES, LANES)),
        in_specs=[hbm] * 3,
        out_specs=vmem,
        scratch_shapes=[
            pltpu.VMEM((per_dev, points), jnp.float32),
            pltpu.VMEM((per_dev, points), jnp.int32),
            pltpu.VMEM((coord_dims, per_dev), jnp.float32),
            pltpu.SemaphoreType.DMA((3,)),
        ],
        compiler_params=params,
        name="pack",
    )(*(pltpu.with_memory_space_constraint(array, pltpu.HBM) for array in inputs))
    far, near, side = devices // 2, devices // 4, devices // 8
    cross = 1
    held = {0: packed}
    for offset in (far, side, near, near | side, far | near | side):
        held[offset | cross] = swap(packed, offset | cross)
    for step in (near, side):
        held[far | step] = swap(held[far | cross], step | cross)
    early = [0, far | cross, near | cross, side | cross]
    late = [offset for offset in held if offset not in early]
    block = packed.shape[0]

    def join(group, flops):
        return pl.pallas_call(
            join_kernel,
            out_shape=f32((len(group) * block, SUBLANES, LANES)),
            in_specs=[vmem] * len(group),
            out_specs=vmem,
            compiler_params=params,
            cost_estimate=pl.CostEstimate(flops=flops, bytes_accessed=0, transcendentals=0),
            name="join",
        )(*(held[offset] for offset in group))

    first, second = join(early, 1), join(late, 1)
    slots = [first, swap(first, 1), second, swap(second, 1)]
    offsets = [early, [o ^ 1 for o in early], late, [o ^ 1 for o in late]]
    final, stress = pl.pallas_call(
        functools.partial(group_kernel, offsets, per_dev),
        out_shape=(f32((coord_dims, per_dev)), f32((1, ITERS))),
        in_specs=[vmem] * len(slots),
        out_specs=(vmem, vmem),
        scratch_shapes=[
            pltpu.VMEM((points, points), jnp.float32),
            pltpu.VMEM((points, points), jnp.float32),
            pltpu.VMEM((devices, SUBLANES, LANES), jnp.float32),
        ],
        compiler_params=params,
        name="group_smacof",
    )(*slots)
    return (final[:, None, :], stress[0])


def distributed_body(dissim, classes, coords):
    halves = dissim.shape[0]
    per_dev = dissim.shape[1]
    columns = dissim.shape[2]
    coord_dims = coords.shape[0]
    row_count = halves * per_dev
    dis_tile = dissim.reshape(row_count, columns)
    weight = class_weight(classes.reshape(row_count, columns))
    denom_local = jnp.sum(weight * dis_tile * dis_tile)
    half_index = lax.axis_index("narrow")
    denom_total = lax.psum(denom_local, ("wide", "narrow"))
    positions = coords
    numbers = []
    for sweep in range(ITERS):
        row_points = lax.all_gather(positions, "narrow", axis=1, tiled=True)
        row_x = row_points.reshape(coord_dims, row_count)
        row_sq = jnp.sum(row_x * row_x, axis=0)
        fold_column_x = lax.dynamic_index_in_dim(
            lax.all_gather(row_points, "wide", axis=2, tiled=True), half_index, 1, keepdims=False
        )
        inner_prod = lax.dot_general(
            row_x,
            fold_column_x,
            (((0,), (0,)), ((), ())),
            precision=lax.Precision.HIGHEST,
            preferred_element_type=jnp.float32,
        )
        col_sq = jnp.sum(fold_column_x * fold_column_x, axis=0)
        distance = jnp.sqrt(row_sq[:, None] + col_sq[None, :] - 2.0 * inner_prod + 1.0)
        ratios = weight * dis_tile / distance
        pull_term = lax.dot_general(
            weight - ratios,
            fold_column_x,
            (((1,), (1,)), ((), ())),
            precision=lax.Precision.HIGHEST,
            preferred_element_type=jnp.float32,
        )
        misfit = dis_tile - distance
        pull_sums = pull_term.reshape(halves, per_dev, coord_dims).transpose(0, 2, 1)
        weight_sum, ratio_sum, pull_share = (
            lax.psum_scatter(
                jnp.sum(weight, axis=1).reshape(halves, per_dev),
                "narrow",
                scatter_dimension=0,
                tiled=True,
            ),
            lax.psum_scatter(
                jnp.sum(ratios, axis=1).reshape(halves, per_dev),
                "narrow",
                scatter_dimension=0,
                tiled=True,
            ),
            lax.psum_scatter(pull_sums, "narrow", scatter_dimension=0, tiled=True),
        )
        own_coords = positions[:, 0, :]
        updated = (own_coords * (1.0 + ratio_sum[0]) + pull_share[0]) / (1.0 + weight_sum[0])
        positions = updated[:, None, :]
        numbers.append(
            lax.psum(jnp.sum(weight * misfit * misfit), ("wide", "narrow")) / denom_total
        )
    stress = jnp.stack(numbers)
    return (positions, stress)


def solution(mesh):
    def body(dissim, classes, coords):
        coord_dims, halves, per_dev = coords.shape
        points, devices = dissim.shape[2], mesh.shape["wide"]
        small = halves == 1 and mesh.shape["narrow"] == 1 and points * points <= MOST_PAIRS
        small = small and coord_dims == 2 * SUBLANES and 2 * per_dev <= LANES
        small = small and per_dev % SUBLANES == 0 and points % LANES == 0
        small = small and devices == 16
        return (small_body if small else distributed_body)(dissim, classes, coords)

    return jax.shard_map(
        body,
        mesh=mesh,
        in_specs=(
            P(None, ("grp", "wide"), "narrow"),
            P(None, ("grp", "wide"), "narrow"),
            P(None, "narrow", ("grp", "wide")),
        ),
        out_specs=(P(None, "narrow", ("grp", "wide")), P("grp")),
        check_vma=False,
    )
```

```python
import functools

import jax
import jax.numpy as jnp
from jax import lax
from jax.experimental import pallas as pl
from jax.experimental.pallas import tpu as pltpu
from jax.sharding import PartitionSpec as P

ITERS = 3
LANES = 128
MOST_PAIRS = 1 << 19


def class_weight(class_codes):
    return jnp.where(
        class_codes == 3,
        1.0,
        jnp.where(class_codes == 2, 0.5, jnp.where(class_codes == 1, 0.25, 0.0)),
    ).astype(jnp.float32)


def split_bf16(value, terms):
    parts = []
    for _ in range(terms):
        part = value.astype(jnp.bfloat16)
        parts.append(part)
        value = value - part.astype(jnp.float32)
    return parts


SUBLANES = 8
NT = (((1,), (1,)), ((), ()))
TN = (((0,), (0,)), ((), ()))
dot = functools.partial(lax.dot_general, preferred_element_type=jnp.float32)


def lane_sums(value):
    rows = jnp.sum(value, axis=0, keepdims=True)
    return sum(rows[:, i : i + LANES] for i in range(0, rows.shape[1], LANES))


def tile_spots(per_dev, points):
    return [
        (slice(row, row + SUBLANES), slice(column, column + LANES))
        for row in range(0, per_dev, SUBLANES)
        for column in range(0, points, LANES)
    ]


def pack_kernel(dis_hbm, cls_hbm, x_hbm, out_ref, dis_ref, cls_ref, x_ref, sems):
    copies = [
        pltpu.make_async_copy(src, dst, sems.at[i])
        for i, (src, dst) in enumerate(
            [(dis_hbm, dis_ref), (cls_hbm, cls_ref), (x_hbm, x_ref)]
        )
    ]
    for copy in copies:
        copy.start()
    for copy in copies:
        copy.wait()
    spots = tile_spots(*dis_ref.shape)
    for i, spot in enumerate(spots):
        out_ref[i] = dis_ref[spot]
        out_ref[len(spots) + i] = class_weight(cls_ref[spot])
    half, per_dev = x_ref.shape[0] // 2, x_ref.shape[1]
    pad = jnp.zeros((half, LANES - 2 * per_dev), jnp.float32)
    out_ref[2 * len(spots)] = jnp.concatenate([x_ref[:half], x_ref[half:], pad], axis=1)


def held_slots(offsets, refs, tiles):
    me = lax.axis_index("wide")
    for group, ref in zip(offsets, refs):
        for slot, offset in enumerate(group):
            yield ref, slot * tiles, me ^ offset


def norm_rows(top, bottom, coord_dims):
    pad = jnp.zeros((coord_dims - 6, top[0].shape[1]), jnp.float32)
    rows = [p.astype(jnp.float32) for p in (*top, *bottom)]
    return jnp.concatenate([*rows, pad], axis=0).astype(jnp.bfloat16)


def left_side(x, parts):
    hi, mid, lo = (-2.0 * p for p in parts)
    norm = split_bf16(jnp.sum(x * x, axis=0, keepdims=True), 3)
    ones = [jnp.ones((3, x.shape[1]), jnp.bfloat16)]
    return jnp.concatenate([hi, hi, hi, mid, mid, lo, norm_rows(norm, ones, x.shape[0])], axis=0)


def right_side(x, parts):
    hi, mid, lo = parts
    norm = split_bf16(jnp.sum(x * x, axis=0, keepdims=True) + 1.0, 3)
    ones = [jnp.ones((3, x.shape[1]), jnp.bfloat16)]
    return jnp.concatenate([hi, mid, lo, hi, mid, hi, norm_rows(ones, norm, x.shape[0])], axis=0)


def inverse_weight(weight, ones):
    return 1.0 / (1.0 + dot(weight.astype(jnp.bfloat16), ones, NT).T[0:1])


def moved(x, sides, push, scale):
    coord_dims = x.shape[0]
    parts = jnp.concatenate(split_bf16(push, 2), axis=1)
    sums = dot(parts, jnp.concatenate([sides, sides], axis=1), NT).T
    pushed = sums[:coord_dims] + sums[coord_dims : 2 * coord_dims]
    return x + (x * sums[2 * coord_dims : 2 * coord_dims + 1] - pushed) * scale


def join_kernel(*refs):
    *block_refs, out_ref = refs
    size = block_refs[0].shape[0]
    for i, ref in enumerate(block_refs):
        out_ref[i * size : (i + 1) * size] = ref[...]


def group_kernel(offsets, per_dev, *refs):
    slot_refs = refs[: len(offsets)]
    out_ref, stress_ref, dis_ref, weight_ref, tile_ref = refs[len(offsets) :]
    points = dis_ref.shape[0]
    spots = tile_spots(per_dev, points)
    tiles = 2 * len(spots) + 1
    for ref, base, place in held_slots(offsets, slot_refs, tiles):
        tile_ref[place] = ref[base + tiles - 1]
        for i, (rows, columns) in enumerate(spots):
            start = pl.multiple_of(place * per_dev + rows.start, SUBLANES)
            dis_ref[pl.ds(start, SUBLANES), columns] = ref[base + i]
            weight_ref[pl.ds(start, SUBLANES), columns] = ref[base + len(spots) + i]
    blocks = [tile_ref[i] for i in range(tile_ref.shape[0])]
    halves = [
        jnp.concatenate([t[:, low : low + per_dev] for t in blocks], axis=1)
        for low in (0, per_dev)
    ]
    x = jnp.concatenate(halves, axis=0)
    coord_dims = x.shape[0]
    chunks = [slice(row, row + LANES) for row in range(0, points, LANES)]
    ones = jnp.ones((coord_dims, points), jnp.bfloat16)
    scales = [inverse_weight(weight_ref[rows], ones) for rows in chunks]
    denom = sum(lane_sums(weight_ref[rows] * dis_ref[rows] * dis_ref[rows]) for rows in chunks)
    place = lax.axis_index("wide")
    own_rows = pl.ds(pl.multiple_of(place * per_dev, SUBLANES), per_dev)
    shape = (points, per_dev)
    pick = lax.broadcasted_iota(jnp.int32, shape, 0) - lax.broadcasted_iota(jnp.int32, shape, 1)
    pick = (pick == place * per_dev).astype(jnp.float32).astype(jnp.bfloat16)
    sums = [denom]
    for sweep in range(ITERS):
        parts = split_bf16(x, 3)
        sides = jnp.concatenate([parts[0], parts[1], ones], axis=0)
        left, right = left_side(x, parts), right_side(x, parts)
        last = sweep == ITERS - 1
        stress, following = 0.0, []
        for rows, scale in zip(chunks, scales):
            square = dot(left[:, rows], right, TN)
            inverse = lax.rsqrt(square)
            weight, dis = weight_ref[rows], dis_ref[rows]
            misfit = dis - square * inverse
            weighted = weight * misfit
            stress += lane_sums(weighted * misfit)
            if not last:
                following.append(moved(x[:, rows], sides, weighted * inverse, scale))
        sums.append(stress)
        if last:
            own = dot(jnp.concatenate(parts, axis=0), pick, (((1,), (0,)), ((), ())))
            own = sum(own[i * coord_dims : (i + 1) * coord_dims] for i in range(3))
            square = dot(left_side(own, split_bf16(own, 3)), right, TN)
            inverse = lax.rsqrt(square)
            weight = weight_ref[own_rows, :]
            push = weight * (dis_ref[own_rows, :] - square * inverse) * inverse
            out_ref[...] = moved(own, sides, push, inverse_weight(weight, ones))
        else:
            x = jnp.concatenate(following, axis=1)
    total = jnp.sum(jnp.concatenate(sums, axis=0), axis=1, keepdims=True)
    ratios = total[1:] / total[:1]
    lanes = lax.broadcasted_iota(jnp.int32, (ITERS, LANES), 1)
    lined = jnp.where(lanes == lax.broadcasted_iota(jnp.int32, (ITERS, LANES), 0), ratios, 0.0)
    stress_ref[...] = jnp.sum(lined, axis=0, keepdims=True)[:, :ITERS]


def small_body(dissim, classes, coords):
    coord_dims, _, per_dev = coords.shape
    points = dissim.shape[2]
    devices = points // per_dev
    vmem = pl.BlockSpec(memory_space=pltpu.VMEM)
    hbm = pl.BlockSpec(memory_space=pltpu.HBM)
    f32 = functools.partial(jax.ShapeDtypeStruct, dtype=jnp.float32)
    params = pltpu.CompilerParams(vmem_limit_bytes=16 << 20)

    def swap(value, offset):
        return lax.ppermute(value, "wide", [(i, i ^ offset) for i in range(devices)])

    tiles = 2 * len(tile_spots(per_dev, points)) + 1
    inputs = (dissim[0], classes[0], coords[:, 0, :])
    packed = pl.pallas_call(
        pack_kernel,
        out_shape=f32((tiles, SUBLANES, LANES)),
        in_specs=[hbm] * 3,
        out_specs=vmem,
        scratch_shapes=[
            pltpu.VMEM((per_dev, points), jnp.float32),
            pltpu.VMEM((per_dev, points), jnp.int32),
            pltpu.VMEM((coord_dims, per_dev), jnp.float32),
            pltpu.SemaphoreType.DMA((3,)),
        ],
        compiler_params=params,
        name="pack",
    )(*(pltpu.with_memory_space_constraint(array, pltpu.HBM) for array in inputs))
    far, near, side = devices // 2, devices // 4, devices // 8
    held = {0: packed}
    for offset in (far, side, near, far | near | side):
        held[offset] = swap(packed, offset)
    for source, step in ((far, near), (far, side), (side, near)):
        held[source | step] = swap(held[source], step)
    early = [0, far, near, side]
    late = [offset for offset in held if offset not in early]
    block = packed.shape[0]

    def join(group, flops):
        return pl.pallas_call(
            join_kernel,
            out_shape=f32((len(group) * block, SUBLANES, LANES)),
            in_specs=[vmem] * len(group),
            out_specs=vmem,
            compiler_params=params,
            cost_estimate=pl.CostEstimate(flops=flops, bytes_accessed=0, transcendentals=0),
            name="join",
        )(*(held[offset] for offset in group))

    first, second = join(early, 1), join(late, 1)
    slots = [first, swap(first, 1), second, swap(second, 1)]
    offsets = [early, [o ^ 1 for o in early], late, [o ^ 1 for o in late]]
    final, stress = pl.pallas_call(
        functools.partial(group_kernel, offsets, per_dev),
        out_shape=(f32((coord_dims, per_dev)), f32((1, ITERS))),
        in_specs=[vmem] * len(slots),
        out_specs=(vmem, vmem),
        scratch_shapes=[
            pltpu.VMEM((points, points), jnp.float32),
            pltpu.VMEM((points, points), jnp.float32),
            pltpu.VMEM((devices, SUBLANES, LANES), jnp.float32),
        ],
        compiler_params=params,
        name="group_smacof",
    )(*slots)
    return (final[:, None, :], stress[0])


def distributed_body(dissim, classes, coords):
    halves = dissim.shape[0]
    per_dev = dissim.shape[1]
    columns = dissim.shape[2]
    coord_dims = coords.shape[0]
    row_count = halves * per_dev
    dis_tile = dissim.reshape(row_count, columns)
    weight = class_weight(classes.reshape(row_count, columns))
    denom_local = jnp.sum(weight * dis_tile * dis_tile)
    half_index = lax.axis_index("narrow")
    denom_total = lax.psum(denom_local, ("wide", "narrow"))
    positions = coords
    numbers = []
    for sweep in range(ITERS):
        row_points = lax.all_gather(positions, "narrow", axis=1, tiled=True)
        row_x = row_points.reshape(coord_dims, row_count)
        row_sq = jnp.sum(row_x * row_x, axis=0)
        fold_column_x = lax.dynamic_index_in_dim(
            lax.all_gather(row_points, "wide", axis=2, tiled=True), half_index, 1, keepdims=False
        )
        inner_prod = lax.dot_general(
            row_x,
            fold_column_x,
            (((0,), (0,)), ((), ())),
            precision=lax.Precision.HIGHEST,
            preferred_element_type=jnp.float32,
        )
        col_sq = jnp.sum(fold_column_x * fold_column_x, axis=0)
        distance = jnp.sqrt(row_sq[:, None] + col_sq[None, :] - 2.0 * inner_prod + 1.0)
        ratios = weight * dis_tile / distance
        pull_term = lax.dot_general(
            weight - ratios,
            fold_column_x,
            (((1,), (1,)), ((), ())),
            precision=lax.Precision.HIGHEST,
            preferred_element_type=jnp.float32,
        )
        misfit = dis_tile - distance
        pull_sums = pull_term.reshape(halves, per_dev, coord_dims).transpose(0, 2, 1)
        weight_sum, ratio_sum, pull_share = (
            lax.psum_scatter(
                jnp.sum(weight, axis=1).reshape(halves, per_dev),
                "narrow",
                scatter_dimension=0,
                tiled=True,
            ),
            lax.psum_scatter(
                jnp.sum(ratios, axis=1).reshape(halves, per_dev),
                "narrow",
                scatter_dimension=0,
                tiled=True,
            ),
            lax.psum_scatter(pull_sums, "narrow", scatter_dimension=0, tiled=True),
        )
        own_coords = positions[:, 0, :]
        updated = (own_coords * (1.0 + ratio_sum[0]) + pull_share[0]) / (1.0 + weight_sum[0])
        positions = updated[:, None, :]
        numbers.append(
            lax.psum(jnp.sum(weight * misfit * misfit), ("wide", "narrow")) / denom_total
        )
    stress = jnp.stack(numbers)
    return (positions, stress)


def solution(mesh):
    def body(dissim, classes, coords):
        coord_dims, halves, per_dev = coords.shape
        points, devices = dissim.shape[2], mesh.shape["wide"]
        small = halves == 1 and mesh.shape["narrow"] == 1 and points * points <= MOST_PAIRS
        small = small and coord_dims == 2 * SUBLANES and 2 * per_dev <= LANES
        small = small and per_dev % SUBLANES == 0 and points % LANES == 0
        small = small and devices == 16
        return (small_body if small else distributed_body)(dissim, classes, coords)

    return jax.shard_map(
        body,
        mesh=mesh,
        in_specs=(
            P(None, ("grp", "wide"), "narrow"),
            P(None, ("grp", "wide"), "narrow"),
            P(None, "narrow", ("grp", "wide")),
        ),
        out_specs=(P(None, "narrow", ("grp", "wide")), P("grp")),
        check_vma=False,
    )
```

```python
import functools

import jax
import jax.numpy as jnp
from jax import lax
from jax.experimental import pallas as pl
from jax.experimental.pallas import tpu as pltpu
from jax.sharding import PartitionSpec as P

ITERS = 3
LANES = 128
MOST_PAIRS = 1 << 19


def class_weight(class_codes):
    return jnp.where(
        class_codes == 3,
        1.0,
        jnp.where(class_codes == 2, 0.5, jnp.where(class_codes == 1, 0.25, 0.0)),
    ).astype(jnp.float32)


def split_bf16(value, terms):
    parts = []
    for _ in range(terms):
        part = value.astype(jnp.bfloat16)
        parts.append(part)
        value = value - part.astype(jnp.float32)
    return parts


SUBLANES = 8
NT = (((1,), (1,)), ((), ()))
TN = (((0,), (0,)), ((), ()))
dot = functools.partial(lax.dot_general, preferred_element_type=jnp.float32)


def lane_sums(value):
    rows = jnp.sum(value, axis=0, keepdims=True)
    return sum(rows[:, i : i + LANES] for i in range(0, rows.shape[1], LANES))


def tile_spots(per_dev, points):
    return [
        (slice(row, row + SUBLANES), slice(column, column + LANES))
        for row in range(0, per_dev, SUBLANES)
        for column in range(0, points, LANES)
    ]


def pack_kernel(dis_hbm, cls_hbm, x_hbm, out_ref, dis_ref, cls_ref, x_ref, sems):
    copies = [
        pltpu.make_async_copy(src, dst, sems.at[i])
        for i, (src, dst) in enumerate(
            [(dis_hbm, dis_ref), (cls_hbm, cls_ref), (x_hbm, x_ref)]
        )
    ]
    for copy in copies:
        copy.start()
    for copy in copies:
        copy.wait()
    spots = tile_spots(*dis_ref.shape)
    for i, spot in enumerate(spots):
        out_ref[i] = dis_ref[spot]
        out_ref[len(spots) + i] = class_weight(cls_ref[spot])
    half, per_dev = x_ref.shape[0] // 2, x_ref.shape[1]
    pad = jnp.zeros((half, LANES - 2 * per_dev), jnp.float32)
    out_ref[2 * len(spots)] = jnp.concatenate([x_ref[:half], x_ref[half:], pad], axis=1)


def held_slots(offsets, refs, tiles):
    me = lax.axis_index("wide")
    for group, ref in zip(offsets, refs):
        for slot, offset in enumerate(group):
            yield ref, slot * tiles, me ^ offset


def norm_rows(top, bottom, coord_dims):
    pad = jnp.zeros((coord_dims - 6, top[0].shape[1]), jnp.float32)
    rows = [p.astype(jnp.float32) for p in (*top, *bottom)]
    return jnp.concatenate([*rows, pad], axis=0).astype(jnp.bfloat16)


def left_side(x, parts):
    hi, mid, lo = (-2.0 * p for p in parts)
    norm = split_bf16(jnp.sum(x * x, axis=0, keepdims=True), 3)
    ones = [jnp.ones((3, x.shape[1]), jnp.bfloat16)]
    return jnp.concatenate([hi, hi, hi, mid, mid, lo, norm_rows(norm, ones, x.shape[0])], axis=0)


def right_side(x, parts):
    hi, mid, lo = parts
    norm = split_bf16(jnp.sum(x * x, axis=0, keepdims=True) + 1.0, 3)
    ones = [jnp.ones((3, x.shape[1]), jnp.bfloat16)]
    return jnp.concatenate([hi, mid, lo, hi, mid, hi, norm_rows(ones, norm, x.shape[0])], axis=0)


def inverse_weight(weight, ones):
    return 1.0 / (1.0 + dot(weight.astype(jnp.bfloat16), ones, NT).T[0:1])


def moved(x, sides, push, scale):
    coord_dims = x.shape[0]
    parts = jnp.concatenate(split_bf16(push, 2), axis=1)
    sums = dot(parts, jnp.concatenate([sides, sides], axis=1), NT).T
    pushed = sums[:coord_dims] + sums[coord_dims : 2 * coord_dims]
    return x + (x * sums[2 * coord_dims : 2 * coord_dims + 1] - pushed) * scale


def join_kernel(*refs):
    *block_refs, out_ref = refs
    size = block_refs[0].shape[0]
    for i, ref in enumerate(block_refs):
        out_ref[i * size : (i + 1) * size] = ref[...]


def group_kernel(offsets, per_dev, *refs):
    slot_refs = refs[: len(offsets)]
    out_ref, stress_ref, dis_ref, weight_ref, tile_ref = refs[len(offsets) :]
    points = dis_ref.shape[0]
    spots = tile_spots(per_dev, points)
    tiles = 2 * len(spots) + 1
    for ref, base, place in held_slots(offsets, slot_refs, tiles):
        tile_ref[place] = ref[base + tiles - 1]
        for i, (rows, columns) in enumerate(spots):
            start = pl.multiple_of(place * per_dev + rows.start, SUBLANES)
            dis_ref[pl.ds(start, SUBLANES), columns] = ref[base + i]
            weight_ref[pl.ds(start, SUBLANES), columns] = ref[base + len(spots) + i]
    blocks = [tile_ref[i] for i in range(tile_ref.shape[0])]
    halves = [
        jnp.concatenate([t[:, low : low + per_dev] for t in blocks], axis=1)
        for low in (0, per_dev)
    ]
    x = jnp.concatenate(halves, axis=0)
    coord_dims = x.shape[0]
    chunks = [slice(row, row + LANES) for row in range(0, points, LANES)]
    ones = jnp.ones((coord_dims, points), jnp.bfloat16)
    scales = [inverse_weight(weight_ref[rows], ones) for rows in chunks]
    denom = sum(lane_sums(weight_ref[rows] * dis_ref[rows] * dis_ref[rows]) for rows in chunks)
    place = lax.axis_index("wide")
    own_rows = pl.ds(pl.multiple_of(place * per_dev, SUBLANES), per_dev)
    shape = (points, per_dev)
    pick = lax.broadcasted_iota(jnp.int32, shape, 0) - lax.broadcasted_iota(jnp.int32, shape, 1)
    pick = (pick == place * per_dev).astype(jnp.float32).astype(jnp.bfloat16)
    sums = [denom]
    for sweep in range(ITERS):
        parts = split_bf16(x, 3)
        sides = jnp.concatenate([parts[0], parts[1], ones], axis=0)
        left, right = left_side(x, parts), right_side(x, parts)
        last = sweep == ITERS - 1
        stress, following = 0.0, []
        for rows, scale in zip(chunks, scales):
            square = dot(left[:, rows], right, TN)
            inverse = lax.rsqrt(square)
            weight, dis = weight_ref[rows], dis_ref[rows]
            misfit = dis - square * inverse
            weighted = weight * misfit
            stress += lane_sums(weighted * misfit)
            if not last:
                following.append(moved(x[:, rows], sides, weighted * inverse, scale))
        sums.append(stress)
        if last:
            own = dot(jnp.concatenate(parts, axis=0), pick, (((1,), (0,)), ((), ())))
            own = sum(own[i * coord_dims : (i + 1) * coord_dims] for i in range(3))
            square = dot(left_side(own, split_bf16(own, 3)), right, TN)
            inverse = lax.rsqrt(square)
            weight = weight_ref[own_rows, :]
            push = weight * (dis_ref[own_rows, :] - square * inverse) * inverse
            out_ref[...] = moved(own, sides, push, inverse_weight(weight, ones))
        else:
            x = jnp.concatenate(following, axis=1)
    total = jnp.sum(jnp.concatenate(sums, axis=0), axis=1, keepdims=True)
    ratios = total[1:] / total[:1]
    lanes = lax.broadcasted_iota(jnp.int32, (ITERS, LANES), 1)
    lined = jnp.where(lanes == lax.broadcasted_iota(jnp.int32, (ITERS, LANES), 0), ratios, 0.0)
    stress_ref[...] = jnp.sum(lined, axis=0, keepdims=True)[:, :ITERS]


def small_body(dissim, classes, coords):
    coord_dims, _, per_dev = coords.shape
    points = dissim.shape[2]
    devices = points // per_dev
    vmem = pl.BlockSpec(memory_space=pltpu.VMEM)
    hbm = pl.BlockSpec(memory_space=pltpu.HBM)
    f32 = functools.partial(jax.ShapeDtypeStruct, dtype=jnp.float32)
    params = pltpu.CompilerParams(vmem_limit_bytes=16 << 20)

    def swap(value, offset):
        return lax.ppermute(value, "wide", [(i, i ^ offset) for i in range(devices)])

    tiles = 2 * len(tile_spots(per_dev, points)) + 1
    inputs = (dissim[0], classes[0], coords[:, 0, :])
    packed = pl.pallas_call(
        pack_kernel,
        out_shape=f32((tiles, SUBLANES, LANES)),
        in_specs=[hbm] * 3,
        out_specs=vmem,
        scratch_shapes=[
            pltpu.VMEM((per_dev, points), jnp.float32),
            pltpu.VMEM((per_dev, points), jnp.int32),
            pltpu.VMEM((coord_dims, per_dev), jnp.float32),
            pltpu.SemaphoreType.DMA((3,)),
        ],
        compiler_params=params,
        name="pack",
    )(*(pltpu.with_memory_space_constraint(array, pltpu.HBM) for array in inputs))
    far, near, side = devices // 2, devices // 4, devices // 8
    held = {0: packed}
    for offset in (side, far, near, far | near | side):
        held[offset] = swap(packed, offset)
    for source, step in ((far, side), (side, near), (far, near)):
        held[source | step] = swap(held[source], step)
    early = [0, side, near, far]
    late = [offset for offset in held if offset not in early]
    block = packed.shape[0]

    def join(group, flops):
        return pl.pallas_call(
            join_kernel,
            out_shape=f32((len(group) * block, SUBLANES, LANES)),
            in_specs=[vmem] * len(group),
            out_specs=vmem,
            compiler_params=params,
            cost_estimate=pl.CostEstimate(flops=flops, bytes_accessed=0, transcendentals=0),
            name="join",
        )(*(held[offset] for offset in group))

    first, second = join(early, 1), join(late, 1)
    slots = [first, swap(first, 1), second, swap(second, 1)]
    offsets = [early, [o ^ 1 for o in early], late, [o ^ 1 for o in late]]
    final, stress = pl.pallas_call(
        functools.partial(group_kernel, offsets, per_dev),
        out_shape=(f32((coord_dims, per_dev)), f32((1, ITERS))),
        in_specs=[vmem] * len(slots),
        out_specs=(vmem, vmem),
        scratch_shapes=[
            pltpu.VMEM((points, points), jnp.float32),
            pltpu.VMEM((points, points), jnp.float32),
            pltpu.VMEM((devices, SUBLANES, LANES), jnp.float32),
        ],
        compiler_params=params,
        name="group_smacof",
    )(*slots)
    return (final[:, None, :], stress[0])


def distributed_body(dissim, classes, coords):
    halves = dissim.shape[0]
    per_dev = dissim.shape[1]
    columns = dissim.shape[2]
    coord_dims = coords.shape[0]
    row_count = halves * per_dev
    dis_tile = dissim.reshape(row_count, columns)
    weight = class_weight(classes.reshape(row_count, columns))
    denom_local = jnp.sum(weight * dis_tile * dis_tile)
    half_index = lax.axis_index("narrow")
    denom_total = lax.psum(denom_local, ("wide", "narrow"))
    positions = coords
    numbers = []
    for sweep in range(ITERS):
        row_points = lax.all_gather(positions, "narrow", axis=1, tiled=True)
        row_x = row_points.reshape(coord_dims, row_count)
        row_sq = jnp.sum(row_x * row_x, axis=0)
        fold_column_x = lax.dynamic_index_in_dim(
            lax.all_gather(row_points, "wide", axis=2, tiled=True), half_index, 1, keepdims=False
        )
        inner_prod = lax.dot_general(
            row_x,
            fold_column_x,
            (((0,), (0,)), ((), ())),
            precision=lax.Precision.HIGHEST,
            preferred_element_type=jnp.float32,
        )
        col_sq = jnp.sum(fold_column_x * fold_column_x, axis=0)
        distance = jnp.sqrt(row_sq[:, None] + col_sq[None, :] - 2.0 * inner_prod + 1.0)
        ratios = weight * dis_tile / distance
        pull_term = lax.dot_general(
            weight - ratios,
            fold_column_x,
            (((1,), (1,)), ((), ())),
            precision=lax.Precision.HIGHEST,
            preferred_element_type=jnp.float32,
        )
        misfit = dis_tile - distance
        pull_sums = pull_term.reshape(halves, per_dev, coord_dims).transpose(0, 2, 1)
        weight_sum, ratio_sum, pull_share = (
            lax.psum_scatter(
                jnp.sum(weight, axis=1).reshape(halves, per_dev),
                "narrow",
                scatter_dimension=0,
                tiled=True,
            ),
            lax.psum_scatter(
                jnp.sum(ratios, axis=1).reshape(halves, per_dev),
                "narrow",
                scatter_dimension=0,
                tiled=True,
            ),
            lax.psum_scatter(pull_sums, "narrow", scatter_dimension=0, tiled=True),
        )
        own_coords = positions[:, 0, :]
        updated = (own_coords * (1.0 + ratio_sum[0]) + pull_share[0]) / (1.0 + weight_sum[0])
        positions = updated[:, None, :]
        numbers.append(
            lax.psum(jnp.sum(weight * misfit * misfit), ("wide", "narrow")) / denom_total
        )
    stress = jnp.stack(numbers)
    return (positions, stress)


def solution(mesh):
    def body(dissim, classes, coords):
        coord_dims, halves, per_dev = coords.shape
        points, devices = dissim.shape[2], mesh.shape["wide"]
        small = halves == 1 and mesh.shape["narrow"] == 1 and points * points <= MOST_PAIRS
        small = small and coord_dims == 2 * SUBLANES and 2 * per_dev <= LANES
        small = small and per_dev % SUBLANES == 0 and points % LANES == 0
        small = small and devices == 16
        return (small_body if small else distributed_body)(dissim, classes, coords)

    return jax.shard_map(
        body,
        mesh=mesh,
        in_specs=(
            P(None, ("grp", "wide"), "narrow"),
            P(None, ("grp", "wide"), "narrow"),
            P(None, "narrow", ("grp", "wide")),
        ),
        out_specs=(P(None, "narrow", ("grp", "wide")), P("grp")),
        check_vma=False,
    )
```

```python
import functools

import jax
import jax.numpy as jnp
from jax import lax
from jax.experimental import pallas as pl
from jax.experimental.pallas import tpu as pltpu
from jax.sharding import PartitionSpec as P

ITERS = 3
LANES = 128
MOST_PAIRS = 1 << 19


def class_weight(class_codes):
    return jnp.where(
        class_codes == 3,
        1.0,
        jnp.where(class_codes == 2, 0.5, jnp.where(class_codes == 1, 0.25, 0.0)),
    ).astype(jnp.float32)


def split_bf16(value, terms):
    parts = []
    for _ in range(terms):
        part = value.astype(jnp.bfloat16)
        parts.append(part)
        value = value - part.astype(jnp.float32)
    return parts


SUBLANES = 8
NT = (((1,), (1,)), ((), ()))
TN = (((0,), (0,)), ((), ()))
dot = functools.partial(lax.dot_general, preferred_element_type=jnp.float32)


def lane_sums(value):
    rows = jnp.sum(value, axis=0, keepdims=True)
    return sum(rows[:, i : i + LANES] for i in range(0, rows.shape[1], LANES))


def tile_spots(per_dev, points):
    return [
        (slice(row, row + SUBLANES), slice(column, column + LANES))
        for row in range(0, per_dev, SUBLANES)
        for column in range(0, points, LANES)
    ]


def pack_kernel(dis_hbm, cls_hbm, x_hbm, out_ref, dis_ref, cls_ref, x_ref, sems):
    copies = [
        pltpu.make_async_copy(src, dst, sems.at[i])
        for i, (src, dst) in enumerate(
            [(dis_hbm, dis_ref), (cls_hbm, cls_ref), (x_hbm, x_ref)]
        )
    ]
    for copy in copies:
        copy.start()
    for copy in copies:
        copy.wait()
    spots = tile_spots(*dis_ref.shape)
    for i, spot in enumerate(spots):
        out_ref[i] = dis_ref[spot]
        out_ref[len(spots) + i] = class_weight(cls_ref[spot])
    half, per_dev = x_ref.shape[0] // 2, x_ref.shape[1]
    pad = jnp.zeros((half, LANES - 2 * per_dev), jnp.float32)
    out_ref[2 * len(spots)] = jnp.concatenate([x_ref[:half], x_ref[half:], pad], axis=1)


def held_slots(offsets, refs, tiles):
    me = lax.axis_index("wide")
    for group, ref in zip(offsets, refs):
        for slot, offset in enumerate(group):
            yield ref, slot * tiles, me ^ offset


def norm_rows(top, bottom, coord_dims):
    pad = jnp.zeros((coord_dims - 6, top[0].shape[1]), jnp.float32)
    rows = [p.astype(jnp.float32) for p in (*top, *bottom)]
    return jnp.concatenate([*rows, pad], axis=0).astype(jnp.bfloat16)


def left_side(x, parts):
    hi, mid, lo = (-2.0 * p for p in parts)
    norm = split_bf16(jnp.sum(x * x, axis=0, keepdims=True), 3)
    ones = [jnp.ones((3, x.shape[1]), jnp.bfloat16)]
    return jnp.concatenate([hi, hi, hi, mid, mid, lo, norm_rows(norm, ones, x.shape[0])], axis=0)


def right_side(x, parts):
    hi, mid, lo = parts
    norm = split_bf16(jnp.sum(x * x, axis=0, keepdims=True) + 1.0, 3)
    ones = [jnp.ones((3, x.shape[1]), jnp.bfloat16)]
    return jnp.concatenate([hi, mid, lo, hi, mid, hi, norm_rows(ones, norm, x.shape[0])], axis=0)


def inverse_weight(weight, ones):
    return 1.0 / (1.0 + dot(weight.astype(jnp.bfloat16), ones, NT).T[0:1])


def moved(x, sides, push, scale):
    coord_dims = x.shape[0]
    parts = jnp.concatenate(split_bf16(push, 2), axis=1)
    sums = dot(parts, jnp.concatenate([sides, sides], axis=1), NT).T
    pushed = sums[:coord_dims] + sums[coord_dims : 2 * coord_dims]
    return x + (x * sums[2 * coord_dims : 2 * coord_dims + 1] - pushed) * scale


def join_kernel(*refs):
    *block_refs, out_ref = refs
    size = block_refs[0].shape[0]
    for i, ref in enumerate(block_refs):
        out_ref[i * size : (i + 1) * size] = ref[...]


def group_kernel(offsets, per_dev, *refs):
    slot_refs = refs[: len(offsets)]
    out_ref, stress_ref, dis_ref, weight_ref, tile_ref = refs[len(offsets) :]
    points = dis_ref.shape[0]
    spots = tile_spots(per_dev, points)
    tiles = 2 * len(spots) + 1
    for ref, base, place in held_slots(offsets, slot_refs, tiles):
        tile_ref[place] = ref[base + tiles - 1]
        for i, (rows, columns) in enumerate(spots):
            start = pl.multiple_of(place * per_dev + rows.start, SUBLANES)
            dis_ref[pl.ds(start, SUBLANES), columns] = ref[base + i]
            weight_ref[pl.ds(start, SUBLANES), columns] = ref[base + len(spots) + i]
    blocks = [tile_ref[i] for i in range(tile_ref.shape[0])]
    halves = [
        jnp.concatenate([t[:, low : low + per_dev] for t in blocks], axis=1)
        for low in (0, per_dev)
    ]
    x = jnp.concatenate(halves, axis=0)
    coord_dims = x.shape[0]
    chunks = [slice(row, row + LANES) for row in range(0, points, LANES)]
    ones = jnp.ones((coord_dims, points), jnp.bfloat16)
    scales = [inverse_weight(weight_ref[rows], ones) for rows in chunks]
    denom = sum(lane_sums(weight_ref[rows] * dis_ref[rows] * dis_ref[rows]) for rows in chunks)
    place = lax.axis_index("wide")
    own_rows = pl.ds(pl.multiple_of(place * per_dev, SUBLANES), per_dev)
    shape = (points, per_dev)
    pick = lax.broadcasted_iota(jnp.int32, shape, 0) - lax.broadcasted_iota(jnp.int32, shape, 1)
    pick = (pick == place * per_dev).astype(jnp.float32).astype(jnp.bfloat16)
    sums = [denom]
    for sweep in range(ITERS):
        parts = split_bf16(x, 3)
        sides = jnp.concatenate([parts[0], parts[1], ones], axis=0)
        left, right = left_side(x, parts), right_side(x, parts)
        last = sweep == ITERS - 1
        stress, following = 0.0, []
        for rows, scale in zip(chunks, scales):
            square = dot(left[:, rows], right, TN)
            inverse = lax.rsqrt(square)
            weight, dis = weight_ref[rows], dis_ref[rows]
            misfit = dis - square * inverse
            weighted = weight * misfit
            stress += lane_sums(weighted * misfit)
            if not last:
                following.append(moved(x[:, rows], sides, weighted * inverse, scale))
        sums.append(stress)
        if last:
            own = dot(jnp.concatenate(parts, axis=0), pick, (((1,), (0,)), ((), ())))
            own = sum(own[i * coord_dims : (i + 1) * coord_dims] for i in range(3))
            square = dot(left_side(own, split_bf16(own, 3)), right, TN)
            inverse = lax.rsqrt(square)
            weight = weight_ref[own_rows, :]
            push = weight * (dis_ref[own_rows, :] - square * inverse) * inverse
            out_ref[...] = moved(own, sides, push, inverse_weight(weight, ones))
        else:
            x = jnp.concatenate(following, axis=1)
    total = jnp.sum(jnp.concatenate(sums, axis=0), axis=1, keepdims=True)
    ratios = total[1:] / total[:1]
    lanes = lax.broadcasted_iota(jnp.int32, (ITERS, LANES), 1)
    lined = jnp.where(lanes == lax.broadcasted_iota(jnp.int32, (ITERS, LANES), 0), ratios, 0.0)
    stress_ref[...] = jnp.sum(lined, axis=0, keepdims=True)[:, :ITERS]


def small_body(dissim, classes, coords):
    coord_dims, _, per_dev = coords.shape
    points = dissim.shape[2]
    devices = points // per_dev
    vmem = pl.BlockSpec(memory_space=pltpu.VMEM)
    hbm = pl.BlockSpec(memory_space=pltpu.HBM)
    f32 = functools.partial(jax.ShapeDtypeStruct, dtype=jnp.float32)
    params = pltpu.CompilerParams(vmem_limit_bytes=16 << 20)

    def swap(value, offset):
        return lax.ppermute(value, "wide", [(i, i ^ offset) for i in range(devices)])

    tiles = 2 * len(tile_spots(per_dev, points)) + 1
    inputs = (dissim[0], classes[0], coords[:, 0, :])
    packed = pl.pallas_call(
        pack_kernel,
        out_shape=f32((tiles, SUBLANES, LANES)),
        in_specs=[hbm] * 3,
        out_specs=vmem,
        scratch_shapes=[
            pltpu.VMEM((per_dev, points), jnp.float32),
            pltpu.VMEM((per_dev, points), jnp.int32),
            pltpu.VMEM((coord_dims, per_dev), jnp.float32),
            pltpu.SemaphoreType.DMA((3,)),
        ],
        compiler_params=params,
        name="pack",
    )(*(pltpu.with_memory_space_constraint(array, pltpu.HBM) for array in inputs))
    far, near, side = devices // 2, devices // 4, devices // 8
    held = {0: packed}
    for offset in (far, side, near, far | near | side | 1):
        held[offset] = swap(packed, offset)
    for source, step in ((far, near), (far, side), (side, near)):
        held[source | step] = swap(held[source], step)
    early = [0, far, near, side]
    late = [offset for offset in held if offset not in early]
    block = packed.shape[0]

    def join(group, flops):
        return pl.pallas_call(
            join_kernel,
            out_shape=f32((len(group) * block, SUBLANES, LANES)),
            in_specs=[vmem] * len(group),
            out_specs=vmem,
            compiler_params=params,
            cost_estimate=pl.CostEstimate(flops=flops, bytes_accessed=0, transcendentals=0),
            name="join",
        )(*(held[offset] for offset in group))

    first, second = join(early, 1), join(late, 1)
    slots = [first, swap(first, 1), second, swap(second, 1)]
    offsets = [early, [o ^ 1 for o in early], late, [o ^ 1 for o in late]]
    final, stress = pl.pallas_call(
        functools.partial(group_kernel, offsets, per_dev),
        out_shape=(f32((coord_dims, per_dev)), f32((1, ITERS))),
        in_specs=[vmem] * len(slots),
        out_specs=(vmem, vmem),
        scratch_shapes=[
            pltpu.VMEM((points, points), jnp.float32),
            pltpu.VMEM((points, points), jnp.float32),
            pltpu.VMEM((devices, SUBLANES, LANES), jnp.float32),
        ],
        compiler_params=params,
        name="group_smacof",
    )(*slots)
    return (final[:, None, :], stress[0])


def distributed_body(dissim, classes, coords):
    halves = dissim.shape[0]
    per_dev = dissim.shape[1]
    columns = dissim.shape[2]
    coord_dims = coords.shape[0]
    row_count = halves * per_dev
    dis_tile = dissim.reshape(row_count, columns)
    weight = class_weight(classes.reshape(row_count, columns))
    denom_local = jnp.sum(weight * dis_tile * dis_tile)
    half_index = lax.axis_index("narrow")
    denom_total = lax.psum(denom_local, ("wide", "narrow"))
    positions = coords
    numbers = []
    for sweep in range(ITERS):
        row_points = lax.all_gather(positions, "narrow", axis=1, tiled=True)
        row_x = row_points.reshape(coord_dims, row_count)
        row_sq = jnp.sum(row_x * row_x, axis=0)
        fold_column_x = lax.dynamic_index_in_dim(
            lax.all_gather(row_points, "wide", axis=2, tiled=True), half_index, 1, keepdims=False
        )
        inner_prod = lax.dot_general(
            row_x,
            fold_column_x,
            (((0,), (0,)), ((), ())),
            precision=lax.Precision.HIGHEST,
            preferred_element_type=jnp.float32,
        )
        col_sq = jnp.sum(fold_column_x * fold_column_x, axis=0)
        distance = jnp.sqrt(row_sq[:, None] + col_sq[None, :] - 2.0 * inner_prod + 1.0)
        ratios = weight * dis_tile / distance
        pull_term = lax.dot_general(
            weight - ratios,
            fold_column_x,
            (((1,), (1,)), ((), ())),
            precision=lax.Precision.HIGHEST,
            preferred_element_type=jnp.float32,
        )
        misfit = dis_tile - distance
        pull_sums = pull_term.reshape(halves, per_dev, coord_dims).transpose(0, 2, 1)
        weight_sum, ratio_sum, pull_share = (
            lax.psum_scatter(
                jnp.sum(weight, axis=1).reshape(halves, per_dev),
                "narrow",
                scatter_dimension=0,
                tiled=True,
            ),
            lax.psum_scatter(
                jnp.sum(ratios, axis=1).reshape(halves, per_dev),
                "narrow",
                scatter_dimension=0,
                tiled=True,
            ),
            lax.psum_scatter(pull_sums, "narrow", scatter_dimension=0, tiled=True),
        )
        own_coords = positions[:, 0, :]
        updated = (own_coords * (1.0 + ratio_sum[0]) + pull_share[0]) / (1.0 + weight_sum[0])
        positions = updated[:, None, :]
        numbers.append(
            lax.psum(jnp.sum(weight * misfit * misfit), ("wide", "narrow")) / denom_total
        )
    stress = jnp.stack(numbers)
    return (positions, stress)


def solution(mesh):
    def body(dissim, classes, coords):
        coord_dims, halves, per_dev = coords.shape
        points, devices = dissim.shape[2], mesh.shape["wide"]
        small = halves == 1 and mesh.shape["narrow"] == 1 and points * points <= MOST_PAIRS
        small = small and coord_dims == 2 * SUBLANES and 2 * per_dev <= LANES
        small = small and per_dev % SUBLANES == 0 and points % LANES == 0
        small = small and devices == 16
        return (small_body if small else distributed_body)(dissim, classes, coords)

    return jax.shard_map(
        body,
        mesh=mesh,
        in_specs=(
            P(None, ("grp", "wide"), "narrow"),
            P(None, ("grp", "wide"), "narrow"),
            P(None, "narrow", ("grp", "wide")),
        ),
        out_specs=(P(None, "narrow", ("grp", "wide")), P("grp")),
        check_vma=False,
    )
```

```python
import functools

import jax
import jax.numpy as jnp
from jax import lax
from jax.experimental import pallas as pl
from jax.experimental.pallas import tpu as pltpu
from jax.sharding import PartitionSpec as P

ITERS = 3
LANES = 128
MOST_PAIRS = 1 << 19


def class_weight(class_codes):
    return jnp.where(
        class_codes == 3,
        1.0,
        jnp.where(class_codes == 2, 0.5, jnp.where(class_codes == 1, 0.25, 0.0)),
    ).astype(jnp.float32)


def split_bf16(value, terms):
    parts = []
    for _ in range(terms):
        part = value.astype(jnp.bfloat16)
        parts.append(part)
        value = value - part.astype(jnp.float32)
    return parts


SUBLANES = 8
NT = (((1,), (1,)), ((), ()))
TN = (((0,), (0,)), ((), ()))
dot = functools.partial(lax.dot_general, preferred_element_type=jnp.float32)


def lane_sums(value):
    rows = jnp.sum(value, axis=0, keepdims=True)
    return sum(rows[:, i : i + LANES] for i in range(0, rows.shape[1], LANES))


def tile_spots(per_dev, points):
    return [
        (slice(row, row + SUBLANES), slice(column, column + LANES))
        for row in range(0, per_dev, SUBLANES)
        for column in range(0, points, LANES)
    ]


def pack_kernel(dis_hbm, cls_hbm, x_hbm, out_ref, dis_ref, cls_ref, x_ref, sems):
    copies = [
        pltpu.make_async_copy(src, dst, sems.at[i])
        for i, (src, dst) in enumerate(
            [(dis_hbm, dis_ref), (cls_hbm, cls_ref), (x_hbm, x_ref)]
        )
    ]
    for copy in copies:
        copy.start()
    for copy in copies:
        copy.wait()
    spots = tile_spots(*dis_ref.shape)
    for i, spot in enumerate(spots):
        out_ref[i] = dis_ref[spot]
        out_ref[len(spots) + i] = class_weight(cls_ref[spot])
    half, per_dev = x_ref.shape[0] // 2, x_ref.shape[1]
    pad = jnp.zeros((half, LANES - 2 * per_dev), jnp.float32)
    out_ref[2 * len(spots)] = jnp.concatenate([x_ref[:half], x_ref[half:], pad], axis=1)


def held_slots(offsets, refs, tiles):
    me = lax.axis_index("wide")
    for group, ref in zip(offsets, refs):
        for slot, offset in enumerate(group):
            yield ref, slot * tiles, me ^ offset


def norm_rows(top, bottom, coord_dims):
    pad = jnp.zeros((coord_dims - 6, top[0].shape[1]), jnp.float32)
    rows = [p.astype(jnp.float32) for p in (*top, *bottom)]
    return jnp.concatenate([*rows, pad], axis=0).astype(jnp.bfloat16)


def left_side(x, parts):
    hi, mid, lo = (-2.0 * p for p in parts)
    norm = split_bf16(jnp.sum(x * x, axis=0, keepdims=True), 3)
    ones = [jnp.ones((3, x.shape[1]), jnp.bfloat16)]
    return jnp.concatenate([hi, hi, hi, mid, mid, lo, norm_rows(norm, ones, x.shape[0])], axis=0)


def right_side(x, parts):
    hi, mid, lo = parts
    norm = split_bf16(jnp.sum(x * x, axis=0, keepdims=True) + 1.0, 3)
    ones = [jnp.ones((3, x.shape[1]), jnp.bfloat16)]
    return jnp.concatenate([hi, mid, lo, hi, mid, hi, norm_rows(ones, norm, x.shape[0])], axis=0)


def inverse_weight(weight, ones):
    return 1.0 / (1.0 + dot(weight.astype(jnp.bfloat16), ones, NT).T[0:1])


def moved(x, sides, push, scale):
    coord_dims = x.shape[0]
    parts = jnp.concatenate(split_bf16(push, 2), axis=1)
    sums = dot(parts, jnp.concatenate([sides, sides], axis=1), NT).T
    pushed = sums[:coord_dims] + sums[coord_dims : 2 * coord_dims]
    return x + (x * sums[2 * coord_dims : 2 * coord_dims + 1] - pushed) * scale


def join_kernel(*refs):
    *block_refs, out_ref = refs
    size = block_refs[0].shape[0]
    for i, ref in enumerate(block_refs):
        out_ref[i * size : (i + 1) * size] = ref[...]


def group_kernel(offsets, per_dev, *refs):
    slot_refs = refs[: len(offsets)]
    out_ref, stress_ref, dis_ref, weight_ref, tile_ref = refs[len(offsets) :]
    points = dis_ref.shape[0]
    spots = tile_spots(per_dev, points)
    tiles = 2 * len(spots) + 1
    for ref, base, place in held_slots(offsets, slot_refs, tiles):
        tile_ref[place] = ref[base + tiles - 1]
        for i, (rows, columns) in enumerate(spots):
            start = pl.multiple_of(place * per_dev + rows.start, SUBLANES)
            dis_ref[pl.ds(start, SUBLANES), columns] = ref[base + i]
            weight_ref[pl.ds(start, SUBLANES), columns] = ref[base + len(spots) + i]
    blocks = [tile_ref[i] for i in range(tile_ref.shape[0])]
    halves = [
        jnp.concatenate([t[:, low : low + per_dev] for t in blocks], axis=1)
        for low in (0, per_dev)
    ]
    x = jnp.concatenate(halves, axis=0)
    coord_dims = x.shape[0]
    chunks = [slice(0, points)]
    ones = jnp.ones((coord_dims, points), jnp.bfloat16)
    scales = [inverse_weight(weight_ref[rows], ones) for rows in chunks]
    denom = sum(lane_sums(weight_ref[rows] * dis_ref[rows] * dis_ref[rows]) for rows in chunks)
    place = lax.axis_index("wide")
    own_rows = pl.ds(pl.multiple_of(place * per_dev, SUBLANES), per_dev)
    shape = (points, per_dev)
    pick = lax.broadcasted_iota(jnp.int32, shape, 0) - lax.broadcasted_iota(jnp.int32, shape, 1)
    pick = (pick == place * per_dev).astype(jnp.float32).astype(jnp.bfloat16)
    sums = [denom]
    for sweep in range(ITERS):
        parts = split_bf16(x, 3)
        sides = jnp.concatenate([parts[0], parts[1], ones], axis=0)
        left, right = left_side(x, parts), right_side(x, parts)
        last = sweep == ITERS - 1
        stress, following = 0.0, []
        for rows, scale in zip(chunks, scales):
            square = dot(left[:, rows], right, TN)
            inverse = lax.rsqrt(square)
            weight, dis = weight_ref[rows], dis_ref[rows]
            misfit = dis - square * inverse
            weighted = weight * misfit
            stress += lane_sums(weighted * misfit)
            if not last:
                following.append(moved(x[:, rows], sides, weighted * inverse, scale))
        sums.append(stress)
        if last:
            own = dot(jnp.concatenate(parts, axis=0), pick, (((1,), (0,)), ((), ())))
            own = sum(own[i * coord_dims : (i + 1) * coord_dims] for i in range(3))
            square = dot(left_side(own, split_bf16(own, 3)), right, TN)
            inverse = lax.rsqrt(square)
            weight = weight_ref[own_rows, :]
            push = weight * (dis_ref[own_rows, :] - square * inverse) * inverse
            out_ref[...] = moved(own, sides, push, inverse_weight(weight, ones))
        else:
            x = jnp.concatenate(following, axis=1)
    total = jnp.sum(jnp.concatenate(sums, axis=0), axis=1, keepdims=True)
    ratios = total[1:] / total[:1]
    lanes = lax.broadcasted_iota(jnp.int32, (ITERS, LANES), 1)
    lined = jnp.where(lanes == lax.broadcasted_iota(jnp.int32, (ITERS, LANES), 0), ratios, 0.0)
    stress_ref[...] = jnp.sum(lined, axis=0, keepdims=True)[:, :ITERS]


def small_body(dissim, classes, coords):
    coord_dims, _, per_dev = coords.shape
    points = dissim.shape[2]
    devices = points // per_dev
    vmem = pl.BlockSpec(memory_space=pltpu.VMEM)
    hbm = pl.BlockSpec(memory_space=pltpu.HBM)
    f32 = functools.partial(jax.ShapeDtypeStruct, dtype=jnp.float32)
    params = pltpu.CompilerParams(vmem_limit_bytes=16 << 20)

    def swap(value, offset):
        return lax.ppermute(value, "wide", [(i, i ^ offset) for i in range(devices)])

    tiles = 2 * len(tile_spots(per_dev, points)) + 1
    inputs = (dissim[0], classes[0], coords[:, 0, :])
    packed = pl.pallas_call(
        pack_kernel,
        out_shape=f32((tiles, SUBLANES, LANES)),
        in_specs=[hbm] * 3,
        out_specs=vmem,
        scratch_shapes=[
            pltpu.VMEM((per_dev, points), jnp.float32),
            pltpu.VMEM((per_dev, points), jnp.int32),
            pltpu.VMEM((coord_dims, per_dev), jnp.float32),
            pltpu.SemaphoreType.DMA((3,)),
        ],
        compiler_params=params,
        name="pack",
    )(*(pltpu.with_memory_space_constraint(array, pltpu.HBM) for array in inputs))
    far, near, side = devices // 2, devices // 4, devices // 8
    held = {0: packed}
    for offset in (far, side, near, far | near | side):
        held[offset] = swap(packed, offset)
    for source, step in ((far, near), (far, side), (side, near)):
        held[source | step] = swap(held[source], step)
    early = [0, far, near, side]
    late = [offset for offset in held if offset not in early]
    block = packed.shape[0]

    def join(group, flops):
        return pl.pallas_call(
            join_kernel,
            out_shape=f32((len(group) * block, SUBLANES, LANES)),
            in_specs=[vmem] * len(group),
            out_specs=vmem,
            compiler_params=params,
            cost_estimate=pl.CostEstimate(flops=flops, bytes_accessed=0, transcendentals=0),
            name="join",
        )(*(held[offset] for offset in group))

    first, second = join(early, 1), join(late, 1)
    slots = [first, swap(first, 1), second, swap(second, 1)]
    offsets = [early, [o ^ 1 for o in early], late, [o ^ 1 for o in late]]
    final, stress = pl.pallas_call(
        functools.partial(group_kernel, offsets, per_dev),
        out_shape=(f32((coord_dims, per_dev)), f32((1, ITERS))),
        in_specs=[vmem] * len(slots),
        out_specs=(vmem, vmem),
        scratch_shapes=[
            pltpu.VMEM((points, points), jnp.float32),
            pltpu.VMEM((points, points), jnp.float32),
            pltpu.VMEM((devices, SUBLANES, LANES), jnp.float32),
        ],
        compiler_params=params,
        name="group_smacof",
    )(*slots)
    return (final[:, None, :], stress[0])


def distributed_body(dissim, classes, coords):
    halves = dissim.shape[0]
    per_dev = dissim.shape[1]
    columns = dissim.shape[2]
    coord_dims = coords.shape[0]
    row_count = halves * per_dev
    dis_tile = dissim.reshape(row_count, columns)
    weight = class_weight(classes.reshape(row_count, columns))
    denom_local = jnp.sum(weight * dis_tile * dis_tile)
    half_index = lax.axis_index("narrow")
    denom_total = lax.psum(denom_local, ("wide", "narrow"))
    positions = coords
    numbers = []
    for sweep in range(ITERS):
        row_points = lax.all_gather(positions, "narrow", axis=1, tiled=True)
        row_x = row_points.reshape(coord_dims, row_count)
        row_sq = jnp.sum(row_x * row_x, axis=0)
        fold_column_x = lax.dynamic_index_in_dim(
            lax.all_gather(row_points, "wide", axis=2, tiled=True), half_index, 1, keepdims=False
        )
        inner_prod = lax.dot_general(
            row_x,
            fold_column_x,
            (((0,), (0,)), ((), ())),
            precision=lax.Precision.HIGHEST,
            preferred_element_type=jnp.float32,
        )
        col_sq = jnp.sum(fold_column_x * fold_column_x, axis=0)
        distance = jnp.sqrt(row_sq[:, None] + col_sq[None, :] - 2.0 * inner_prod + 1.0)
        ratios = weight * dis_tile / distance
        pull_term = lax.dot_general(
            weight - ratios,
            fold_column_x,
            (((1,), (1,)), ((), ())),
            precision=lax.Precision.HIGHEST,
            preferred_element_type=jnp.float32,
        )
        misfit = dis_tile - distance
        pull_sums = pull_term.reshape(halves, per_dev, coord_dims).transpose(0, 2, 1)
        weight_sum, ratio_sum, pull_share = (
            lax.psum_scatter(
                jnp.sum(weight, axis=1).reshape(halves, per_dev),
                "narrow",
                scatter_dimension=0,
                tiled=True,
            ),
            lax.psum_scatter(
                jnp.sum(ratios, axis=1).reshape(halves, per_dev),
                "narrow",
                scatter_dimension=0,
                tiled=True,
            ),
            lax.psum_scatter(pull_sums, "narrow", scatter_dimension=0, tiled=True),
        )
        own_coords = positions[:, 0, :]
        updated = (own_coords * (1.0 + ratio_sum[0]) + pull_share[0]) / (1.0 + weight_sum[0])
        positions = updated[:, None, :]
        numbers.append(
            lax.psum(jnp.sum(weight * misfit * misfit), ("wide", "narrow")) / denom_total
        )
    stress = jnp.stack(numbers)
    return (positions, stress)


def solution(mesh):
    def body(dissim, classes, coords):
        coord_dims, halves, per_dev = coords.shape
        points, devices = dissim.shape[2], mesh.shape["wide"]
        small = halves == 1 and mesh.shape["narrow"] == 1 and points * points <= MOST_PAIRS
        small = small and coord_dims == 2 * SUBLANES and 2 * per_dev <= LANES
        small = small and per_dev % SUBLANES == 0 and points % LANES == 0
        small = small and devices == 16
        return (small_body if small else distributed_body)(dissim, classes, coords)

    return jax.shard_map(
        body,
        mesh=mesh,
        in_specs=(
            P(None, ("grp", "wide"), "narrow"),
            P(None, ("grp", "wide"), "narrow"),
            P(None, "narrow", ("grp", "wide")),
        ),
        out_specs=(P(None, "narrow", ("grp", "wide")), P("grp")),
        check_vma=False,
    )
```

```python
import functools

import jax
import jax.numpy as jnp
from jax import lax
from jax.experimental import pallas as pl
from jax.experimental.pallas import tpu as pltpu
from jax.sharding import PartitionSpec as P

ITERS = 3
LANES = 128
MOST_PAIRS = 1 << 19


def class_weight(class_codes):
    return jnp.where(
        class_codes == 3,
        1.0,
        jnp.where(class_codes == 2, 0.5, jnp.where(class_codes == 1, 0.25, 0.0)),
    ).astype(jnp.float32)


def split_bf16(value, terms):
    parts = []
    for _ in range(terms):
        part = value.astype(jnp.bfloat16)
        parts.append(part)
        value = value - part.astype(jnp.float32)
    return parts


SUBLANES = 8
NT = (((1,), (1,)), ((), ()))
TN = (((0,), (0,)), ((), ()))
dot = functools.partial(lax.dot_general, preferred_element_type=jnp.float32)


def lane_sums(value):
    rows = jnp.sum(value, axis=0, keepdims=True)
    return sum(rows[:, i : i + LANES] for i in range(0, rows.shape[1], LANES))


def tile_spots(per_dev, points):
    return [
        (slice(row, row + SUBLANES), slice(column, column + LANES))
        for row in range(0, per_dev, SUBLANES)
        for column in range(0, points, LANES)
    ]


def pack_kernel(dis_hbm, cls_hbm, x_hbm, out_ref, dis_ref, cls_ref, x_ref, sems):
    copies = [
        pltpu.make_async_copy(src, dst, sems.at[i])
        for i, (src, dst) in enumerate(
            [(dis_hbm, dis_ref), (cls_hbm, cls_ref), (x_hbm, x_ref)]
        )
    ]
    for copy in copies:
        copy.start()
    for copy in copies:
        copy.wait()
    spots = tile_spots(*dis_ref.shape)
    for i, spot in enumerate(spots):
        out_ref[i] = dis_ref[spot]
        out_ref[len(spots) + i] = class_weight(cls_ref[spot])
    half, per_dev = x_ref.shape[0] // 2, x_ref.shape[1]
    pad = jnp.zeros((half, LANES - 2 * per_dev), jnp.float32)
    out_ref[2 * len(spots)] = jnp.concatenate([x_ref[:half], x_ref[half:], pad], axis=1)


def norm_rows(top, bottom, coord_dims):
    pad = jnp.zeros((coord_dims - 6, top[0].shape[1]), jnp.float32)
    rows = [p.astype(jnp.float32) for p in (*top, *bottom)]
    return jnp.concatenate([*rows, pad], axis=0).astype(jnp.bfloat16)


def left_side(x, parts):
    hi, mid, lo = (-2.0 * p for p in parts)
    norm = split_bf16(jnp.sum(x * x, axis=0, keepdims=True), 3)
    ones = [jnp.ones((3, x.shape[1]), jnp.bfloat16)]
    return jnp.concatenate([hi, hi, hi, mid, mid, lo, norm_rows(norm, ones, x.shape[0])], axis=0)


def right_side(x, parts):
    hi, mid, lo = parts
    norm = split_bf16(jnp.sum(x * x, axis=0, keepdims=True) + 1.0, 3)
    ones = [jnp.ones((3, x.shape[1]), jnp.bfloat16)]
    return jnp.concatenate([hi, mid, lo, hi, mid, hi, norm_rows(ones, norm, x.shape[0])], axis=0)


def inverse_weight(weight, ones):
    return 1.0 / (1.0 + dot(weight.astype(jnp.bfloat16), ones, NT).T[0:1])


def moved(x, sides, push, scale):
    coord_dims = x.shape[0]
    parts = jnp.concatenate(split_bf16(push, 2), axis=1)
    sums = dot(parts, jnp.concatenate([sides, sides], axis=1), NT).T
    pushed = sums[:coord_dims] + sums[coord_dims : 2 * coord_dims]
    return x + (x * sums[2 * coord_dims : 2 * coord_dims + 1] - pushed) * scale


def join_kernel(*refs):
    *block_refs, out_ref = refs
    size = block_refs[0].shape[0]
    for i, ref in enumerate(block_refs):
        out_ref[i * size : (i + 1) * size] = ref[...]


def group_kernel(offsets, per_dev, *refs):
    slot_refs = refs[: len(offsets)]
    out_ref, stress_ref, dis_ref, weight_ref = refs[len(offsets) :]
    points = dis_ref.shape[0]
    spots = tile_spots(per_dev, points)
    tiles = 2 * len(spots) + 1
    me = lax.axis_index("wide")
    shape = (per_dev, points)
    lanes = lax.broadcasted_iota(jnp.int32, shape, 1) - lax.broadcasted_iota(jnp.int32, shape, 0)
    blocks, order = [], []
    for group, ref in zip(offsets, slot_refs):
        for slot, offset in enumerate(group):
            base, first = slot * tiles, len(blocks) * per_dev
            blocks.append(ref[base + tiles - 1])
            order.append((lanes == (me ^ offset) * per_dev).astype(jnp.float32))
            for i, (rows, columns) in enumerate(spots):
                spot = slice(first + rows.start, first + rows.stop)
                dis_ref[spot, columns] = ref[base + i]
                weight_ref[spot, columns] = ref[base + len(spots) + i]
    order = jnp.concatenate(order, axis=0).astype(jnp.bfloat16)
    halves = [
        jnp.concatenate([t[:, low : low + per_dev] for t in blocks], axis=1)
        for low in (0, per_dev)
    ]
    x = jnp.concatenate(halves, axis=0)
    coord_dims = x.shape[0]
    ones = jnp.ones((coord_dims, points), jnp.bfloat16)
    scale = inverse_weight(weight_ref[...], ones)
    sums = [lane_sums(weight_ref[...] * dis_ref[...] * dis_ref[...])]
    for sweep in range(ITERS):
        parts = split_bf16(x, 3)
        ordered = dot(jnp.concatenate(parts, axis=0), order, (((1,), (0,)), ((), ())))
        ordered = [ordered[i * coord_dims : (i + 1) * coord_dims] for i in range(3)]
        columns = [part.astype(jnp.bfloat16) for part in ordered]
        sides = jnp.concatenate([columns[0], columns[1], ones], axis=0)
        square = dot(left_side(x, parts), right_side(sum(ordered), columns), TN)
        inverse = lax.rsqrt(square)
        misfit = dis_ref[...] - square * inverse
        weighted = weight_ref[...] * misfit
        sums.append(lane_sums(weighted * misfit))
        if sweep < ITERS - 1:
            x = moved(x, sides, weighted * inverse, scale)
    push = weighted[:per_dev] * inverse[:per_dev]
    out_ref[...] = moved(x[:, :per_dev], sides, push, scale[:, :per_dev])
    total = jnp.sum(jnp.concatenate(sums, axis=0), axis=1, keepdims=True)
    ratios = total[1:] / total[:1]
    lanes = lax.broadcasted_iota(jnp.int32, (ITERS, LANES), 1)
    lined = jnp.where(lanes == lax.broadcasted_iota(jnp.int32, (ITERS, LANES), 0), ratios, 0.0)
    stress_ref[...] = jnp.sum(lined, axis=0, keepdims=True)[:, :ITERS]


def small_body(dissim, classes, coords):
    coord_dims, _, per_dev = coords.shape
    points = dissim.shape[2]
    devices = points // per_dev
    vmem = pl.BlockSpec(memory_space=pltpu.VMEM)
    hbm = pl.BlockSpec(memory_space=pltpu.HBM)
    f32 = functools.partial(jax.ShapeDtypeStruct, dtype=jnp.float32)
    params = pltpu.CompilerParams(vmem_limit_bytes=16 << 20)

    def swap(value, offset):
        return lax.ppermute(value, "wide", [(i, i ^ offset) for i in range(devices)])

    tiles = 2 * len(tile_spots(per_dev, points)) + 1
    inputs = (dissim[0], classes[0], coords[:, 0, :])
    packed = pl.pallas_call(
        pack_kernel,
        out_shape=f32((tiles, SUBLANES, LANES)),
        in_specs=[hbm] * 3,
        out_specs=vmem,
        scratch_shapes=[
            pltpu.VMEM((per_dev, points), jnp.float32),
            pltpu.VMEM((per_dev, points), jnp.int32),
            pltpu.VMEM((coord_dims, per_dev), jnp.float32),
            pltpu.SemaphoreType.DMA((3,)),
        ],
        compiler_params=params,
        name="pack",
    )(*(pltpu.with_memory_space_constraint(array, pltpu.HBM) for array in inputs))
    far, near, side = devices // 2, devices // 4, devices // 8
    held = {0: packed}
    for offset in (far, side, near, far | near | side):
        held[offset] = swap(packed, offset)
    for source, step in ((far, near), (far, side), (side, near)):
        held[source | step] = swap(held[source], step)
    early = [0, far, near, side]
    late = [offset for offset in held if offset not in early]
    block = packed.shape[0]

    def join(group, flops):
        return pl.pallas_call(
            join_kernel,
            out_shape=f32((len(group) * block, SUBLANES, LANES)),
            in_specs=[vmem] * len(group),
            out_specs=vmem,
            compiler_params=params,
            cost_estimate=pl.CostEstimate(flops=flops, bytes_accessed=0, transcendentals=0),
            name="join",
        )(*(held[offset] for offset in group))

    first, second = join(early, 1), join(late, 1)
    slots = [first, swap(first, 1), second, swap(second, 1)]
    offsets = [early, [o ^ 1 for o in early], late, [o ^ 1 for o in late]]
    final, stress = pl.pallas_call(
        functools.partial(group_kernel, offsets, per_dev),
        out_shape=(f32((coord_dims, per_dev)), f32((1, ITERS))),
        in_specs=[vmem] * len(slots),
        out_specs=(vmem, vmem),
        scratch_shapes=[
            pltpu.VMEM((points, points), jnp.float32),
            pltpu.VMEM((points, points), jnp.float32),
        ],
        compiler_params=params,
        name="group_smacof",
    )(*slots)
    return (final[:, None, :], stress[0])


def distributed_body(dissim, classes, coords):
    halves = dissim.shape[0]
    per_dev = dissim.shape[1]
    columns = dissim.shape[2]
    coord_dims = coords.shape[0]
    row_count = halves * per_dev
    dis_tile = dissim.reshape(row_count, columns)
    weight = class_weight(classes.reshape(row_count, columns))
    denom_local = jnp.sum(weight * dis_tile * dis_tile)
    half_index = lax.axis_index("narrow")
    denom_total = lax.psum(denom_local, ("wide", "narrow"))
    positions = coords
    numbers = []
    for sweep in range(ITERS):
        row_points = lax.all_gather(positions, "narrow", axis=1, tiled=True)
        row_x = row_points.reshape(coord_dims, row_count)
        row_sq = jnp.sum(row_x * row_x, axis=0)
        fold_column_x = lax.dynamic_index_in_dim(
            lax.all_gather(row_points, "wide", axis=2, tiled=True), half_index, 1, keepdims=False
        )
        inner_prod = lax.dot_general(
            row_x,
            fold_column_x,
            (((0,), (0,)), ((), ())),
            precision=lax.Precision.HIGHEST,
            preferred_element_type=jnp.float32,
        )
        col_sq = jnp.sum(fold_column_x * fold_column_x, axis=0)
        distance = jnp.sqrt(row_sq[:, None] + col_sq[None, :] - 2.0 * inner_prod + 1.0)
        ratios = weight * dis_tile / distance
        pull_term = lax.dot_general(
            weight - ratios,
            fold_column_x,
            (((1,), (1,)), ((), ())),
            precision=lax.Precision.HIGHEST,
            preferred_element_type=jnp.float32,
        )
        misfit = dis_tile - distance
        pull_sums = pull_term.reshape(halves, per_dev, coord_dims).transpose(0, 2, 1)
        weight_sum, ratio_sum, pull_share = (
            lax.psum_scatter(
                jnp.sum(weight, axis=1).reshape(halves, per_dev),
                "narrow",
                scatter_dimension=0,
                tiled=True,
            ),
            lax.psum_scatter(
                jnp.sum(ratios, axis=1).reshape(halves, per_dev),
                "narrow",
                scatter_dimension=0,
                tiled=True,
            ),
            lax.psum_scatter(pull_sums, "narrow", scatter_dimension=0, tiled=True),
        )
        own_coords = positions[:, 0, :]
        updated = (own_coords * (1.0 + ratio_sum[0]) + pull_share[0]) / (1.0 + weight_sum[0])
        positions = updated[:, None, :]
        numbers.append(
            lax.psum(jnp.sum(weight * misfit * misfit), ("wide", "narrow")) / denom_total
        )
    stress = jnp.stack(numbers)
    return (positions, stress)


def solution(mesh):
    def body(dissim, classes, coords):
        coord_dims, halves, per_dev = coords.shape
        points, devices = dissim.shape[2], mesh.shape["wide"]
        small = halves == 1 and mesh.shape["narrow"] == 1 and points * points <= MOST_PAIRS
        small = small and coord_dims == 2 * SUBLANES and 2 * per_dev <= LANES
        small = small and per_dev % SUBLANES == 0 and points % LANES == 0
        small = small and devices == 16
        return (small_body if small else distributed_body)(dissim, classes, coords)

    return jax.shard_map(
        body,
        mesh=mesh,
        in_specs=(
            P(None, ("grp", "wide"), "narrow"),
            P(None, ("grp", "wide"), "narrow"),
            P(None, "narrow", ("grp", "wide")),
        ),
        out_specs=(P(None, "narrow", ("grp", "wide")), P("grp")),
        check_vma=False,
    )
```

```python
import functools

import jax
import jax.numpy as jnp
from jax import lax
from jax.experimental import pallas as pl
from jax.experimental.pallas import tpu as pltpu
from jax.sharding import PartitionSpec as P

ITERS = 3
LANES = 128
MOST_PAIRS = 1 << 19


def class_weight(class_codes):
    return jnp.where(
        class_codes == 3,
        1.0,
        jnp.where(class_codes == 2, 0.5, jnp.where(class_codes == 1, 0.25, 0.0)),
    ).astype(jnp.float32)


def split_bf16(value, terms):
    parts = []
    for _ in range(terms):
        part = value.astype(jnp.bfloat16)
        parts.append(part)
        value = value - part.astype(jnp.float32)
    return parts


SUBLANES = 8
NT = (((1,), (1,)), ((), ()))
TN = (((0,), (0,)), ((), ()))
dot = functools.partial(lax.dot_general, preferred_element_type=jnp.float32)


def lane_sums(value):
    rows = jnp.sum(value, axis=0, keepdims=True)
    return sum(rows[:, i : i + LANES] for i in range(0, rows.shape[1], LANES))


def tile_spots(per_dev, points):
    return [
        (slice(row, row + SUBLANES), slice(column, column + LANES))
        for row in range(0, per_dev, SUBLANES)
        for column in range(0, points, LANES)
    ]


def pack_kernel(dis_hbm, cls_hbm, x_hbm, out_ref, dis_ref, cls_ref, x_ref, sems):
    copies = [
        pltpu.make_async_copy(src, dst, sems.at[i])
        for i, (src, dst) in enumerate(
            [(dis_hbm, dis_ref), (cls_hbm, cls_ref), (x_hbm, x_ref)]
        )
    ]
    for copy in copies:
        copy.start()
    for copy in copies:
        copy.wait()
    spots = tile_spots(*dis_ref.shape)
    for i, spot in enumerate(spots):
        out_ref[i] = dis_ref[spot]
        out_ref[len(spots) + i] = class_weight(cls_ref[spot])
    half, per_dev = x_ref.shape[0] // 2, x_ref.shape[1]
    pad = jnp.zeros((half, LANES - 2 * per_dev), jnp.float32)
    out_ref[2 * len(spots)] = jnp.concatenate([x_ref[:half], x_ref[half:], pad], axis=1)


def held_slots(offsets, refs, tiles):
    me = lax.axis_index("wide")
    for group, ref in zip(offsets, refs):
        for slot, offset in enumerate(group):
            yield ref, slot * tiles, me ^ offset


def norm_rows(top, bottom, coord_dims):
    pad = jnp.zeros((coord_dims - 6, top[0].shape[1]), jnp.float32)
    rows = [p.astype(jnp.float32) for p in (*top, *bottom)]
    return jnp.concatenate([*rows, pad], axis=0).astype(jnp.bfloat16)


def left_side(x, parts):
    hi, mid, lo = (-2.0 * p for p in parts)
    norm = split_bf16(jnp.sum(x * x, axis=0, keepdims=True), 3)
    ones = [jnp.ones((3, x.shape[1]), jnp.bfloat16)]
    return jnp.concatenate([hi, hi, hi, mid, mid, lo, norm_rows(norm, ones, x.shape[0])], axis=0)


def right_side(x, parts):
    hi, mid, lo = parts
    norm = split_bf16(jnp.sum(x * x, axis=0, keepdims=True) + 1.0, 3)
    ones = [jnp.ones((3, x.shape[1]), jnp.bfloat16)]
    return jnp.concatenate([hi, mid, lo, hi, mid, hi, norm_rows(ones, norm, x.shape[0])], axis=0)


def inverse_weight(weight, ones):
    return 1.0 / (1.0 + dot(weight.astype(jnp.bfloat16), ones, NT).T[0:1])


def moved(x, sides, push, scale):
    coord_dims = x.shape[0]
    parts = jnp.concatenate(split_bf16(push, 2), axis=1)
    sums = dot(parts, jnp.concatenate([sides, sides], axis=1), NT).T
    pushed = sums[:coord_dims] + sums[coord_dims : 2 * coord_dims]
    return x + (x * sums[2 * coord_dims : 2 * coord_dims + 1] - pushed) * scale


def join_kernel(*refs):
    *block_refs, out_ref = refs
    size = block_refs[0].shape[0]
    for i, ref in enumerate(block_refs):
        out_ref[i * size : (i + 1) * size] = ref[...]


def group_kernel(offsets, per_dev, *refs):
    slot_refs = refs[: len(offsets)]
    out_ref, stress_ref, dis_ref, weight_ref, tile_ref = refs[len(offsets) :]
    points = dis_ref.shape[0]
    spots = tile_spots(per_dev, points)
    tiles = 2 * len(spots) + 1
    for ref, base, place in held_slots(offsets, slot_refs, tiles):
        tile_ref[place] = ref[base + tiles - 1]
        for i, (rows, columns) in enumerate(spots):
            start = pl.multiple_of(place * per_dev + rows.start, SUBLANES)
            dis_ref[pl.ds(start, SUBLANES), columns] = ref[base + i]
            weight_ref[pl.ds(start, SUBLANES), columns] = ref[base + len(spots) + i]
    blocks = [tile_ref[i] for i in range(tile_ref.shape[0])]
    halves = [
        jnp.concatenate([t[:, low : low + per_dev] for t in blocks], axis=1)
        for low in (0, per_dev)
    ]
    x = jnp.concatenate(halves, axis=0)
    coord_dims = x.shape[0]
    chunks = [slice(row, row + LANES) for row in range(0, points, LANES)]
    ones = jnp.ones((coord_dims, points), jnp.bfloat16)
    scales = [inverse_weight(weight_ref[rows], ones) for rows in chunks]
    denom = sum(lane_sums(weight_ref[rows] * dis_ref[rows] * dis_ref[rows]) for rows in chunks)
    place = lax.axis_index("wide")
    own_rows = pl.ds(pl.multiple_of(place * per_dev, SUBLANES), per_dev)
    shape = (points, per_dev)
    pick = lax.broadcasted_iota(jnp.int32, shape, 0) - lax.broadcasted_iota(jnp.int32, shape, 1)
    pick = (pick == place * per_dev).astype(jnp.float32).astype(jnp.bfloat16)
    sums = [denom]
    for sweep in range(ITERS):
        parts = split_bf16(x, 3)
        sides = jnp.concatenate([parts[0], parts[1], ones], axis=0)
        left, right = left_side(x, parts), right_side(x, parts)
        last = sweep == ITERS - 1
        stress, following = 0.0, []
        for rows, scale in zip(chunks, scales):
            square = dot(left[:, rows], right, TN)
            inverse = lax.rsqrt(square)
            weight, dis = weight_ref[rows], dis_ref[rows]
            misfit = dis - square * inverse
            weighted = weight * misfit
            stress += lane_sums(weighted * misfit)
            if not last:
                following.append(moved(x[:, rows], sides, weighted * inverse, scale))
        sums.append(stress)
        if last:
            own = dot(jnp.concatenate(parts, axis=0), pick, (((1,), (0,)), ((), ())))
            own = sum(own[i * coord_dims : (i + 1) * coord_dims] for i in range(3))
            square = dot(left_side(own, split_bf16(own, 3)), right, TN)
            inverse = lax.rsqrt(square)
            weight = weight_ref[own_rows, :]
            push = weight * (dis_ref[own_rows, :] - square * inverse) * inverse
            out_ref[...] = moved(own, sides, push, inverse_weight(weight, ones))
        else:
            x = jnp.concatenate(following, axis=1)
    total = jnp.sum(jnp.concatenate(sums, axis=0), axis=1, keepdims=True)
    ratios = total[1:] / total[:1]
    lanes = lax.broadcasted_iota(jnp.int32, (ITERS, LANES), 1)
    lined = jnp.where(lanes == lax.broadcasted_iota(jnp.int32, (ITERS, LANES), 0), ratios, 0.0)
    stress_ref[...] = jnp.sum(lined, axis=0, keepdims=True)[:, :ITERS]


def small_body(dissim, classes, coords):
    coord_dims, _, per_dev = coords.shape
    points = dissim.shape[2]
    devices = points // per_dev
    vmem = pl.BlockSpec(memory_space=pltpu.VMEM)
    hbm = pl.BlockSpec(memory_space=pltpu.HBM)
    f32 = functools.partial(jax.ShapeDtypeStruct, dtype=jnp.float32)
    params = pltpu.CompilerParams(vmem_limit_bytes=16 << 20)

    def swap(value, offset):
        return lax.ppermute(value, "wide", [(i, i ^ offset) for i in range(devices)])

    tiles = 2 * len(tile_spots(per_dev, points)) + 1
    inputs = (dissim[0], classes[0], coords[:, 0, :])
    packed = pl.pallas_call(
        pack_kernel,
        out_shape=f32((tiles, SUBLANES, LANES)),
        in_specs=[hbm] * 3,
        out_specs=vmem,
        scratch_shapes=[
            pltpu.VMEM((per_dev, points), jnp.float32),
            pltpu.VMEM((per_dev, points), jnp.int32),
            pltpu.VMEM((coord_dims, per_dev), jnp.float32),
            pltpu.SemaphoreType.DMA((3,)),
        ],
        compiler_params=params,
        name="pack",
    )(*(pltpu.with_memory_space_constraint(array, pltpu.HBM) for array in inputs))
    far, near, side = devices // 2, devices // 4, devices // 8
    held = {0: packed}
    for offset in (far, near, side, far | near | side):
        held[offset] = swap(packed, offset)
    for source, step in ((far, side), (far, near), (near, side)):
        held[source | step] = swap(held[source], step)
    early = [0, far, side, near]
    late = [offset for offset in held if offset not in early]
    block = packed.shape[0]

    def join(group, flops):
        return pl.pallas_call(
            join_kernel,
            out_shape=f32((len(group) * block, SUBLANES, LANES)),
            in_specs=[vmem] * len(group),
            out_specs=vmem,
            compiler_params=params,
            cost_estimate=pl.CostEstimate(flops=flops, bytes_accessed=0, transcendentals=0),
            name="join",
        )(*(held[offset] for offset in group))

    first, second = join(early, 1), join(late, 1)
    slots = [first, swap(first, 1), second, swap(second, 1)]
    offsets = [early, [o ^ 1 for o in early], late, [o ^ 1 for o in late]]
    final, stress = pl.pallas_call(
        functools.partial(group_kernel, offsets, per_dev),
        out_shape=(f32((coord_dims, per_dev)), f32((1, ITERS))),
        in_specs=[vmem] * len(slots),
        out_specs=(vmem, vmem),
        scratch_shapes=[
            pltpu.VMEM((points, points), jnp.float32),
            pltpu.VMEM((points, points), jnp.float32),
            pltpu.VMEM((devices, SUBLANES, LANES), jnp.float32),
        ],
        compiler_params=params,
        name="group_smacof",
    )(*slots)
    return (final[:, None, :], stress[0])


def distributed_body(dissim, classes, coords):
    halves = dissim.shape[0]
    per_dev = dissim.shape[1]
    columns = dissim.shape[2]
    coord_dims = coords.shape[0]
    row_count = halves * per_dev
    dis_tile = dissim.reshape(row_count, columns)
    weight = class_weight(classes.reshape(row_count, columns))
    denom_local = jnp.sum(weight * dis_tile * dis_tile)
    half_index = lax.axis_index("narrow")
    denom_total = lax.psum(denom_local, ("wide", "narrow"))
    positions = coords
    numbers = []
    for sweep in range(ITERS):
        row_points = lax.all_gather(positions, "narrow", axis=1, tiled=True)
        row_x = row_points.reshape(coord_dims, row_count)
        row_sq = jnp.sum(row_x * row_x, axis=0)
        fold_column_x = lax.dynamic_index_in_dim(
            lax.all_gather(row_points, "wide", axis=2, tiled=True), half_index, 1, keepdims=False
        )
        inner_prod = lax.dot_general(
            row_x,
            fold_column_x,
            (((0,), (0,)), ((), ())),
            precision=lax.Precision.HIGHEST,
            preferred_element_type=jnp.float32,
        )
        col_sq = jnp.sum(fold_column_x * fold_column_x, axis=0)
        distance = jnp.sqrt(row_sq[:, None] + col_sq[None, :] - 2.0 * inner_prod + 1.0)
        ratios = weight * dis_tile / distance
        pull_term = lax.dot_general(
            weight - ratios,
            fold_column_x,
            (((1,), (1,)), ((), ())),
            precision=lax.Precision.HIGHEST,
            preferred_element_type=jnp.float32,
        )
        misfit = dis_tile - distance
        pull_sums = pull_term.reshape(halves, per_dev, coord_dims).transpose(0, 2, 1)
        weight_sum, ratio_sum, pull_share = (
            lax.psum_scatter(
                jnp.sum(weight, axis=1).reshape(halves, per_dev),
                "narrow",
                scatter_dimension=0,
                tiled=True,
            ),
            lax.psum_scatter(
                jnp.sum(ratios, axis=1).reshape(halves, per_dev),
                "narrow",
                scatter_dimension=0,
                tiled=True,
            ),
            lax.psum_scatter(pull_sums, "narrow", scatter_dimension=0, tiled=True),
        )
        own_coords = positions[:, 0, :]
        updated = (own_coords * (1.0 + ratio_sum[0]) + pull_share[0]) / (1.0 + weight_sum[0])
        positions = updated[:, None, :]
        numbers.append(
            lax.psum(jnp.sum(weight * misfit * misfit), ("wide", "narrow")) / denom_total
        )
    stress = jnp.stack(numbers)
    return (positions, stress)


def solution(mesh):
    def body(dissim, classes, coords):
        coord_dims, halves, per_dev = coords.shape
        points, devices = dissim.shape[2], mesh.shape["wide"]
        small = halves == 1 and mesh.shape["narrow"] == 1 and points * points <= MOST_PAIRS
        small = small and coord_dims == 2 * SUBLANES and 2 * per_dev <= LANES
        small = small and per_dev % SUBLANES == 0 and points % LANES == 0
        small = small and devices == 16
        return (small_body if small else distributed_body)(dissim, classes, coords)

    return jax.shard_map(
        body,
        mesh=mesh,
        in_specs=(
            P(None, ("grp", "wide"), "narrow"),
            P(None, ("grp", "wide"), "narrow"),
            P(None, "narrow", ("grp", "wide")),
        ),
        out_specs=(P(None, "narrow", ("grp", "wide")), P("grp")),
        check_vma=False,
    )
```

```python
import functools

import jax
import jax.numpy as jnp
from jax import lax
from jax.experimental import pallas as pl
from jax.experimental.pallas import tpu as pltpu
from jax.sharding import PartitionSpec as P

ITERS = 3
LANES = 128
MOST_PAIRS = 1 << 19


def class_weight(class_codes):
    return jnp.where(
        class_codes == 3,
        1.0,
        jnp.where(class_codes == 2, 0.5, jnp.where(class_codes == 1, 0.25, 0.0)),
    ).astype(jnp.float32)


def split_bf16(value, terms):
    parts = []
    for _ in range(terms):
        part = value.astype(jnp.bfloat16)
        parts.append(part)
        value = value - part.astype(jnp.float32)
    return parts


SUBLANES = 8
NT = (((1,), (1,)), ((), ()))
TN = (((0,), (0,)), ((), ()))
dot = functools.partial(lax.dot_general, preferred_element_type=jnp.float32)


def lane_sums(value):
    rows = jnp.sum(value, axis=0, keepdims=True)
    return sum(rows[:, i : i + LANES] for i in range(0, rows.shape[1], LANES))


def tile_spots(per_dev, points):
    return [
        (slice(row, row + SUBLANES), slice(column, column + LANES))
        for row in range(0, per_dev, SUBLANES)
        for column in range(0, points, LANES)
    ]


def pack_kernel(dis_hbm, cls_hbm, x_hbm, out_ref, dis_ref, cls_ref, x_ref, sems):
    copies = [
        pltpu.make_async_copy(src, dst, sems.at[i])
        for i, (src, dst) in enumerate(
            [(dis_hbm, dis_ref), (cls_hbm, cls_ref), (x_hbm, x_ref)]
        )
    ]
    for copy in copies:
        copy.start()
    for copy in copies:
        copy.wait()
    spots = tile_spots(*dis_ref.shape)
    for i, spot in enumerate(spots):
        out_ref[i] = dis_ref[spot]
        out_ref[len(spots) + i] = class_weight(cls_ref[spot])
    half, per_dev = x_ref.shape[0] // 2, x_ref.shape[1]
    pad = jnp.zeros((half, LANES - 2 * per_dev), jnp.float32)
    out_ref[2 * len(spots)] = jnp.concatenate([x_ref[:half], x_ref[half:], pad], axis=1)


def held_slots(offsets, refs, tiles):
    me = lax.axis_index("wide")
    for group, ref in zip(offsets, refs):
        for slot, offset in enumerate(group):
            yield ref, slot * tiles, me ^ offset


def norm_rows(top, bottom, coord_dims):
    pad = jnp.zeros((coord_dims - 6, top[0].shape[1]), jnp.float32)
    rows = [p.astype(jnp.float32) for p in (*top, *bottom)]
    return jnp.concatenate([*rows, pad], axis=0).astype(jnp.bfloat16)


def left_side(x, parts):
    hi, mid, lo = (-2.0 * p for p in parts)
    norm = split_bf16(jnp.sum(x * x, axis=0, keepdims=True), 3)
    ones = [jnp.ones((3, x.shape[1]), jnp.bfloat16)]
    return jnp.concatenate([hi, hi, hi, mid, mid, lo, norm_rows(norm, ones, x.shape[0])], axis=0)


def right_side(x, parts):
    hi, mid, lo = parts
    norm = split_bf16(jnp.sum(x * x, axis=0, keepdims=True) + 1.0, 3)
    ones = [jnp.ones((3, x.shape[1]), jnp.bfloat16)]
    return jnp.concatenate([hi, mid, lo, hi, mid, hi, norm_rows(ones, norm, x.shape[0])], axis=0)


def inverse_weight(weight, ones):
    return 1.0 / (1.0 + dot(weight.astype(jnp.bfloat16), ones, NT).T[0:1])


def moved(x, sides, push, scale):
    coord_dims = x.shape[0]
    parts = jnp.concatenate(split_bf16(push, 2), axis=1)
    sums = dot(parts, jnp.concatenate([sides, sides], axis=1), NT).T
    pushed = sums[:coord_dims] + sums[coord_dims : 2 * coord_dims]
    return x + (x * sums[2 * coord_dims : 2 * coord_dims + 1] - pushed) * scale


def join_kernel(*refs):
    *block_refs, out_ref = refs
    size = block_refs[0].shape[0]
    for i, ref in enumerate(block_refs):
        out_ref[i * size : (i + 1) * size] = ref[...]


def group_kernel(offsets, per_dev, *refs):
    slot_refs = refs[: len(offsets)]
    out_ref, stress_ref, dis_ref, weight_ref, tile_ref = refs[len(offsets) :]
    points = dis_ref.shape[0]
    spots = tile_spots(per_dev, points)
    tiles = 2 * len(spots) + 1
    for ref, base, place in held_slots(offsets, slot_refs, tiles):
        tile_ref[place] = ref[base + tiles - 1]
        for i, (rows, columns) in enumerate(spots):
            start = pl.multiple_of(place * per_dev + rows.start, SUBLANES)
            dis_ref[pl.ds(start, SUBLANES), columns] = ref[base + i]
            weight_ref[pl.ds(start, SUBLANES), columns] = ref[base + len(spots) + i]
    blocks = [tile_ref[i] for i in range(tile_ref.shape[0])]
    halves = [
        jnp.concatenate([t[:, low : low + per_dev] for t in blocks], axis=1)
        for low in (0, per_dev)
    ]
    x = jnp.concatenate(halves, axis=0)
    coord_dims = x.shape[0]
    chunks = [slice(row, row + LANES) for row in range(0, points, LANES)]
    ones = jnp.ones((coord_dims, points), jnp.bfloat16)
    scales = [inverse_weight(weight_ref[rows], ones) for rows in chunks]
    denom = sum(lane_sums(weight_ref[rows] * dis_ref[rows] * dis_ref[rows]) for rows in chunks)
    place = lax.axis_index("wide")
    own_rows = pl.ds(pl.multiple_of(place * per_dev, SUBLANES), per_dev)
    shape = (points, per_dev)
    pick = lax.broadcasted_iota(jnp.int32, shape, 0) - lax.broadcasted_iota(jnp.int32, shape, 1)
    pick = (pick == place * per_dev).astype(jnp.float32).astype(jnp.bfloat16)
    sums = [denom]
    for sweep in range(ITERS):
        parts = split_bf16(x, 3)
        sides = jnp.concatenate([parts[0], parts[1], ones], axis=0)
        left, right = left_side(x, parts), right_side(x, parts)
        last = sweep == ITERS - 1
        stress, following = 0.0, []
        for rows, scale in zip(chunks, scales):
            square = dot(left[:, rows], right, TN)
            inverse = lax.rsqrt(square)
            weight, dis = weight_ref[rows], dis_ref[rows]
            misfit = dis - square * inverse
            weighted = weight * misfit
            stress += lane_sums(weighted * misfit)
            if not last:
                following.append(moved(x[:, rows], sides, weighted * inverse, scale))
        sums.append(stress)
        if last:
            own = dot(jnp.concatenate(parts, axis=0), pick, (((1,), (0,)), ((), ())))
            own = sum(own[i * coord_dims : (i + 1) * coord_dims] for i in range(3))
            square = dot(left_side(own, split_bf16(own, 3)), right, TN)
            inverse = lax.rsqrt(square)
            weight = weight_ref[own_rows, :]
            push = weight * (dis_ref[own_rows, :] - square * inverse) * inverse
            out_ref[...] = moved(own, sides, push, inverse_weight(weight, ones))
        else:
            x = jnp.concatenate(following, axis=1)
    total = jnp.sum(jnp.concatenate(sums, axis=0), axis=1, keepdims=True)
    ratios = total[1:] / total[:1]
    lanes = lax.broadcasted_iota(jnp.int32, (ITERS, LANES), 1)
    lined = jnp.where(lanes == lax.broadcasted_iota(jnp.int32, (ITERS, LANES), 0), ratios, 0.0)
    stress_ref[...] = jnp.sum(lined, axis=0, keepdims=True)[:, :ITERS]


def small_body(dissim, classes, coords):
    coord_dims, _, per_dev = coords.shape
    points = dissim.shape[2]
    devices = points // per_dev
    vmem = pl.BlockSpec(memory_space=pltpu.VMEM)
    hbm = pl.BlockSpec(memory_space=pltpu.HBM)
    f32 = functools.partial(jax.ShapeDtypeStruct, dtype=jnp.float32)
    params = pltpu.CompilerParams(vmem_limit_bytes=16 << 20)

    def swap(value, offset):
        return lax.ppermute(value, "wide", [(i, i ^ offset) for i in range(devices)])

    tiles = 2 * len(tile_spots(per_dev, points)) + 1
    inputs = (dissim[0], classes[0], coords[:, 0, :])
    packed = pl.pallas_call(
        pack_kernel,
        out_shape=f32((tiles, SUBLANES, LANES)),
        in_specs=[hbm] * 3,
        out_specs=vmem,
        scratch_shapes=[
            pltpu.VMEM((per_dev, points), jnp.float32),
            pltpu.VMEM((per_dev, points), jnp.int32),
            pltpu.VMEM((coord_dims, per_dev), jnp.float32),
            pltpu.SemaphoreType.DMA((3,)),
        ],
        compiler_params=params,
        name="pack",
    )(*(pltpu.with_memory_space_constraint(array, pltpu.HBM) for array in inputs))
    far, near, side = devices // 2, devices // 4, devices // 8
    held = {0: packed}
    for offset in (far, near, side, far | near | side):
        held[offset] = swap(packed, offset)
    for source, step in ((far, near), (far, side), (near, side)):
        held[source | step] = swap(held[source], step)
    early = [0, far, side, near]
    late = [offset for offset in held if offset not in early]
    block = packed.shape[0]

    def join(group, flops):
        return pl.pallas_call(
            join_kernel,
            out_shape=f32((len(group) * block, SUBLANES, LANES)),
            in_specs=[vmem] * len(group),
            out_specs=vmem,
            compiler_params=params,
            cost_estimate=pl.CostEstimate(flops=flops, bytes_accessed=0, transcendentals=0),
            name="join",
        )(*(held[offset] for offset in group))

    first, second = join(early, 1), join(late, 1)
    slots = [first, swap(first, 1), second, swap(second, 1)]
    offsets = [early, [o ^ 1 for o in early], late, [o ^ 1 for o in late]]
    final, stress = pl.pallas_call(
        functools.partial(group_kernel, offsets, per_dev),
        out_shape=(f32((coord_dims, per_dev)), f32((1, ITERS))),
        in_specs=[vmem] * len(slots),
        out_specs=(vmem, vmem),
        scratch_shapes=[
            pltpu.VMEM((points, points), jnp.float32),
            pltpu.VMEM((points, points), jnp.float32),
            pltpu.VMEM((devices, SUBLANES, LANES), jnp.float32),
        ],
        compiler_params=params,
        name="group_smacof",
    )(*slots)
    return (final[:, None, :], stress[0])


def distributed_body(dissim, classes, coords):
    halves = dissim.shape[0]
    per_dev = dissim.shape[1]
    columns = dissim.shape[2]
    coord_dims = coords.shape[0]
    row_count = halves * per_dev
    dis_tile = dissim.reshape(row_count, columns)
    weight = class_weight(classes.reshape(row_count, columns))
    denom_local = jnp.sum(weight * dis_tile * dis_tile)
    half_index = lax.axis_index("narrow")
    denom_total = lax.psum(denom_local, ("wide", "narrow"))
    positions = coords
    numbers = []
    for sweep in range(ITERS):
        row_points = lax.all_gather(positions, "narrow", axis=1, tiled=True)
        row_x = row_points.reshape(coord_dims, row_count)
        row_sq = jnp.sum(row_x * row_x, axis=0)
        fold_column_x = lax.dynamic_index_in_dim(
            lax.all_gather(row_points, "wide", axis=2, tiled=True), half_index, 1, keepdims=False
        )
        inner_prod = lax.dot_general(
            row_x,
            fold_column_x,
            (((0,), (0,)), ((), ())),
            precision=lax.Precision.HIGHEST,
            preferred_element_type=jnp.float32,
        )
        col_sq = jnp.sum(fold_column_x * fold_column_x, axis=0)
        distance = jnp.sqrt(row_sq[:, None] + col_sq[None, :] - 2.0 * inner_prod + 1.0)
        ratios = weight * dis_tile / distance
        pull_term = lax.dot_general(
            weight - ratios,
            fold_column_x,
            (((1,), (1,)), ((), ())),
            precision=lax.Precision.HIGHEST,
            preferred_element_type=jnp.float32,
        )
        misfit = dis_tile - distance
        pull_sums = pull_term.reshape(halves, per_dev, coord_dims).transpose(0, 2, 1)
        weight_sum, ratio_sum, pull_share = (
            lax.psum_scatter(
                jnp.sum(weight, axis=1).reshape(halves, per_dev),
                "narrow",
                scatter_dimension=0,
                tiled=True,
            ),
            lax.psum_scatter(
                jnp.sum(ratios, axis=1).reshape(halves, per_dev),
                "narrow",
                scatter_dimension=0,
                tiled=True,
            ),
            lax.psum_scatter(pull_sums, "narrow", scatter_dimension=0, tiled=True),
        )
        own_coords = positions[:, 0, :]
        updated = (own_coords * (1.0 + ratio_sum[0]) + pull_share[0]) / (1.0 + weight_sum[0])
        positions = updated[:, None, :]
        numbers.append(
            lax.psum(jnp.sum(weight * misfit * misfit), ("wide", "narrow")) / denom_total
        )
    stress = jnp.stack(numbers)
    return (positions, stress)


def solution(mesh):
    def body(dissim, classes, coords):
        coord_dims, halves, per_dev = coords.shape
        points, devices = dissim.shape[2], mesh.shape["wide"]
        small = halves == 1 and mesh.shape["narrow"] == 1 and points * points <= MOST_PAIRS
        small = small and coord_dims == 2 * SUBLANES and 2 * per_dev <= LANES
        small = small and per_dev % SUBLANES == 0 and points % LANES == 0
        small = small and devices == 16
        return (small_body if small else distributed_body)(dissim, classes, coords)

    return jax.shard_map(
        body,
        mesh=mesh,
        in_specs=(
            P(None, ("grp", "wide"), "narrow"),
            P(None, ("grp", "wide"), "narrow"),
            P(None, "narrow", ("grp", "wide")),
        ),
        out_specs=(P(None, "narrow", ("grp", "wide")), P("grp")),
        check_vma=False,
    )
```

```python
import functools

import jax
import jax.numpy as jnp
from jax import lax
from jax.experimental import pallas as pl
from jax.experimental.pallas import tpu as pltpu
from jax.sharding import PartitionSpec as P

ITERS = 3
LANES = 128
MOST_PAIRS = 1 << 19


def class_weight(class_codes):
    return jnp.where(
        class_codes == 3,
        1.0,
        jnp.where(class_codes == 2, 0.5, jnp.where(class_codes == 1, 0.25, 0.0)),
    ).astype(jnp.float32)


def split_bf16(value, terms):
    parts = []
    for _ in range(terms):
        part = value.astype(jnp.bfloat16)
        parts.append(part)
        value = value - part.astype(jnp.float32)
    return parts


SUBLANES = 8
NT = (((1,), (1,)), ((), ()))
TN = (((0,), (0,)), ((), ()))
dot = functools.partial(lax.dot_general, preferred_element_type=jnp.float32)


def lane_sums(value):
    rows = jnp.sum(value, axis=0, keepdims=True)
    return sum(rows[:, i : i + LANES] for i in range(0, rows.shape[1], LANES))


def tile_spots(per_dev, points):
    return [
        (slice(row, row + SUBLANES), slice(column, column + LANES))
        for row in range(0, per_dev, SUBLANES)
        for column in range(0, points, LANES)
    ]


def pack_kernel(dis_hbm, cls_hbm, x_hbm, out_ref, dis_ref, cls_ref, x_ref, sems):
    copies = [
        pltpu.make_async_copy(src, dst, sems.at[i])
        for i, (src, dst) in enumerate(
            [(dis_hbm, dis_ref), (cls_hbm, cls_ref), (x_hbm, x_ref)]
        )
    ]
    for copy in copies:
        copy.start()
    for copy in copies:
        copy.wait()
    spots = tile_spots(*dis_ref.shape)
    for i, spot in enumerate(spots):
        out_ref[i] = dis_ref[spot]
        out_ref[len(spots) + i] = class_weight(cls_ref[spot])
    half, per_dev = x_ref.shape[0] // 2, x_ref.shape[1]
    pad = jnp.zeros((half, LANES - 2 * per_dev), jnp.float32)
    out_ref[2 * len(spots)] = jnp.concatenate([x_ref[:half], x_ref[half:], pad], axis=1)


def held_slots(offsets, refs, tiles):
    me = lax.axis_index("wide")
    for group, ref in zip(offsets, refs):
        for slot, offset in enumerate(group):
            yield ref, slot * tiles, me ^ offset


def norm_rows(top, bottom, coord_dims):
    pad = jnp.zeros((coord_dims - 6, top[0].shape[1]), jnp.float32)
    rows = [p.astype(jnp.float32) for p in (*top, *bottom)]
    return jnp.concatenate([*rows, pad], axis=0).astype(jnp.bfloat16)


def left_side(x, parts):
    hi, mid, lo = (-2.0 * p for p in parts)
    norm = split_bf16(jnp.sum(x * x, axis=0, keepdims=True), 3)
    ones = [jnp.ones((3, x.shape[1]), jnp.bfloat16)]
    return jnp.concatenate([hi, hi, hi, mid, mid, lo, norm_rows(norm, ones, x.shape[0])], axis=0)


def right_side(x, parts):
    hi, mid, lo = parts
    norm = split_bf16(jnp.sum(x * x, axis=0, keepdims=True) + 1.0, 3)
    ones = [jnp.ones((3, x.shape[1]), jnp.bfloat16)]
    return jnp.concatenate([hi, mid, lo, hi, mid, hi, norm_rows(ones, norm, x.shape[0])], axis=0)


def inverse_weight(weight, ones):
    return 1.0 / (1.0 + dot(weight.astype(jnp.bfloat16), ones, NT).T[0:1])


def moved(x, sides, push, scale):
    coord_dims = x.shape[0]
    parts = jnp.concatenate(split_bf16(push, 2), axis=1)
    sums = dot(parts, jnp.concatenate([sides, sides], axis=1), NT).T
    pushed = sums[:coord_dims] + sums[coord_dims : 2 * coord_dims]
    return x + (x * sums[2 * coord_dims : 2 * coord_dims + 1] - pushed) * scale


def join_kernel(*refs):
    *block_refs, out_ref = refs
    size = block_refs[0].shape[0]
    for i, ref in enumerate(block_refs):
        out_ref[i * size : (i + 1) * size] = ref[...]


def group_kernel(offsets, per_dev, *refs):
    slot_refs = refs[: len(offsets)]
    out_ref, stress_ref, dis_ref, weight_ref, tile_ref = refs[len(offsets) :]
    points = dis_ref.shape[0]
    spots = tile_spots(per_dev, points)
    tiles = 2 * len(spots) + 1
    for ref, base, place in held_slots(offsets, slot_refs, tiles):
        tile_ref[place] = ref[base + tiles - 1]
        for i, (rows, columns) in enumerate(spots):
            start = pl.multiple_of(place * per_dev + rows.start, SUBLANES)
            dis_ref[pl.ds(start, SUBLANES), columns] = ref[base + i]
            weight_ref[pl.ds(start, SUBLANES), columns] = ref[base + len(spots) + i]
    blocks = [tile_ref[i] for i in range(tile_ref.shape[0])]
    halves = [
        jnp.concatenate([t[:, low : low + per_dev] for t in blocks], axis=1)
        for low in (0, per_dev)
    ]
    x = jnp.concatenate(halves, axis=0)
    coord_dims = x.shape[0]
    chunks = [slice(row, row + LANES) for row in range(0, points, LANES)]
    ones = jnp.ones((coord_dims, points), jnp.bfloat16)
    scales = [inverse_weight(weight_ref[rows], ones) for rows in chunks]
    denom = sum(lane_sums(weight_ref[rows] * dis_ref[rows] * dis_ref[rows]) for rows in chunks)
    place = lax.axis_index("wide")
    own_rows = pl.ds(pl.multiple_of(place * per_dev, SUBLANES), per_dev)
    shape = (points, per_dev)
    pick = lax.broadcasted_iota(jnp.int32, shape, 0) - lax.broadcasted_iota(jnp.int32, shape, 1)
    pick = (pick == place * per_dev).astype(jnp.float32).astype(jnp.bfloat16)
    sums = [denom]
    for sweep in range(ITERS):
        parts = split_bf16(x, 3)
        sides = jnp.concatenate([parts[0], parts[1], ones], axis=0)
        left, right = left_side(x, parts), right_side(x, parts)
        last = sweep == ITERS - 1
        stress, following = 0.0, []
        for rows, scale in zip(chunks, scales):
            square = dot(left[:, rows], right, TN)
            inverse = lax.rsqrt(square)
            weight, dis = weight_ref[rows], dis_ref[rows]
            misfit = dis - square * inverse
            weighted = weight * misfit
            stress += lane_sums(weighted * misfit)
            if not last:
                following.append(moved(x[:, rows], sides, weighted * inverse, scale))
        sums.append(stress)
        if last:
            own = dot(jnp.concatenate(parts, axis=0), pick, (((1,), (0,)), ((), ())))
            own = sum(own[i * coord_dims : (i + 1) * coord_dims] for i in range(3))
            square = dot(left_side(own, split_bf16(own, 3)), right, TN)
            inverse = lax.rsqrt(square)
            weight = weight_ref[own_rows, :]
            push = weight * (dis_ref[own_rows, :] - square * inverse) * inverse
            out_ref[...] = moved(own, sides, push, inverse_weight(weight, ones))
        else:
            x = jnp.concatenate(following, axis=1)
    total = jnp.sum(jnp.concatenate(sums, axis=0), axis=1, keepdims=True)
    ratios = total[1:] / total[:1]
    lanes = lax.broadcasted_iota(jnp.int32, (ITERS, LANES), 1)
    lined = jnp.where(lanes == lax.broadcasted_iota(jnp.int32, (ITERS, LANES), 0), ratios, 0.0)
    stress_ref[...] = jnp.sum(lined, axis=0, keepdims=True)[:, :ITERS]


def small_body(dissim, classes, coords):
    coord_dims, _, per_dev = coords.shape
    points = dissim.shape[2]
    devices = points // per_dev
    vmem = pl.BlockSpec(memory_space=pltpu.VMEM)
    hbm = pl.BlockSpec(memory_space=pltpu.HBM)
    f32 = functools.partial(jax.ShapeDtypeStruct, dtype=jnp.float32)
    params = pltpu.CompilerParams(vmem_limit_bytes=16 << 20)

    def swap(value, offset):
        return lax.ppermute(value, "wide", [(i, i ^ offset) for i in range(devices)])

    tiles = 2 * len(tile_spots(per_dev, points)) + 1
    inputs = (dissim[0], classes[0], coords[:, 0, :])
    packed = pl.pallas_call(
        pack_kernel,
        out_shape=f32((tiles, SUBLANES, LANES)),
        in_specs=[hbm] * 3,
        out_specs=vmem,
        scratch_shapes=[
            pltpu.VMEM((per_dev, points), jnp.float32),
            pltpu.VMEM((per_dev, points), jnp.int32),
            pltpu.VMEM((coord_dims, per_dev), jnp.float32),
            pltpu.SemaphoreType.DMA((3,)),
        ],
        compiler_params=params,
        name="pack",
    )(*(pltpu.with_memory_space_constraint(array, pltpu.HBM) for array in inputs))
    far, near, side = devices // 2, devices // 4, devices // 8
    held = {0: packed}
    for offset in (side, far, near, far | near | side):
        held[offset] = swap(packed, offset)
    ordered, _ = lax.optimization_barrier((held[far], held[side]))
    held[side | near] = swap(held[side], near)
    held[far | side] = swap(ordered, side)
    held[far | near] = swap(ordered, near)
    early = [0, side, near, far]
    late = [offset for offset in held if offset not in early]
    block = packed.shape[0]

    def join(group, flops):
        return pl.pallas_call(
            join_kernel,
            out_shape=f32((len(group) * block, SUBLANES, LANES)),
            in_specs=[vmem] * len(group),
            out_specs=vmem,
            compiler_params=params,
            cost_estimate=pl.CostEstimate(flops=flops, bytes_accessed=0, transcendentals=0),
            name="join",
        )(*(held[offset] for offset in group))

    first, second = join(early, 1), join(late, 1)
    slots = [first, swap(first, 1), second, swap(second, 1)]
    offsets = [early, [o ^ 1 for o in early], late, [o ^ 1 for o in late]]
    final, stress = pl.pallas_call(
        functools.partial(group_kernel, offsets, per_dev),
        out_shape=(f32((coord_dims, per_dev)), f32((1, ITERS))),
        in_specs=[vmem] * len(slots),
        out_specs=(vmem, vmem),
        scratch_shapes=[
            pltpu.VMEM((points, points), jnp.float32),
            pltpu.VMEM((points, points), jnp.float32),
            pltpu.VMEM((devices, SUBLANES, LANES), jnp.float32),
        ],
        compiler_params=params,
        name="group_smacof",
    )(*slots)
    return (final[:, None, :], stress[0])


def distributed_body(dissim, classes, coords):
    halves = dissim.shape[0]
    per_dev = dissim.shape[1]
    columns = dissim.shape[2]
    coord_dims = coords.shape[0]
    row_count = halves * per_dev
    dis_tile = dissim.reshape(row_count, columns)
    weight = class_weight(classes.reshape(row_count, columns))
    denom_local = jnp.sum(weight * dis_tile * dis_tile)
    half_index = lax.axis_index("narrow")
    denom_total = lax.psum(denom_local, ("wide", "narrow"))
    positions = coords
    numbers = []
    for sweep in range(ITERS):
        row_points = lax.all_gather(positions, "narrow", axis=1, tiled=True)
        row_x = row_points.reshape(coord_dims, row_count)
        row_sq = jnp.sum(row_x * row_x, axis=0)
        fold_column_x = lax.dynamic_index_in_dim(
            lax.all_gather(row_points, "wide", axis=2, tiled=True), half_index, 1, keepdims=False
        )
        inner_prod = lax.dot_general(
            row_x,
            fold_column_x,
            (((0,), (0,)), ((), ())),
            precision=lax.Precision.HIGHEST,
            preferred_element_type=jnp.float32,
        )
        col_sq = jnp.sum(fold_column_x * fold_column_x, axis=0)
        distance = jnp.sqrt(row_sq[:, None] + col_sq[None, :] - 2.0 * inner_prod + 1.0)
        ratios = weight * dis_tile / distance
        pull_term = lax.dot_general(
            weight - ratios,
            fold_column_x,
            (((1,), (1,)), ((), ())),
            precision=lax.Precision.HIGHEST,
            preferred_element_type=jnp.float32,
        )
        misfit = dis_tile - distance
        pull_sums = pull_term.reshape(halves, per_dev, coord_dims).transpose(0, 2, 1)
        weight_sum, ratio_sum, pull_share = (
            lax.psum_scatter(
                jnp.sum(weight, axis=1).reshape(halves, per_dev),
                "narrow",
                scatter_dimension=0,
                tiled=True,
            ),
            lax.psum_scatter(
                jnp.sum(ratios, axis=1).reshape(halves, per_dev),
                "narrow",
                scatter_dimension=0,
                tiled=True,
            ),
            lax.psum_scatter(pull_sums, "narrow", scatter_dimension=0, tiled=True),
        )
        own_coords = positions[:, 0, :]
        updated = (own_coords * (1.0 + ratio_sum[0]) + pull_share[0]) / (1.0 + weight_sum[0])
        positions = updated[:, None, :]
        numbers.append(
            lax.psum(jnp.sum(weight * misfit * misfit), ("wide", "narrow")) / denom_total
        )
    stress = jnp.stack(numbers)
    return (positions, stress)


def solution(mesh):
    def body(dissim, classes, coords):
        coord_dims, halves, per_dev = coords.shape
        points, devices = dissim.shape[2], mesh.shape["wide"]
        small = halves == 1 and mesh.shape["narrow"] == 1 and points * points <= MOST_PAIRS
        small = small and coord_dims == 2 * SUBLANES and 2 * per_dev <= LANES
        small = small and per_dev % SUBLANES == 0 and points % LANES == 0
        small = small and devices == 16
        return (small_body if small else distributed_body)(dissim, classes, coords)

    return jax.shard_map(
        body,
        mesh=mesh,
        in_specs=(
            P(None, ("grp", "wide"), "narrow"),
            P(None, ("grp", "wide"), "narrow"),
            P(None, "narrow", ("grp", "wide")),
        ),
        out_specs=(P(None, "narrow", ("grp", "wide")), P("grp")),
        check_vma=False,
    )
```

```python
import functools

import jax
import jax.numpy as jnp
from jax import lax
from jax.experimental import pallas as pl
from jax.experimental.pallas import tpu as pltpu
from jax.sharding import PartitionSpec as P

ITERS = 3
LANES = 128
MOST_PAIRS = 1 << 19


def class_weight(class_codes):
    return jnp.where(
        class_codes == 3,
        1.0,
        jnp.where(class_codes == 2, 0.5, jnp.where(class_codes == 1, 0.25, 0.0)),
    ).astype(jnp.float32)


def split_bf16(value, terms):
    parts = []
    for _ in range(terms):
        part = value.astype(jnp.bfloat16)
        parts.append(part)
        value = value - part.astype(jnp.float32)
    return parts


SUBLANES = 8
NT = (((1,), (1,)), ((), ()))
TN = (((0,), (0,)), ((), ()))
dot = functools.partial(lax.dot_general, preferred_element_type=jnp.float32)


def lane_sums(value):
    rows = jnp.sum(value, axis=0, keepdims=True)
    return sum(rows[:, i : i + LANES] for i in range(0, rows.shape[1], LANES))


def tile_spots(per_dev, points):
    return [
        (slice(row, row + SUBLANES), slice(column, column + LANES))
        for row in range(0, per_dev, SUBLANES)
        for column in range(0, points, LANES)
    ]


def pack_kernel(dis_hbm, cls_hbm, x_hbm, out_ref, dis_ref, cls_ref, x_ref, sems):
    copies = [
        pltpu.make_async_copy(src, dst, sems.at[i])
        for i, (src, dst) in enumerate(
            [(dis_hbm, dis_ref), (cls_hbm, cls_ref), (x_hbm, x_ref)]
        )
    ]
    for copy in copies:
        copy.start()
    for copy in copies:
        copy.wait()
    spots = tile_spots(*dis_ref.shape)
    for i, spot in enumerate(spots):
        out_ref[i] = dis_ref[spot]
        out_ref[len(spots) + i] = class_weight(cls_ref[spot])
    half, per_dev = x_ref.shape[0] // 2, x_ref.shape[1]
    pad = jnp.zeros((half, LANES - 2 * per_dev), jnp.float32)
    out_ref[2 * len(spots)] = jnp.concatenate([x_ref[:half], x_ref[half:], pad], axis=1)


def held_slots(offsets, refs, tiles):
    me = lax.axis_index("wide")
    for group, ref in zip(offsets, refs):
        for slot, offset in enumerate(group):
            yield ref, slot * tiles, me ^ offset


def norm_rows(top, bottom, coord_dims):
    pad = jnp.zeros((coord_dims - 6, top[0].shape[1]), jnp.float32)
    rows = [p.astype(jnp.float32) for p in (*top, *bottom)]
    return jnp.concatenate([*rows, pad], axis=0).astype(jnp.bfloat16)


def left_side(x, parts):
    hi, mid, lo = (-2.0 * p for p in parts)
    norm = split_bf16(jnp.sum(x * x, axis=0, keepdims=True), 3)
    ones = [jnp.ones((3, x.shape[1]), jnp.bfloat16)]
    return jnp.concatenate([hi, hi, hi, mid, mid, lo, norm_rows(norm, ones, x.shape[0])], axis=0)


def right_side(x, parts):
    hi, mid, lo = parts
    norm = split_bf16(jnp.sum(x * x, axis=0, keepdims=True) + 1.0, 3)
    ones = [jnp.ones((3, x.shape[1]), jnp.bfloat16)]
    return jnp.concatenate([hi, mid, lo, hi, mid, hi, norm_rows(ones, norm, x.shape[0])], axis=0)


def inverse_weight(weight, ones):
    return 1.0 / (1.0 + dot(weight.astype(jnp.bfloat16), ones, NT).T[0:1])


def moved(x, sides, push, scale):
    coord_dims = x.shape[0]
    parts = jnp.concatenate(split_bf16(push, 2), axis=1)
    sums = dot(parts, jnp.concatenate([sides, sides], axis=1), NT).T
    pushed = sums[:coord_dims] + sums[coord_dims : 2 * coord_dims]
    return x + (x * sums[2 * coord_dims : 2 * coord_dims + 1] - pushed) * scale


def join_kernel(*refs):
    *block_refs, out_ref = refs
    size = block_refs[0].shape[0]
    for i, ref in enumerate(block_refs):
        out_ref[i * size : (i + 1) * size] = ref[...]


def group_kernel(offsets, per_dev, *refs):
    slot_refs = refs[: len(offsets)]
    out_ref, stress_ref, dis_ref, weight_ref, tile_ref = refs[len(offsets) :]
    points = dis_ref.shape[0]
    spots = tile_spots(per_dev, points)
    tiles = 2 * len(spots) + 1
    for ref, base, place in held_slots(offsets, slot_refs, tiles):
        tile_ref[place] = ref[base + tiles - 1]
        for i, (rows, columns) in enumerate(spots):
            start = pl.multiple_of(place * per_dev + rows.start, SUBLANES)
            dis_ref[pl.ds(start, SUBLANES), columns] = ref[base + i]
            weight_ref[pl.ds(start, SUBLANES), columns] = ref[base + len(spots) + i]
    blocks = [tile_ref[i] for i in range(tile_ref.shape[0])]
    halves = [
        jnp.concatenate([t[:, low : low + per_dev] for t in blocks], axis=1)
        for low in (0, per_dev)
    ]
    x = jnp.concatenate(halves, axis=0)
    coord_dims = x.shape[0]
    chunks = [slice(row, row + LANES) for row in range(0, points, LANES)]
    ones = jnp.ones((coord_dims, points), jnp.bfloat16)
    scales = [inverse_weight(weight_ref[rows], ones) for rows in chunks]
    denom = sum(lane_sums(weight_ref[rows] * dis_ref[rows] * dis_ref[rows]) for rows in chunks)
    place = lax.axis_index("wide")
    own_rows = pl.ds(pl.multiple_of(place * per_dev, SUBLANES), per_dev)
    shape = (points, per_dev)
    pick = lax.broadcasted_iota(jnp.int32, shape, 0) - lax.broadcasted_iota(jnp.int32, shape, 1)
    pick = (pick == place * per_dev).astype(jnp.float32).astype(jnp.bfloat16)
    sums = [denom]
    for sweep in range(ITERS):
        parts = split_bf16(x, 3)
        sides = jnp.concatenate([parts[0], parts[1], ones], axis=0)
        left, right = left_side(x, parts), right_side(x, parts)
        last = sweep == ITERS - 1
        stress, following = 0.0, []
        for rows, scale in zip(chunks, scales):
            square = dot(left[:, rows], right, TN)
            inverse = lax.rsqrt(square)
            weight, dis = weight_ref[rows], dis_ref[rows]
            misfit = dis - square * inverse
            weighted = weight * misfit
            stress += lane_sums(weighted * misfit)
            if not last:
                following.append(moved(x[:, rows], sides, weighted * inverse, scale))
        sums.append(stress)
        if last:
            own = dot(jnp.concatenate(parts, axis=0), pick, (((1,), (0,)), ((), ())))
            own = sum(own[i * coord_dims : (i + 1) * coord_dims] for i in range(3))
            square = dot(left_side(own, split_bf16(own, 3)), right, TN)
            inverse = lax.rsqrt(square)
            weight = weight_ref[own_rows, :]
            push = weight * (dis_ref[own_rows, :] - square * inverse) * inverse
            out_ref[...] = moved(own, sides, push, inverse_weight(weight, ones))
        else:
            x = jnp.concatenate(following, axis=1)
    total = jnp.sum(jnp.concatenate(sums, axis=0), axis=1, keepdims=True)
    ratios = total[1:] / total[:1]
    lanes = lax.broadcasted_iota(jnp.int32, (ITERS, LANES), 1)
    lined = jnp.where(lanes == lax.broadcasted_iota(jnp.int32, (ITERS, LANES), 0), ratios, 0.0)
    stress_ref[...] = jnp.sum(lined, axis=0, keepdims=True)[:, :ITERS]


def small_body(dissim, classes, coords):
    coord_dims, _, per_dev = coords.shape
    points = dissim.shape[2]
    devices = points // per_dev
    vmem = pl.BlockSpec(memory_space=pltpu.VMEM)
    hbm = pl.BlockSpec(memory_space=pltpu.HBM)
    f32 = functools.partial(jax.ShapeDtypeStruct, dtype=jnp.float32)
    params = pltpu.CompilerParams(vmem_limit_bytes=16 << 20)

    def swap(value, offset):
        return lax.ppermute(value, "wide", [(i, i ^ offset) for i in range(devices)])

    tiles = 2 * len(tile_spots(per_dev, points)) + 1
    inputs = (dissim[0], classes[0], coords[:, 0, :])
    packed = pl.pallas_call(
        pack_kernel,
        out_shape=f32((tiles, SUBLANES, LANES)),
        in_specs=[hbm] * 3,
        out_specs=vmem,
        scratch_shapes=[
            pltpu.VMEM((per_dev, points), jnp.float32),
            pltpu.VMEM((per_dev, points), jnp.int32),
            pltpu.VMEM((coord_dims, per_dev), jnp.float32),
            pltpu.SemaphoreType.DMA((3,)),
        ],
        compiler_params=params,
        name="pack",
    )(*(pltpu.with_memory_space_constraint(array, pltpu.HBM) for array in inputs))
    far, near, side = devices // 2, devices // 4, devices // 8
    held = {0: packed}
    for offset in (far, side, near, far | near | side):
        held[offset] = swap(packed, offset)
    ordered, _ = lax.optimization_barrier((held[far], held[side]))
    held[far | near] = swap(ordered, near)
    held[far | side] = swap(ordered, side)
    held[side | near] = swap(held[side], near)
    early = [0, far, near, side]
    late = [offset for offset in held if offset not in early]
    block = packed.shape[0]

    def join(group, flops):
        return pl.pallas_call(
            join_kernel,
            out_shape=f32((len(group) * block, SUBLANES, LANES)),
            in_specs=[vmem] * len(group),
            out_specs=vmem,
            compiler_params=params,
            cost_estimate=pl.CostEstimate(flops=flops, bytes_accessed=0, transcendentals=0),
            name="join",
        )(*(held[offset] for offset in group))

    first, second = join(early, 1), join(late, 1)
    slots = [first, swap(first, 1), second, swap(second, 1)]
    offsets = [early, [o ^ 1 for o in early], late, [o ^ 1 for o in late]]
    final, stress = pl.pallas_call(
        functools.partial(group_kernel, offsets, per_dev),
        out_shape=(f32((coord_dims, per_dev)), f32((1, ITERS))),
        in_specs=[vmem] * len(slots),
        out_specs=(vmem, vmem),
        scratch_shapes=[
            pltpu.VMEM((points, points), jnp.float32),
            pltpu.VMEM((points, points), jnp.float32),
            pltpu.VMEM((devices, SUBLANES, LANES), jnp.float32),
        ],
        compiler_params=params,
        name="group_smacof",
    )(*slots)
    return (final[:, None, :], stress[0])


def distributed_body(dissim, classes, coords):
    halves = dissim.shape[0]
    per_dev = dissim.shape[1]
    columns = dissim.shape[2]
    coord_dims = coords.shape[0]
    row_count = halves * per_dev
    dis_tile = dissim.reshape(row_count, columns)
    weight = class_weight(classes.reshape(row_count, columns))
    denom_local = jnp.sum(weight * dis_tile * dis_tile)
    half_index = lax.axis_index("narrow")
    denom_total = lax.psum(denom_local, ("wide", "narrow"))
    positions = coords
    numbers = []
    for sweep in range(ITERS):
        row_points = lax.all_gather(positions, "narrow", axis=1, tiled=True)
        row_x = row_points.reshape(coord_dims, row_count)
        row_sq = jnp.sum(row_x * row_x, axis=0)
        fold_column_x = lax.dynamic_index_in_dim(
            lax.all_gather(row_points, "wide", axis=2, tiled=True), half_index, 1, keepdims=False
        )
        inner_prod = lax.dot_general(
            row_x,
            fold_column_x,
            (((0,), (0,)), ((), ())),
            precision=lax.Precision.HIGHEST,
            preferred_element_type=jnp.float32,
        )
        col_sq = jnp.sum(fold_column_x * fold_column_x, axis=0)
        distance = jnp.sqrt(row_sq[:, None] + col_sq[None, :] - 2.0 * inner_prod + 1.0)
        ratios = weight * dis_tile / distance
        pull_term = lax.dot_general(
            weight - ratios,
            fold_column_x,
            (((1,), (1,)), ((), ())),
            precision=lax.Precision.HIGHEST,
            preferred_element_type=jnp.float32,
        )
        misfit = dis_tile - distance
        pull_sums = pull_term.reshape(halves, per_dev, coord_dims).transpose(0, 2, 1)
        weight_sum, ratio_sum, pull_share = (
            lax.psum_scatter(
                jnp.sum(weight, axis=1).reshape(halves, per_dev),
                "narrow",
                scatter_dimension=0,
                tiled=True,
            ),
            lax.psum_scatter(
                jnp.sum(ratios, axis=1).reshape(halves, per_dev),
                "narrow",
                scatter_dimension=0,
                tiled=True,
            ),
            lax.psum_scatter(pull_sums, "narrow", scatter_dimension=0, tiled=True),
        )
        own_coords = positions[:, 0, :]
        updated = (own_coords * (1.0 + ratio_sum[0]) + pull_share[0]) / (1.0 + weight_sum[0])
        positions = updated[:, None, :]
        numbers.append(
            lax.psum(jnp.sum(weight * misfit * misfit), ("wide", "narrow")) / denom_total
        )
    stress = jnp.stack(numbers)
    return (positions, stress)


def solution(mesh):
    def body(dissim, classes, coords):
        coord_dims, halves, per_dev = coords.shape
        points, devices = dissim.shape[2], mesh.shape["wide"]
        small = halves == 1 and mesh.shape["narrow"] == 1 and points * points <= MOST_PAIRS
        small = small and coord_dims == 2 * SUBLANES and 2 * per_dev <= LANES
        small = small and per_dev % SUBLANES == 0 and points % LANES == 0
        small = small and devices == 16
        return (small_body if small else distributed_body)(dissim, classes, coords)

    return jax.shard_map(
        body,
        mesh=mesh,
        in_specs=(
            P(None, ("grp", "wide"), "narrow"),
            P(None, ("grp", "wide"), "narrow"),
            P(None, "narrow", ("grp", "wide")),
        ),
        out_specs=(P(None, "narrow", ("grp", "wide")), P("grp")),
        check_vma=False,
    )
```

```python
import functools

import jax
import jax.numpy as jnp
from jax import lax
from jax.experimental import pallas as pl
from jax.experimental.pallas import tpu as pltpu
from jax.sharding import PartitionSpec as P

ITERS = 3
LANES = 128
MOST_PAIRS = 1 << 19


def class_weight(class_codes):
    return jnp.where(
        class_codes == 3,
        1.0,
        jnp.where(class_codes == 2, 0.5, jnp.where(class_codes == 1, 0.25, 0.0)),
    ).astype(jnp.float32)


def split_bf16(value, terms):
    parts = []
    for _ in range(terms):
        part = value.astype(jnp.bfloat16)
        parts.append(part)
        value = value - part.astype(jnp.float32)
    return parts


SUBLANES = 8
NT = (((1,), (1,)), ((), ()))
TN = (((0,), (0,)), ((), ()))
dot = functools.partial(lax.dot_general, preferred_element_type=jnp.float32)


def lane_sums(value):
    rows = jnp.sum(value, axis=0, keepdims=True)
    return sum(rows[:, i : i + LANES] for i in range(0, rows.shape[1], LANES))


def tile_spots(per_dev, points):
    return [
        (slice(row, row + SUBLANES), slice(column, column + LANES))
        for row in range(0, per_dev, SUBLANES)
        for column in range(0, points, LANES)
    ]


def pack_kernel(dis_hbm, cls_hbm, x_hbm, out_ref, dis_ref, cls_ref, x_ref, sems):
    copies = [
        pltpu.make_async_copy(src, dst, sems.at[i])
        for i, (src, dst) in enumerate(
            [(dis_hbm, dis_ref), (cls_hbm, cls_ref), (x_hbm, x_ref)]
        )
    ]
    for copy in copies:
        copy.start()
    for copy in copies:
        copy.wait()
    spots = tile_spots(*dis_ref.shape)
    for i, spot in enumerate(spots):
        out_ref[i] = dis_ref[spot]
        out_ref[len(spots) + i] = class_weight(cls_ref[spot])
    half, per_dev = x_ref.shape[0] // 2, x_ref.shape[1]
    pad = jnp.zeros((half, LANES - 2 * per_dev), jnp.float32)
    out_ref[2 * len(spots)] = jnp.concatenate([x_ref[:half], x_ref[half:], pad], axis=1)


def held_slots(offsets, refs, tiles):
    me = lax.axis_index("wide")
    for group, ref in zip(offsets, refs):
        for slot, offset in enumerate(group):
            yield ref, slot * tiles, me ^ offset


def norm_rows(top, bottom, coord_dims):
    pad = jnp.zeros((coord_dims - 6, top[0].shape[1]), jnp.float32)
    rows = [p.astype(jnp.float32) for p in (*top, *bottom)]
    return jnp.concatenate([*rows, pad], axis=0).astype(jnp.bfloat16)


def left_side(x, parts):
    hi, mid, lo = (-2.0 * p for p in parts)
    norm = split_bf16(jnp.sum(x * x, axis=0, keepdims=True), 3)
    ones = [jnp.ones((3, x.shape[1]), jnp.bfloat16)]
    return jnp.concatenate([hi, hi, hi, mid, mid, lo, norm_rows(norm, ones, x.shape[0])], axis=0)


def right_side(x, parts):
    hi, mid, lo = parts
    norm = split_bf16(jnp.sum(x * x, axis=0, keepdims=True) + 1.0, 3)
    ones = [jnp.ones((3, x.shape[1]), jnp.bfloat16)]
    return jnp.concatenate([hi, mid, lo, hi, mid, hi, norm_rows(ones, norm, x.shape[0])], axis=0)


def inverse_weight(weight, ones):
    return 1.0 / (1.0 + dot(weight.astype(jnp.bfloat16), ones, NT).T[0:1])


def moved(x, sides, push, scale):
    coord_dims = x.shape[0]
    parts = jnp.concatenate(split_bf16(push, 2), axis=1)
    sums = dot(parts, jnp.concatenate([sides, sides], axis=1), NT).T
    pushed = sums[:coord_dims] + sums[coord_dims : 2 * coord_dims]
    return x + (x * sums[2 * coord_dims : 2 * coord_dims + 1] - pushed) * scale


def join_kernel(*refs):
    *block_refs, out_ref = refs
    size = block_refs[0].shape[0]
    for i, ref in enumerate(block_refs):
        out_ref[i * size : (i + 1) * size] = ref[...]


def group_kernel(offsets, per_dev, *refs):
    slot_refs = refs[: len(offsets)]
    out_ref, stress_ref, dis_ref, weight_ref, tile_ref = refs[len(offsets) :]
    points = dis_ref.shape[0]
    spots = tile_spots(per_dev, points)
    tiles = 2 * len(spots) + 1
    for ref, base, place in held_slots(offsets, slot_refs, tiles):
        tile_ref[place] = ref[base + tiles - 1]
        for i, (rows, columns) in enumerate(spots):
            start = pl.multiple_of(place * per_dev + rows.start, SUBLANES)
            dis_ref[pl.ds(start, SUBLANES), columns] = ref[base + i]
            weight_ref[pl.ds(start, SUBLANES), columns] = ref[base + len(spots) + i]
    blocks = [tile_ref[i] for i in range(tile_ref.shape[0])]
    halves = [
        jnp.concatenate([t[:, low : low + per_dev] for t in blocks], axis=1)
        for low in (0, per_dev)
    ]
    x = jnp.concatenate(halves, axis=0)
    coord_dims = x.shape[0]
    chunks = [slice(row, row + LANES) for row in range(0, points, LANES)]
    ones = jnp.ones((coord_dims, points), jnp.bfloat16)
    scales = [inverse_weight(weight_ref[rows], ones) for rows in chunks]
    denom = sum(lane_sums(weight_ref[rows] * dis_ref[rows] * dis_ref[rows]) for rows in chunks)
    place = lax.axis_index("wide")
    own_rows = pl.ds(pl.multiple_of(place * per_dev, SUBLANES), per_dev)
    shape = (points, per_dev)
    pick = lax.broadcasted_iota(jnp.int32, shape, 0) - lax.broadcasted_iota(jnp.int32, shape, 1)
    pick = (pick == place * per_dev).astype(jnp.float32).astype(jnp.bfloat16)
    sums = [denom]
    for sweep in range(ITERS):
        parts = split_bf16(x, 3)
        sides = jnp.concatenate([parts[0], parts[1], ones], axis=0)
        left, right = left_side(x, parts), right_side(x, parts)
        last = sweep == ITERS - 1
        stress, following = 0.0, []
        for rows, scale in zip(chunks, scales):
            square = dot(left[:, rows], right, TN)
            inverse = lax.rsqrt(square)
            weight, dis = weight_ref[rows], dis_ref[rows]
            misfit = dis - square * inverse
            weighted = weight * misfit
            stress += lane_sums(weighted * misfit)
            if not last:
                following.append(moved(x[:, rows], sides, weighted * inverse, scale))
        sums.append(stress)
        if last:
            own = dot(jnp.concatenate(parts, axis=0), pick, (((1,), (0,)), ((), ())))
            own = sum(own[i * coord_dims : (i + 1) * coord_dims] for i in range(3))
            square = dot(left_side(own, split_bf16(own, 3)), right, TN)
            inverse = lax.rsqrt(square)
            weight = weight_ref[own_rows, :]
            push = weight * (dis_ref[own_rows, :] - square * inverse) * inverse
            out_ref[...] = moved(own, sides, push, inverse_weight(weight, ones))
        else:
            x = jnp.concatenate(following, axis=1)
    total = jnp.sum(jnp.concatenate(sums, axis=0), axis=1, keepdims=True)
    ratios = total[1:] / total[:1]
    lanes = lax.broadcasted_iota(jnp.int32, (ITERS, LANES), 1)
    lined = jnp.where(lanes == lax.broadcasted_iota(jnp.int32, (ITERS, LANES), 0), ratios, 0.0)
    stress_ref[...] = jnp.sum(lined, axis=0, keepdims=True)[:, :ITERS]


def small_body(dissim, classes, coords):
    coord_dims, _, per_dev = coords.shape
    points = dissim.shape[2]
    devices = points // per_dev
    vmem = pl.BlockSpec(memory_space=pltpu.VMEM)
    hbm = pl.BlockSpec(memory_space=pltpu.HBM)
    f32 = functools.partial(jax.ShapeDtypeStruct, dtype=jnp.float32)
    params = pltpu.CompilerParams(vmem_limit_bytes=16 << 20)

    def swap(value, offset):
        return lax.ppermute(value, "wide", [(i, i ^ offset) for i in range(devices)])

    tiles = 2 * len(tile_spots(per_dev, points)) + 1
    inputs = (dissim[0], classes[0], coords[:, 0, :])
    packed = pl.pallas_call(
        pack_kernel,
        out_shape=f32((tiles, SUBLANES, LANES)),
        in_specs=[hbm] * 3,
        out_specs=vmem,
        scratch_shapes=[
            pltpu.VMEM((per_dev, points), jnp.float32),
            pltpu.VMEM((per_dev, points), jnp.int32),
            pltpu.VMEM((coord_dims, per_dev), jnp.float32),
            pltpu.SemaphoreType.DMA((3,)),
        ],
        compiler_params=params,
        name="pack",
    )(*(pltpu.with_memory_space_constraint(array, pltpu.HBM) for array in inputs))
    far, near, side = devices // 2, devices // 4, devices // 8
    held = {0: packed}
    for offset in (far, side, near, far | near | side):
        held[offset] = swap(packed, offset)
    for source, step in ((far, near | 1), (far, side), (side, near)):
        held[source | step] = swap(held[source], step)
    early = [0, far, near, side]
    late = [offset for offset in held if offset not in early]
    block = packed.shape[0]

    def join(group, flops):
        return pl.pallas_call(
            join_kernel,
            out_shape=f32((len(group) * block, SUBLANES, LANES)),
            in_specs=[vmem] * len(group),
            out_specs=vmem,
            compiler_params=params,
            cost_estimate=pl.CostEstimate(flops=flops, bytes_accessed=0, transcendentals=0),
            name="join",
        )(*(held[offset] for offset in group))

    first, second = join(early, 1), join(late, 1)
    slots = [first, swap(first, 1), second, swap(second, 1)]
    offsets = [early, [o ^ 1 for o in early], late, [o ^ 1 for o in late]]
    final, stress = pl.pallas_call(
        functools.partial(group_kernel, offsets, per_dev),
        out_shape=(f32((coord_dims, per_dev)), f32((1, ITERS))),
        in_specs=[vmem] * len(slots),
        out_specs=(vmem, vmem),
        scratch_shapes=[
            pltpu.VMEM((points, points), jnp.float32),
            pltpu.VMEM((points, points), jnp.float32),
            pltpu.VMEM((devices, SUBLANES, LANES), jnp.float32),
        ],
        compiler_params=params,
        name="group_smacof",
    )(*slots)
    return (final[:, None, :], stress[0])


def distributed_body(dissim, classes, coords):
    halves = dissim.shape[0]
    per_dev = dissim.shape[1]
    columns = dissim.shape[2]
    coord_dims = coords.shape[0]
    row_count = halves * per_dev
    dis_tile = dissim.reshape(row_count, columns)
    weight = class_weight(classes.reshape(row_count, columns))
    denom_local = jnp.sum(weight * dis_tile * dis_tile)
    half_index = lax.axis_index("narrow")
    denom_total = lax.psum(denom_local, ("wide", "narrow"))
    positions = coords
    numbers = []
    for sweep in range(ITERS):
        row_points = lax.all_gather(positions, "narrow", axis=1, tiled=True)
        row_x = row_points.reshape(coord_dims, row_count)
        row_sq = jnp.sum(row_x * row_x, axis=0)
        fold_column_x = lax.dynamic_index_in_dim(
            lax.all_gather(row_points, "wide", axis=2, tiled=True), half_index, 1, keepdims=False
        )
        inner_prod = lax.dot_general(
            row_x,
            fold_column_x,
            (((0,), (0,)), ((), ())),
            precision=lax.Precision.HIGHEST,
            preferred_element_type=jnp.float32,
        )
        col_sq = jnp.sum(fold_column_x * fold_column_x, axis=0)
        distance = jnp.sqrt(row_sq[:, None] + col_sq[None, :] - 2.0 * inner_prod + 1.0)
        ratios = weight * dis_tile / distance
        pull_term = lax.dot_general(
            weight - ratios,
            fold_column_x,
            (((1,), (1,)), ((), ())),
            precision=lax.Precision.HIGHEST,
            preferred_element_type=jnp.float32,
        )
        misfit = dis_tile - distance
        pull_sums = pull_term.reshape(halves, per_dev, coord_dims).transpose(0, 2, 1)
        weight_sum, ratio_sum, pull_share = (
            lax.psum_scatter(
                jnp.sum(weight, axis=1).reshape(halves, per_dev),
                "narrow",
                scatter_dimension=0,
                tiled=True,
            ),
            lax.psum_scatter(
                jnp.sum(ratios, axis=1).reshape(halves, per_dev),
                "narrow",
                scatter_dimension=0,
                tiled=True,
            ),
            lax.psum_scatter(pull_sums, "narrow", scatter_dimension=0, tiled=True),
        )
        own_coords = positions[:, 0, :]
        updated = (own_coords * (1.0 + ratio_sum[0]) + pull_share[0]) / (1.0 + weight_sum[0])
        positions = updated[:, None, :]
        numbers.append(
            lax.psum(jnp.sum(weight * misfit * misfit), ("wide", "narrow")) / denom_total
        )
    stress = jnp.stack(numbers)
    return (positions, stress)


def solution(mesh):
    def body(dissim, classes, coords):
        coord_dims, halves, per_dev = coords.shape
        points, devices = dissim.shape[2], mesh.shape["wide"]
        small = halves == 1 and mesh.shape["narrow"] == 1 and points * points <= MOST_PAIRS
        small = small and coord_dims == 2 * SUBLANES and 2 * per_dev <= LANES
        small = small and per_dev % SUBLANES == 0 and points % LANES == 0
        small = small and devices == 16
        return (small_body if small else distributed_body)(dissim, classes, coords)

    return jax.shard_map(
        body,
        mesh=mesh,
        in_specs=(
            P(None, ("grp", "wide"), "narrow"),
            P(None, ("grp", "wide"), "narrow"),
            P(None, "narrow", ("grp", "wide")),
        ),
        out_specs=(P(None, "narrow", ("grp", "wide")), P("grp")),
        check_vma=False,
    )
```

```python
import functools

import jax
import jax.numpy as jnp
from jax import lax
from jax.experimental import pallas as pl
from jax.experimental.pallas import tpu as pltpu
from jax.sharding import PartitionSpec as P

ITERS = 3
LANES = 128
MOST_PAIRS = 1 << 19


def class_weight(class_codes):
    return jnp.where(
        class_codes == 3,
        1.0,
        jnp.where(class_codes == 2, 0.5, jnp.where(class_codes == 1, 0.25, 0.0)),
    ).astype(jnp.float32)


def split_bf16(value, terms):
    parts = []
    for _ in range(terms):
        part = value.astype(jnp.bfloat16)
        parts.append(part)
        value = value - part.astype(jnp.float32)
    return parts


SUBLANES = 8
NT = (((1,), (1,)), ((), ()))
TN = (((0,), (0,)), ((), ()))
dot = functools.partial(lax.dot_general, preferred_element_type=jnp.float32)


def lane_sums(value):
    rows = jnp.sum(value, axis=0, keepdims=True)
    return sum(rows[:, i : i + LANES] for i in range(0, rows.shape[1], LANES))


def tile_spots(per_dev, points):
    return [
        (slice(row, row + SUBLANES), slice(column, column + LANES))
        for row in range(0, per_dev, SUBLANES)
        for column in range(0, points, LANES)
    ]


def pack_kernel(dis_hbm, cls_hbm, x_hbm, out_ref, dis_ref, cls_ref, x_ref, sems):
    copies = [
        pltpu.make_async_copy(src, dst, sems.at[i])
        for i, (src, dst) in enumerate(
            [(dis_hbm, dis_ref), (cls_hbm, cls_ref), (x_hbm, x_ref)]
        )
    ]
    for copy in copies:
        copy.start()
    for copy in copies:
        copy.wait()
    spots = tile_spots(*dis_ref.shape)
    for i, spot in enumerate(spots):
        out_ref[i] = dis_ref[spot]
        out_ref[len(spots) + i] = class_weight(cls_ref[spot])
    half, per_dev = x_ref.shape[0] // 2, x_ref.shape[1]
    pad = jnp.zeros((half, LANES - 2 * per_dev), jnp.float32)
    out_ref[2 * len(spots)] = jnp.concatenate([x_ref[:half], x_ref[half:], pad], axis=1)


def held_slots(offsets, refs, tiles):
    me = lax.axis_index("wide")
    for group, ref in zip(offsets, refs):
        for slot, offset in enumerate(group):
            yield ref, slot * tiles, me ^ offset


def norm_rows(top, bottom, coord_dims):
    pad = jnp.zeros((coord_dims - 6, top[0].shape[1]), jnp.float32)
    rows = [p.astype(jnp.float32) for p in (*top, *bottom)]
    return jnp.concatenate([*rows, pad], axis=0).astype(jnp.bfloat16)


def left_side(x, parts):
    hi, mid, lo = (-2.0 * p for p in parts)
    norm = split_bf16(jnp.sum(x * x, axis=0, keepdims=True), 3)
    ones = [jnp.ones((3, x.shape[1]), jnp.bfloat16)]
    return jnp.concatenate([hi, hi, hi, mid, mid, lo, norm_rows(norm, ones, x.shape[0])], axis=0)


def right_side(x, parts):
    hi, mid, lo = parts
    norm = split_bf16(jnp.sum(x * x, axis=0, keepdims=True) + 1.0, 3)
    ones = [jnp.ones((3, x.shape[1]), jnp.bfloat16)]
    return jnp.concatenate([hi, mid, lo, hi, mid, hi, norm_rows(ones, norm, x.shape[0])], axis=0)


def inverse_weight(weight, ones):
    return 1.0 / (1.0 + dot(weight.astype(jnp.bfloat16), ones, NT).T[0:1])


def moved(x, sides, push, scale):
    coord_dims = x.shape[0]
    parts = jnp.concatenate(split_bf16(push, 2), axis=1)
    sums = dot(parts, jnp.concatenate([sides, sides], axis=1), NT).T
    pushed = sums[:coord_dims] + sums[coord_dims : 2 * coord_dims]
    return x + (x * sums[2 * coord_dims : 2 * coord_dims + 1] - pushed) * scale


def join_kernel(*refs):
    *block_refs, out_ref = refs
    size = block_refs[0].shape[0]
    for i, ref in enumerate(block_refs):
        out_ref[i * size : (i + 1) * size] = ref[...]


def group_kernel(offsets, per_dev, *refs):
    slot_refs = refs[: len(offsets)]
    out_ref, stress_ref, dis_ref, weight_ref, tile_ref = refs[len(offsets) :]
    points = dis_ref.shape[0]
    spots = tile_spots(per_dev, points)
    tiles = 2 * len(spots) + 1
    for ref, base, place in held_slots(offsets, slot_refs, tiles):
        tile_ref[place] = ref[base + tiles - 1]
        for i, (rows, columns) in enumerate(spots):
            start = pl.multiple_of(place * per_dev + rows.start, SUBLANES)
            dis_ref[pl.ds(start, SUBLANES), columns] = ref[base + i]
            weight_ref[pl.ds(start, SUBLANES), columns] = ref[base + len(spots) + i]
    blocks = [tile_ref[i] for i in range(tile_ref.shape[0])]
    halves = [
        jnp.concatenate([t[:, low : low + per_dev] for t in blocks], axis=1)
        for low in (0, per_dev)
    ]
    x = jnp.concatenate(halves, axis=0)
    coord_dims = x.shape[0]
    chunks = [slice(row, row + LANES) for row in range(0, points, LANES)]
    ones = jnp.ones((coord_dims, points), jnp.bfloat16)
    scales = [inverse_weight(weight_ref[rows], ones) for rows in chunks]
    denom = sum(lane_sums(weight_ref[rows] * dis_ref[rows] * dis_ref[rows]) for rows in chunks)
    place = lax.axis_index("wide")
    own_rows = pl.ds(pl.multiple_of(place * per_dev, SUBLANES), per_dev)
    shape = (points, per_dev)
    pick = lax.broadcasted_iota(jnp.int32, shape, 0) - lax.broadcasted_iota(jnp.int32, shape, 1)
    pick = (pick == place * per_dev).astype(jnp.float32).astype(jnp.bfloat16)
    sums = [denom]
    for sweep in range(ITERS):
        parts = split_bf16(x, 3)
        sides = jnp.concatenate([parts[0], parts[1], ones], axis=0)
        left, right = left_side(x, parts), right_side(x, parts)
        last = sweep == ITERS - 1
        stress, following = 0.0, []
        for rows, scale in zip(chunks, scales):
            square = dot(left[:, rows], right, TN)
            inverse = lax.rsqrt(square)
            weight, dis = weight_ref[rows], dis_ref[rows]
            misfit = dis - square * inverse
            weighted = weight * misfit
            stress += lane_sums(weighted * misfit)
            if not last:
                following.append(moved(x[:, rows], sides, weighted * inverse, scale))
        sums.append(stress)
        if last:
            own = dot(jnp.concatenate(parts, axis=0), pick, (((1,), (0,)), ((), ())))
            own = sum(own[i * coord_dims : (i + 1) * coord_dims] for i in range(3))
            square = dot(left_side(own, split_bf16(own, 3)), right, TN)
            inverse = lax.rsqrt(square)
            weight = weight_ref[own_rows, :]
            push = weight * (dis_ref[own_rows, :] - square * inverse) * inverse
            out_ref[...] = moved(own, sides, push, inverse_weight(weight, ones))
        else:
            x = jnp.concatenate(following, axis=1)
    total = jnp.sum(jnp.concatenate(sums, axis=0), axis=1, keepdims=True)
    ratios = total[1:] / total[:1]
    lanes = lax.broadcasted_iota(jnp.int32, (ITERS, LANES), 1)
    lined = jnp.where(lanes == lax.broadcasted_iota(jnp.int32, (ITERS, LANES), 0), ratios, 0.0)
    stress_ref[...] = jnp.sum(lined, axis=0, keepdims=True)[:, :ITERS]


def small_body(dissim, classes, coords):
    coord_dims, _, per_dev = coords.shape
    points = dissim.shape[2]
    devices = points // per_dev
    vmem = pl.BlockSpec(memory_space=pltpu.VMEM)
    hbm = pl.BlockSpec(memory_space=pltpu.HBM)
    f32 = functools.partial(jax.ShapeDtypeStruct, dtype=jnp.float32)
    params = pltpu.CompilerParams(vmem_limit_bytes=16 << 20)

    def swap(value, offset):
        return lax.ppermute(value, "wide", [(i, i ^ offset) for i in range(devices)])

    tiles = 2 * len(tile_spots(per_dev, points)) + 1
    inputs = (dissim[0], classes[0], coords[:, 0, :])
    packed = pl.pallas_call(
        pack_kernel,
        out_shape=f32((tiles, SUBLANES, LANES)),
        in_specs=[hbm] * 3,
        out_specs=vmem,
        scratch_shapes=[
            pltpu.VMEM((per_dev, points), jnp.float32),
            pltpu.VMEM((per_dev, points), jnp.int32),
            pltpu.VMEM((coord_dims, per_dev), jnp.float32),
            pltpu.SemaphoreType.DMA((3,)),
        ],
        compiler_params=params,
        name="pack",
    )(*(pltpu.with_memory_space_constraint(array, pltpu.HBM) for array in inputs))
    far, near, side = devices // 2, devices // 4, devices // 8
    held = {0: packed}
    for offset in (far, side, near, far | near | side | 1):
        held[offset] = swap(packed, offset)
    for source, step in ((far, near | 1), (far, side), (side, near)):
        held[source | step] = swap(held[source], step)
    early = [0, far, near, side]
    late = [offset for offset in held if offset not in early]
    block = packed.shape[0]

    def join(group, flops):
        return pl.pallas_call(
            join_kernel,
            out_shape=f32((len(group) * block, SUBLANES, LANES)),
            in_specs=[vmem] * len(group),
            out_specs=vmem,
            compiler_params=params,
            cost_estimate=pl.CostEstimate(flops=flops, bytes_accessed=0, transcendentals=0),
            name="join",
        )(*(held[offset] for offset in group))

    first, second = join(early, 1), join(late, 1)
    slots = [first, swap(first, 1), second, swap(second, 1)]
    offsets = [early, [o ^ 1 for o in early], late, [o ^ 1 for o in late]]
    final, stress = pl.pallas_call(
        functools.partial(group_kernel, offsets, per_dev),
        out_shape=(f32((coord_dims, per_dev)), f32((1, ITERS))),
        in_specs=[vmem] * len(slots),
        out_specs=(vmem, vmem),
        scratch_shapes=[
            pltpu.VMEM((points, points), jnp.float32),
            pltpu.VMEM((points, points), jnp.float32),
            pltpu.VMEM((devices, SUBLANES, LANES), jnp.float32),
        ],
        compiler_params=params,
        name="group_smacof",
    )(*slots)
    return (final[:, None, :], stress[0])


def distributed_body(dissim, classes, coords):
    halves = dissim.shape[0]
    per_dev = dissim.shape[1]
    columns = dissim.shape[2]
    coord_dims = coords.shape[0]
    row_count = halves * per_dev
    dis_tile = dissim.reshape(row_count, columns)
    weight = class_weight(classes.reshape(row_count, columns))
    denom_local = jnp.sum(weight * dis_tile * dis_tile)
    half_index = lax.axis_index("narrow")
    denom_total = lax.psum(denom_local, ("wide", "narrow"))
    positions = coords
    numbers = []
    for sweep in range(ITERS):
        row_points = lax.all_gather(positions, "narrow", axis=1, tiled=True)
        row_x = row_points.reshape(coord_dims, row_count)
        row_sq = jnp.sum(row_x * row_x, axis=0)
        fold_column_x = lax.dynamic_index_in_dim(
            lax.all_gather(row_points, "wide", axis=2, tiled=True), half_index, 1, keepdims=False
        )
        inner_prod = lax.dot_general(
            row_x,
            fold_column_x,
            (((0,), (0,)), ((), ())),
            precision=lax.Precision.HIGHEST,
            preferred_element_type=jnp.float32,
        )
        col_sq = jnp.sum(fold_column_x * fold_column_x, axis=0)
        distance = jnp.sqrt(row_sq[:, None] + col_sq[None, :] - 2.0 * inner_prod + 1.0)
        ratios = weight * dis_tile / distance
        pull_term = lax.dot_general(
            weight - ratios,
            fold_column_x,
            (((1,), (1,)), ((), ())),
            precision=lax.Precision.HIGHEST,
            preferred_element_type=jnp.float32,
        )
        misfit = dis_tile - distance
        pull_sums = pull_term.reshape(halves, per_dev, coord_dims).transpose(0, 2, 1)
        weight_sum, ratio_sum, pull_share = (
            lax.psum_scatter(
                jnp.sum(weight, axis=1).reshape(halves, per_dev),
                "narrow",
                scatter_dimension=0,
                tiled=True,
            ),
            lax.psum_scatter(
                jnp.sum(ratios, axis=1).reshape(halves, per_dev),
                "narrow",
                scatter_dimension=0,
                tiled=True,
            ),
            lax.psum_scatter(pull_sums, "narrow", scatter_dimension=0, tiled=True),
        )
        own_coords = positions[:, 0, :]
        updated = (own_coords * (1.0 + ratio_sum[0]) + pull_share[0]) / (1.0 + weight_sum[0])
        positions = updated[:, None, :]
        numbers.append(
            lax.psum(jnp.sum(weight * misfit * misfit), ("wide", "narrow")) / denom_total
        )
    stress = jnp.stack(numbers)
    return (positions, stress)


def solution(mesh):
    def body(dissim, classes, coords):
        coord_dims, halves, per_dev = coords.shape
        points, devices = dissim.shape[2], mesh.shape["wide"]
        small = halves == 1 and mesh.shape["narrow"] == 1 and points * points <= MOST_PAIRS
        small = small and coord_dims == 2 * SUBLANES and 2 * per_dev <= LANES
        small = small and per_dev % SUBLANES == 0 and points % LANES == 0
        small = small and devices == 16
        return (small_body if small else distributed_body)(dissim, classes, coords)

    return jax.shard_map(
        body,
        mesh=mesh,
        in_specs=(
            P(None, ("grp", "wide"), "narrow"),
            P(None, ("grp", "wide"), "narrow"),
            P(None, "narrow", ("grp", "wide")),
        ),
        out_specs=(P(None, "narrow", ("grp", "wide")), P("grp")),
        check_vma=False,
    )
```

```python
import functools

import jax
import jax.numpy as jnp
from jax import lax
from jax.experimental import pallas as pl
from jax.experimental.pallas import tpu as pltpu
from jax.sharding import PartitionSpec as P

ITERS = 3
LANES = 128
MOST_PAIRS = 1 << 19


def class_weight(class_codes):
    return jnp.where(
        class_codes == 3,
        1.0,
        jnp.where(class_codes == 2, 0.5, jnp.where(class_codes == 1, 0.25, 0.0)),
    ).astype(jnp.float32)


def split_bf16(value, terms):
    parts = []
    for _ in range(terms):
        part = value.astype(jnp.bfloat16)
        parts.append(part)
        value = value - part.astype(jnp.float32)
    return parts


SUBLANES = 8
NT = (((1,), (1,)), ((), ()))
TN = (((0,), (0,)), ((), ()))
dot = functools.partial(lax.dot_general, preferred_element_type=jnp.float32)


def lane_sums(value):
    rows = jnp.sum(value, axis=0, keepdims=True)
    return sum(rows[:, i : i + LANES] for i in range(0, rows.shape[1], LANES))


def tile_spots(per_dev, points):
    return [
        (slice(row, row + SUBLANES), slice(column, column + LANES))
        for row in range(0, per_dev, SUBLANES)
        for column in range(0, points, LANES)
    ]


def pack_kernel(dis_hbm, cls_hbm, x_hbm, out_ref, dis_ref, cls_ref, x_ref, sems):
    copies = [
        pltpu.make_async_copy(src, dst, sems.at[i])
        for i, (src, dst) in enumerate(
            [(dis_hbm, dis_ref), (cls_hbm, cls_ref), (x_hbm, x_ref)]
        )
    ]
    for copy in copies:
        copy.start()
    for copy in copies:
        copy.wait()
    spots = tile_spots(*dis_ref.shape)
    for i, spot in enumerate(spots):
        out_ref[i] = dis_ref[spot]
        out_ref[len(spots) + i] = class_weight(cls_ref[spot])
    half, per_dev = x_ref.shape[0] // 2, x_ref.shape[1]
    pad = jnp.zeros((half, LANES - 2 * per_dev), jnp.float32)
    out_ref[2 * len(spots)] = jnp.concatenate([x_ref[:half], x_ref[half:], pad], axis=1)


def held_slots(offsets, refs, tiles):
    me = lax.axis_index("wide")
    for group, ref in zip(offsets, refs):
        for slot, offset in enumerate(group):
            yield ref, slot * tiles, me ^ offset


def norm_rows(top, bottom, coord_dims):
    pad = jnp.zeros((coord_dims - 6, top[0].shape[1]), jnp.float32)
    rows = [p.astype(jnp.float32) for p in (*top, *bottom)]
    return jnp.concatenate([*rows, pad], axis=0).astype(jnp.bfloat16)


def left_side(x, parts):
    hi, mid, lo = (-2.0 * p for p in parts)
    norm = split_bf16(jnp.sum(x * x, axis=0, keepdims=True), 3)
    ones = [jnp.ones((3, x.shape[1]), jnp.bfloat16)]
    return jnp.concatenate([hi, hi, hi, mid, mid, lo, norm_rows(norm, ones, x.shape[0])], axis=0)


def right_side(x, parts):
    hi, mid, lo = parts
    norm = split_bf16(jnp.sum(x * x, axis=0, keepdims=True) + 1.0, 3)
    ones = [jnp.ones((3, x.shape[1]), jnp.bfloat16)]
    return jnp.concatenate([hi, mid, lo, hi, mid, hi, norm_rows(ones, norm, x.shape[0])], axis=0)


def inverse_weight(weight, ones):
    return 1.0 / (1.0 + dot(weight.astype(jnp.bfloat16), ones, NT).T[0:1])


def moved(x, sides, push, scale):
    coord_dims = x.shape[0]
    parts = jnp.concatenate(split_bf16(push, 2), axis=1)
    sums = dot(parts, jnp.concatenate([sides, sides], axis=1), NT).T
    pushed = sums[:coord_dims] + sums[coord_dims : 2 * coord_dims]
    return x + (x * sums[2 * coord_dims : 2 * coord_dims + 1] - pushed) * scale


def join_kernel(*refs):
    *block_refs, out_ref = refs
    size = block_refs[0].shape[0]
    for i, ref in enumerate(block_refs):
        out_ref[i * size : (i + 1) * size] = ref[...]


def group_kernel(offsets, per_dev, *refs):
    slot_refs = refs[: len(offsets)]
    out_ref, stress_ref, dis_ref, weight_ref, tile_ref = refs[len(offsets) :]
    points = dis_ref.shape[0]
    spots = tile_spots(per_dev, points)
    tiles = 2 * len(spots) + 1
    for ref, base, place in held_slots(offsets, slot_refs, tiles):
        tile_ref[place] = ref[base + tiles - 1]
        for i, (rows, columns) in enumerate(spots):
            start = pl.multiple_of(place * per_dev + rows.start, SUBLANES)
            dis_ref[pl.ds(start, SUBLANES), columns] = ref[base + i]
            weight_ref[pl.ds(start, SUBLANES), columns] = ref[base + len(spots) + i]
    blocks = [tile_ref[i] for i in range(tile_ref.shape[0])]
    halves = [
        jnp.concatenate([t[:, low : low + per_dev] for t in blocks], axis=1)
        for low in (0, per_dev)
    ]
    x = jnp.concatenate(halves, axis=0)
    coord_dims = x.shape[0]
    chunks = [slice(row, row + LANES) for row in range(0, points, LANES)]
    ones = jnp.ones((coord_dims, points), jnp.bfloat16)
    scales = [inverse_weight(weight_ref[rows], ones) for rows in chunks]
    denom = sum(lane_sums(weight_ref[rows] * dis_ref[rows] * dis_ref[rows]) for rows in chunks)
    place = lax.axis_index("wide")
    own_rows = pl.ds(pl.multiple_of(place * per_dev, SUBLANES), per_dev)
    shape = (points, per_dev)
    pick = lax.broadcasted_iota(jnp.int32, shape, 0) - lax.broadcasted_iota(jnp.int32, shape, 1)
    pick = (pick == place * per_dev).astype(jnp.float32).astype(jnp.bfloat16)
    sums = [denom]
    for sweep in range(ITERS):
        parts = split_bf16(x, 3)
        sides = jnp.concatenate([parts[0], parts[1], ones], axis=0)
        left, right = left_side(x, parts), right_side(x, parts)
        last = sweep == ITERS - 1
        stress, following = 0.0, []
        for rows, scale in zip(chunks, scales):
            square = dot(left[:, rows], right, TN)
            inverse = lax.rsqrt(square)
            weight, dis = weight_ref[rows], dis_ref[rows]
            misfit = dis - square * inverse
            weighted = weight * misfit
            stress += lane_sums(weighted * misfit)
            if not last:
                following.append(moved(x[:, rows], sides, weighted * inverse, scale))
        sums.append(stress)
        if last:
            own = dot(jnp.concatenate(parts, axis=0), pick, (((1,), (0,)), ((), ())))
            own = sum(own[i * coord_dims : (i + 1) * coord_dims] for i in range(3))
            square = dot(left_side(own, split_bf16(own, 3)), right, TN)
            inverse = lax.rsqrt(square)
            weight = weight_ref[own_rows, :]
            push = weight * (dis_ref[own_rows, :] - square * inverse) * inverse
            out_ref[...] = moved(own, sides, push, inverse_weight(weight, ones))
        else:
            x = jnp.concatenate(following, axis=1)
    total = jnp.sum(jnp.concatenate(sums, axis=0), axis=1, keepdims=True)
    ratios = total[1:] / total[:1]
    lanes = lax.broadcasted_iota(jnp.int32, (ITERS, LANES), 1)
    lined = jnp.where(lanes == lax.broadcasted_iota(jnp.int32, (ITERS, LANES), 0), ratios, 0.0)
    stress_ref[...] = jnp.sum(lined, axis=0, keepdims=True)[:, :ITERS]


def small_body(dissim, classes, coords):
    coord_dims, _, per_dev = coords.shape
    points = dissim.shape[2]
    devices = points // per_dev
    vmem = pl.BlockSpec(memory_space=pltpu.VMEM)
    hbm = pl.BlockSpec(memory_space=pltpu.HBM)
    f32 = functools.partial(jax.ShapeDtypeStruct, dtype=jnp.float32)
    params = pltpu.CompilerParams(vmem_limit_bytes=16 << 20)

    def swap(value, offset):
        return lax.ppermute(value, "wide", [(i, i ^ offset) for i in range(devices)])

    tiles = 2 * len(tile_spots(per_dev, points)) + 1
    inputs = (dissim[0], classes[0], coords[:, 0, :])
    packed = pl.pallas_call(
        pack_kernel,
        out_shape=f32((tiles, SUBLANES, LANES)),
        in_specs=[hbm] * 3,
        out_specs=vmem,
        scratch_shapes=[
            pltpu.VMEM((per_dev, points), jnp.float32),
            pltpu.VMEM((per_dev, points), jnp.int32),
            pltpu.VMEM((coord_dims, per_dev), jnp.float32),
            pltpu.SemaphoreType.DMA((3,)),
        ],
        compiler_params=params,
        name="pack",
    )(*(pltpu.with_memory_space_constraint(array, pltpu.HBM) for array in inputs))
    far, near, side = devices // 2, devices // 4, devices // 8
    held = {0: packed}
    for offset in (far, side, near, far | near | side | 1):
        held[offset] = swap(packed, offset)
    for source, step in ((far, near | 1), (far, side | 1), (side, near)):
        held[source | step] = swap(held[source], step)
    early = [0, far, near, side]
    late = [offset for offset in held if offset not in early]
    block = packed.shape[0]

    def join(group, flops):
        return pl.pallas_call(
            join_kernel,
            out_shape=f32((len(group) * block, SUBLANES, LANES)),
            in_specs=[vmem] * len(group),
            out_specs=vmem,
            compiler_params=params,
            cost_estimate=pl.CostEstimate(flops=flops, bytes_accessed=0, transcendentals=0),
            name="join",
        )(*(held[offset] for offset in group))

    first, second = join(early, 1), join(late, 1)
    slots = [first, swap(first, 1), second, swap(second, 1)]
    offsets = [early, [o ^ 1 for o in early], late, [o ^ 1 for o in late]]
    final, stress = pl.pallas_call(
        functools.partial(group_kernel, offsets, per_dev),
        out_shape=(f32((coord_dims, per_dev)), f32((1, ITERS))),
        in_specs=[vmem] * len(slots),
        out_specs=(vmem, vmem),
        scratch_shapes=[
            pltpu.VMEM((points, points), jnp.float32),
            pltpu.VMEM((points, points), jnp.float32),
            pltpu.VMEM((devices, SUBLANES, LANES), jnp.float32),
        ],
        compiler_params=params,
        name="group_smacof",
    )(*slots)
    return (final[:, None, :], stress[0])


def distributed_body(dissim, classes, coords):
    halves = dissim.shape[0]
    per_dev = dissim.shape[1]
    columns = dissim.shape[2]
    coord_dims = coords.shape[0]
    row_count = halves * per_dev
    dis_tile = dissim.reshape(row_count, columns)
    weight = class_weight(classes.reshape(row_count, columns))
    denom_local = jnp.sum(weight * dis_tile * dis_tile)
    half_index = lax.axis_index("narrow")
    denom_total = lax.psum(denom_local, ("wide", "narrow"))
    positions = coords
    numbers = []
    for sweep in range(ITERS):
        row_points = lax.all_gather(positions, "narrow", axis=1, tiled=True)
        row_x = row_points.reshape(coord_dims, row_count)
        row_sq = jnp.sum(row_x * row_x, axis=0)
        fold_column_x = lax.dynamic_index_in_dim(
            lax.all_gather(row_points, "wide", axis=2, tiled=True), half_index, 1, keepdims=False
        )
        inner_prod = lax.dot_general(
            row_x,
            fold_column_x,
            (((0,), (0,)), ((), ())),
            precision=lax.Precision.HIGHEST,
            preferred_element_type=jnp.float32,
        )
        col_sq = jnp.sum(fold_column_x * fold_column_x, axis=0)
        distance = jnp.sqrt(row_sq[:, None] + col_sq[None, :] - 2.0 * inner_prod + 1.0)
        ratios = weight * dis_tile / distance
        pull_term = lax.dot_general(
            weight - ratios,
            fold_column_x,
            (((1,), (1,)), ((), ())),
            precision=lax.Precision.HIGHEST,
            preferred_element_type=jnp.float32,
        )
        misfit = dis_tile - distance
        pull_sums = pull_term.reshape(halves, per_dev, coord_dims).transpose(0, 2, 1)
        weight_sum, ratio_sum, pull_share = (
            lax.psum_scatter(
                jnp.sum(weight, axis=1).reshape(halves, per_dev),
                "narrow",
                scatter_dimension=0,
                tiled=True,
            ),
            lax.psum_scatter(
                jnp.sum(ratios, axis=1).reshape(halves, per_dev),
                "narrow",
                scatter_dimension=0,
                tiled=True,
            ),
            lax.psum_scatter(pull_sums, "narrow", scatter_dimension=0, tiled=True),
        )
        own_coords = positions[:, 0, :]
        updated = (own_coords * (1.0 + ratio_sum[0]) + pull_share[0]) / (1.0 + weight_sum[0])
        positions = updated[:, None, :]
        numbers.append(
            lax.psum(jnp.sum(weight * misfit * misfit), ("wide", "narrow")) / denom_total
        )
    stress = jnp.stack(numbers)
    return (positions, stress)


def solution(mesh):
    def body(dissim, classes, coords):
        coord_dims, halves, per_dev = coords.shape
        points, devices = dissim.shape[2], mesh.shape["wide"]
        small = halves == 1 and mesh.shape["narrow"] == 1 and points * points <= MOST_PAIRS
        small = small and coord_dims == 2 * SUBLANES and 2 * per_dev <= LANES
        small = small and per_dev % SUBLANES == 0 and points % LANES == 0
        small = small and devices == 16
        return (small_body if small else distributed_body)(dissim, classes, coords)

    return jax.shard_map(
        body,
        mesh=mesh,
        in_specs=(
            P(None, ("grp", "wide"), "narrow"),
            P(None, ("grp", "wide"), "narrow"),
            P(None, "narrow", ("grp", "wide")),
        ),
        out_specs=(P(None, "narrow", ("grp", "wide")), P("grp")),
        check_vma=False,
    )
```
